128 devices in a mesh: wide: 16 (over x, z_lo, core), deep: 8 (over z_hi, y).
Axes of the slice: x: 4, y: 4, z: 4 (z_hi: 2, z_lo: 2; z = z_hi * 2 + z_lo), core: 2. Of those that a mesh axis runs over, the one named last changes fastest.
Arguments:
- ocean_level: float32 [512, 1024], P('wide', 'deep'), may hold values from -1.5 to 1.5
- ocean_velocity: float32 [2, 40, 512, 1024], P(None, None, 'wide', 'deep'), may hold values from -1.8 to 1.8
- bathymetry: float32 [512, 1024], P('wide', 'deep'), may hold values from 2 to 6
- sea_mask: int32 [512, 1024], P('wide', 'deep'), may hold values from 0 to 1, as said below
- stress_in: float32 [3, 512, 1024], P(None, 'wide', 'deep'), may hold values from -6 to 6
- spectra: bfloat16 [36, 36, 256, 512], P(None, None, ('wide', 'deep')), may hold values from 0.019897461 to 1
- wind_field: bfloat16 [2, 256, 512], P(None, ('wide', 'deep')), may hold values from -9 to 9
Outputs:
- level_out: float32 [512, 1024], P('wide', 'deep')
- velocity_out: float32 [2, 40, 512, 1024], P(None, None, 'wide', 'deep')
- spectra_out: bfloat16 [36, 36, 256, 512], P(None, None, ('wide', 'deep'))
- stress_out: float32 [3, 256, 512], P(None, 'wide', 'deep')
The draws below stay inside these ranges and needn't reach their ends.
Inputs may be any that keep to these rules, and one draw needn't show every extreme that they name: `sea_mask`: 1 marks sea, 0 land. In each device's tile of 32 x 128 cells the land is a band of whole columns in the middle of the tile along the second dimension, from local column 64 - 2b to 64 + 2b - 1, with b drawn per tile from 8 to 16, so at most half of a tile is land, and some tile is land in exactly half; blocks of 2 x 2 cells starting at even indices are all sea or all land.
All inputs are finite; a program needn't handle non-finite values.
Results may differ from the reference program's by a relative error of at most 0.009.
Values may be sent and summed in bfloat16 or wider, within the bound.
No kernel may reach another device: no remote copies, remote signals or barrier semaphores. Data moves between devices by JAX's collectives and lax.ppermute only.
A program may use at most 192 MiB of HBM per device.

```python
import math
import jax
import jax.numpy as jnp
from jax import lax

CX = 32
CY = 128
K = 40
NDIR = 36
NFREQ = 36
WX = 2
NX = 512
NY = 1024
WNX = 256
WNY = 512


def draw_sea_mask(key, part):
    key = jax.random.fold_in(key, 7)
    band_key, pick_key = jax.random.split(key)
    tiles_x = NX // CX
    tiles_y = NY // CY
    narrow_band = CY // 16
    wide_band = CY // 8
    band_half = jax.random.randint(band_key, (tiles_x, tiles_y), narrow_band, wide_band + 1)
    chosen = jax.random.randint(pick_key, (), 0, tiles_x * tiles_y)
    tile_ids = jnp.arange(tiles_x * tiles_y).reshape(tiles_x, tiles_y)
    band_half = jnp.where(tile_ids == chosen, wide_band, band_half)
    band_full = jnp.repeat(jnp.repeat(band_half, CX, axis=0), CY, axis=1)
    local_cols = jnp.arange(NY) % CY
    centre = CY // 2
    offset = local_cols[None, :] - centre
    land = (offset >= -2 * band_full) & (offset < 2 * band_full)
    return jnp.where(land, 0, 1).astype(jnp.int32)


def block_levels(stream_key, extent, cuts, smallest, top_value):
    loudness, own = 1.0, jax.random.fold_in(stream_key, 6)
    for axis_at, parts in cuts:
        draws = jnp.exp(jax.random.uniform(jax.random.fold_in(own, axis_at), (parts,), jnp.float32, smallest / len(cuts), top_value / len(cuts)))
        loudness = loudness * jnp.repeat(draws, extent[axis_at] // parts).reshape([-1 if axis == axis_at else 1 for axis in range(len(extent))])
    return loudness


def centred(stream_key, extent, deviation, bound, pieces=(), held_as=jnp.bfloat16):
    array = deviation * jax.random.normal(stream_key, extent, jnp.float32)
    if pieces:
        array = array * block_levels(stream_key, extent, pieces, -0.22, 0.18)
    return jnp.clip(array, -bound, bound).astype(held_as)


def setup_inputs(seed: int = 0) -> dict:
    key_list = jax.random.split(jax.random.key(seed), 8)
    return {
        "ocean_level": centred(key_list[0], (NX, NY), 0.25, 1.5, ((0, 16), (1, 8)), jnp.float32),
        "ocean_velocity": centred(key_list[1], (2, K, NX, NY), 0.3, 1.8, ((2, 16), (3, 8)), jnp.float32),
        "bathymetry": jnp.clip(2.0 + 4.0 * jax.random.uniform(key_list[2], (NX, NY), jnp.float32) ** block_levels(key_list[2], (NX, NY), ((0, 16), (1, 8)), -0.2, 0.2), 2.0, 6.0),
        "sea_mask": draw_sea_mask(jax.random.fold_in(key_list[7], 71), 0),
        "stress_in": centred(key_list[4], (3, NX, NY), 1.0, 6.0, ((1, 16), (2, 8)), jnp.float32),
        "spectra": jnp.clip(jnp.exp(math.log(1.0) - 3.9171631 * jax.random.uniform(key_list[5], (NDIR, NFREQ, WNX, WNY), jnp.float32) ** block_levels(key_list[5], (NDIR, NFREQ, WNX, WNY), ((2, 128),), -0.2, 0.2)), 0.019897461, 1.0).astype(jnp.bfloat16),
        "wind_field": centred(key_list[6], (2, WNX, WNY), 1.5, 9.0, ((1, 128),)),
    }


LAM_O = 0.2
F_CORIOLIS = 0.1
NU_H = 0.05
KAPPA_V = 0.2
LAM_W = 0.25
GAMMA_BR = 0.73
A_IN = 0.15
C_NL = 0.5
C_WC = 0.002


def wave_tables(directions, frequencies):
    angles = 2.0 * math.pi * jnp.arange(directions, dtype=jnp.float32) / directions
    sigmas = 0.4 * jnp.power(jnp.float32(1.07), jnp.arange(frequencies, dtype=jnp.float32))
    return jnp.cos(angles), jnp.sin(angles), sigmas


def stress_weights(cos_dir, sin_dir, sigmas):
    directions = cos_dir.shape[0]
    frequencies = sigmas.shape[0]
    weights = (2.0 * math.pi / directions) * 0.5 * sigmas / frequencies
    angular = jnp.stack([cos_dir * cos_dir, cos_dir * sin_dir, sin_dir * sin_dir])
    return angular[:, :, None] * weights[None, None, :]


def coarsen(field_2d):
    row_count, col_count = field_2d.shape
    return jnp.mean(field_2d.reshape(row_count // 2, 2, col_count // 2, 2), axis=(1, 3))


def ocean_update(vel_padded, surface_padded, wet_ocean):
    level_pad = surface_padded[0]
    depth_pad = surface_padded[1] + level_pad
    mean_pad = jnp.mean(vel_padded, axis=1)
    flux_x = depth_pad * mean_pad[0]
    flux_y = depth_pad * mean_pad[1]
    divergence = flux_x[2:, 1:-1] - flux_x[:-2, 1:-1] + flux_y[1:-1, 2:] - flux_y[1:-1, :-2]
    level_now = level_pad[1:-1, 1:-1]
    new_level = level_now - 0.5 * LAM_O * wet_ocean * divergence
    depth_now = depth_pad[1:-1, 1:-1]
    grad_x = 0.5 * (level_pad[2:, 1:-1] - level_pad[:-2, 1:-1])
    grad_y = 0.5 * (level_pad[1:-1, 2:] - level_pad[1:-1, :-2])
    stress_xx = surface_padded[2]
    stress_xy = surface_padded[3]
    stress_yy = surface_padded[4]
    force_x = -0.5 * ((stress_xx[2:, 1:-1] - stress_xx[:-2, 1:-1]) + (stress_xy[1:-1, 2:] - stress_xy[1:-1, :-2])) / depth_now
    force_y = -0.5 * ((stress_xy[2:, 1:-1] - stress_xy[:-2, 1:-1]) + (stress_yy[1:-1, 2:] - stress_yy[1:-1, :-2])) / depth_now
    vel_inner = vel_padded[:, :, 1:-1, 1:-1]
    laplace = (vel_padded[:, :, 2:, 1:-1] + vel_padded[:, :, :-2, 1:-1]
               + vel_padded[:, :, 1:-1, 2:] + vel_padded[:, :, 1:-1, :-2] - 4.0 * vel_inner)
    upper_nb = jnp.concatenate([vel_inner[:, :1], vel_inner[:, :-1]], axis=1)
    lower_nb = jnp.concatenate([vel_inner[:, 1:], vel_inner[:, -1:]], axis=1)
    vertical = upper_nb + lower_nb - 2.0 * vel_inner
    coriolis = jnp.stack([F_CORIOLIS * vel_inner[1], -F_CORIOLIS * vel_inner[0]])
    pressure = jnp.stack([grad_x, grad_y])[:, None]
    force_xy = jnp.stack([force_x, force_y])[:, None]
    tendency = -LAM_O * pressure + coriolis + LAM_O * force_xy + NU_H * laplace + KAPPA_V * vertical
    new_vel = wet_ocean * (vel_inner + tendency)
    return new_vel, new_level


def propagate(spec_padded, cur_padded, cos_dir, sin_dir, sigmas, wet_wave):
    group_speed = 0.5 / sigmas
    speed_x = group_speed[None, :, None, None] * cos_dir[:, None, None, None] + cur_padded[0][None, None]
    speed_y = group_speed[None, :, None, None] * sin_dir[:, None, None, None] + cur_padded[1][None, None]
    face_x = 0.5 * (speed_x[:, :, 1:, 1:-1] + speed_x[:, :, :-1, 1:-1])
    flux_x = jnp.maximum(face_x, 0.0) * spec_padded[:, :, :-1, 1:-1] + jnp.minimum(face_x, 0.0) * spec_padded[:, :, 1:, 1:-1]
    face_y = 0.5 * (speed_y[:, :, 1:-1, 1:] + speed_y[:, :, 1:-1, :-1])
    flux_y = jnp.maximum(face_y, 0.0) * spec_padded[:, :, 1:-1, :-1] + jnp.minimum(face_y, 0.0) * spec_padded[:, :, 1:-1, 1:]
    interior = spec_padded[:, :, 1:-1, 1:-1]
    updated = interior - LAM_W * (flux_x[:, :, 1:] - flux_x[:, :, :-1]) - LAM_W * (flux_y[:, :, :, 1:] - flux_y[:, :, :, :-1])
    return (updated * wet_wave).astype(jnp.bfloat16)


def source_terms(spec_cells, forcing_cells, cos_dir, sin_dir, sigmas):
    rel_x = forcing_cells[0] - forcing_cells[2]
    rel_y = forcing_cells[1] - forcing_cells[3]
    wind_along = rel_x[None, None, :] * cos_dir[:, None, None] + rel_y[None, None, :] * sin_dir[:, None, None]
    sigma_col = sigmas[None, :, None]
    growth = A_IN * jnp.minimum(jnp.maximum(wind_along * sigma_col - 1.0, 0.0), 2.0)
    spread = 0.5 * (jnp.roll(spec_cells, 2, axis=0) + jnp.roll(spec_cells, -2, axis=0))
    zero_row = jnp.zeros_like(spread[:, :1])
    upper_band = jnp.concatenate([spread[:, 1:], zero_row], axis=1)
    lower_band = jnp.concatenate([zero_row, spread[:, :-1]], axis=1)
    moment_zero = jnp.mean(spec_cells, axis=(0, 1))
    moment_two = jnp.mean(spec_cells * sigma_col * sigma_col, axis=(0, 1))
    summed = (spec_cells + growth * spec_cells + C_NL * (upper_band * lower_band - spec_cells * spec_cells)
              - C_WC * sigma_col * sigma_col * sigma_col * moment_two * spec_cells)
    limit_sq = (GAMMA_BR * forcing_cells[4]) * (GAMMA_BR * forcing_cells[4])
    breaking = limit_sq / jnp.maximum(16.0 * moment_zero, limit_sq)
    return summed * breaking


def blockwise_sources(spec_state, forcing, wet_wave, cos_dir, sin_dir, sigmas):
    directions = spec_state.shape[0]
    frequencies = spec_state.shape[1]

    def update(block_id, result):
        row_start = (block_id * WX).astype(jnp.int32)
        block_spec = lax.dynamic_slice_in_dim(spec_state, row_start, WX, 2).astype(jnp.float32)
        block_force = lax.dynamic_slice_in_dim(forcing, row_start, WX, 1)
        block_wet = lax.dynamic_slice_in_dim(wet_wave, row_start, WX, 0)
        flat_spec = block_spec.reshape(directions, frequencies, WX * WNY)
        updated = source_terms(flat_spec, block_force.reshape(5, WX * WNY), cos_dir, sin_dir, sigmas)
        updated = (updated * block_wet.reshape(-1)).astype(jnp.bfloat16)
        return lax.dynamic_update_slice_in_dim(result, updated.reshape(block_spec.shape), row_start, 2)

    return lax.fori_loop(0, WNX // WX, update, spec_state)


def blockwise_stress(spec_state, stress_table):
    def update(block_id, result):
        row_start = (block_id * WX).astype(jnp.int32)
        block_spec = lax.dynamic_slice_in_dim(spec_state, row_start, WX, 2).astype(jnp.float32)
        block_stress = jnp.einsum("cdf,dfxy->cxy", stress_table, block_spec, precision=lax.Precision.HIGHEST)
        return lax.dynamic_update_slice_in_dim(result, block_stress, row_start, 1)

    initial = jnp.zeros((3, WNX, WNY), jnp.float32)
    return lax.fori_loop(0, WNX // WX, update, initial)


def reference(ocean_level, ocean_velocity, bathymetry, sea_mask, stress_in, spectra, wind_field):
    wet_ocean = sea_mask.astype(jnp.float32)
    surface = jnp.stack([ocean_level, bathymetry, stress_in[0], stress_in[1], stress_in[2]])
    surface_padded = jnp.pad(surface, ((0, 0), (1, 1), (1, 1)))
    vel_padded = jnp.pad(ocean_velocity, ((0, 0), (0, 0), (1, 1), (1, 1)))
    velocity_out, level_out = ocean_update(vel_padded, surface_padded, wet_ocean)
    currents = jnp.stack([coarsen(velocity_out[0, 0]), coarsen(velocity_out[1, 0])]).astype(jnp.bfloat16)
    wave_depth = coarsen(bathymetry + level_out).astype(jnp.bfloat16)
    wet_wave = wet_ocean[0::2, 0::2]
    cos_dir, sin_dir, sigmas = wave_tables(NDIR, NFREQ)
    current_padded = jnp.pad(currents.astype(jnp.float32), ((0, 0), (1, 1), (1, 1)))
    forcing = jnp.concatenate([wind_field.astype(jnp.float32), currents.astype(jnp.float32),
                               wave_depth.astype(jnp.float32)[None]], axis=0)
    spec_state = spectra
    for step_index in range(2):
        def one_direction(packed):
            dir_plane, cos_one, sin_one = packed
            padded = jnp.pad(dir_plane.astype(jnp.float32)[None], ((0, 0), (0, 0), (1, 1), (1, 1)))
            return propagate(padded, current_padded, cos_one[None], sin_one[None], sigmas, wet_wave)[0]

        spec_state = lax.map(one_direction, (spec_state, cos_dir, sin_dir))
        spec_state = blockwise_sources(spec_state, forcing, wet_wave, cos_dir, sin_dir, sigmas)
    stress_out = blockwise_stress(spec_state, stress_weights(cos_dir, sin_dir, sigmas))
    return level_out, velocity_out, spec_state, stress_out
```

```python
import math

import numpy as np

import jax
import jax.numpy as jnp
from jax import lax
from jax.experimental import pallas as pl
from jax.experimental.pallas import tpu as pltpu
from jax.sharding import PartitionSpec as P

LAM_O = 0.2
F_CORIOLIS = 0.1
NU_H = 0.05
KAPPA_V = 0.2
LAM_W = 0.25
GAMMA_BR = 0.73
A_IN = 0.15
C_NL = 0.5
C_WC = 0.002

ND = 36
NF = 36
SIGMA = 0.4 * np.power(1.07, np.arange(NF))
ANGLE = 2.0 * math.pi * np.arange(ND) / ND
TRIG = np.stack([np.cos(ANGLE), np.sin(ANGLE)]).astype(np.float32)

F32 = jnp.float32
BF16 = jnp.bfloat16
VMEM = pltpu.VMEM
SMEM = pltpu.SMEM
HIGH = lax.Precision.HIGHEST


def params(mib):
    return pltpu.CompilerParams(vmem_limit_bytes=mib * 1024 * 1024)


def iotas():
    sub = lax.broadcasted_iota(jnp.int32, (8, 128), 0)
    lane = lax.broadcasted_iota(jnp.int32, (8, 128), 1)
    return sub, lane


def sublane_up(x):
    return pltpu.roll(x, 7, 0)


def sublane_down(x):
    return pltpu.roll(x, 1, 0)


def swapped(x, even):
    return jnp.where(even, sublane_up(x), sublane_down(x))


def next_column(x, first_lane):
    return pltpu.roll(jnp.where(first_lane, pltpu.roll(x, 6, 0), x), 127, 1)


def previous_column(x, last_lane):
    return pltpu.roll(jnp.where(last_lane, pltpu.roll(x, 2, 0), x), 1, 1)


def pack_pair(first, second, even):
    upper = jnp.where(even, sublane_up(second), first)
    lower = jnp.where(even, first, sublane_down(second))
    return upper, lower


def split_rows_kernel(spec_ref, upper_ref, lower_ref):
    sub, _ = iotas()
    even = (sub & 1) == 0

    def body(d, carry):
        for quad in range(NF // 4):
            block = spec_ref[d, 32 * quad : 32 * quad + 32, :].astype(F32)
            up0, lo0 = pack_pair(block[0:8], block[8:16], even)
            up1, lo1 = pack_pair(block[16:24], block[24:32], even)
            rows = slice(16 * quad, 16 * quad + 16)
            upper_ref[d, rows, :] = jnp.concatenate([up0, up1], axis=0).astype(BF16)
            lower_ref[d, rows, :] = jnp.concatenate([lo0, lo1], axis=0).astype(BF16)
        return carry

    lax.fori_loop(0, ND, body, 0)


def split_rows(spec):
    half = jax.ShapeDtypeStruct((ND, NF * 4, 128), BF16)
    return pl.pallas_call(
        split_rows_kernel,
        out_shape=(half, half),
        in_specs=[pl.BlockSpec(memory_space=VMEM)],
        out_specs=(pl.BlockSpec(memory_space=VMEM), pl.BlockSpec(memory_space=VMEM)),
        compiler_params=params(24),
        cost_estimate=pl.CostEstimate(flops=4000000, bytes_accessed=5400000, transcendentals=0),
        name="split_rows",
    )(spec)


FIELDS = 12


def gather_kernel(level_ref, vel_ref, bathy_ref, mask_ref, stress_ref, own_ref, low_ref, high_ref):
    levels = vel_ref.shape[1]
    fields = [
        level_ref[...],
        bathy_ref[...],
        mask_ref[...].astype(F32),
        stress_ref[0],
        stress_ref[1],
        stress_ref[2],
        vel_ref[0, 0],
        vel_ref[1, 0],
        vel_ref[0, 1],
        vel_ref[1, 1],
    ]
    for c in range(2):
        total = vel_ref[c, 0]
        for k in range(1, levels):
            total = total + vel_ref[c, k]
        fields.append(total * (1.0 / levels))
    for index, field in enumerate(fields):
        own_ref[index] = field
        low_ref[index] = field[0:8]
        high_ref[index] = field[24:32]


def gather_surface(level, vel, bathy, mask, stress):
    rows, cols = level.shape
    edge = jax.ShapeDtypeStruct((FIELDS, 8, cols), F32)
    return pl.pallas_call(
        gather_kernel,
        out_shape=(jax.ShapeDtypeStruct((FIELDS, rows, cols), F32), edge, edge),
        in_specs=[pl.BlockSpec(memory_space=VMEM)] * 5,
        out_specs=(pl.BlockSpec(memory_space=VMEM),) * 3,
        compiler_params=params(16),
        cost_estimate=pl.CostEstimate(flops=400000, bytes_accessed=1700000, transcendentals=0),
        name="gather_surface",
    )(level, vel, bathy, mask, stress)


EXT = 48
SENT_ROWS = 24


def surface_kernel(parity_ref, own_ref, low_ref, high_ref, out_ref):
    lane = lax.broadcasted_iota(jnp.int32, (EXT, 128), 1)

    def field(index):
        return jnp.concatenate([low_ref[index], own_ref[index], high_ref[index]], axis=0)

    level, bathy, wet, sxx, sxy, syy, u, v, u1, v1, ubar, vbar = [field(i) for i in range(FIELDS)]

    def down(x):
        return pltpu.roll(x, 1, 0)

    def up(x):
        return pltpu.roll(x, EXT - 1, 0)

    def left(x):
        return jnp.where(lane == 0, 0.0, pltpu.roll(x, 1, 1))

    def right(x):
        return jnp.where(lane == 127, 0.0, pltpu.roll(x, 127, 1))

    depth = bathy + level
    inverse = 1.0 / jnp.where(depth > 0.0, depth, 1.0)
    flux_x = depth * ubar
    flux_y = depth * vbar
    divergence = up(flux_x) - down(flux_x) + right(flux_y) - left(flux_y)
    new_depth = bathy + (level - 0.5 * LAM_O * wet * divergence)
    grad_x = 0.5 * (up(level) - down(level))
    grad_y = 0.5 * (right(level) - left(level))
    force_x = -0.5 * (up(sxx) - down(sxx) + (right(sxy) - left(sxy))) * inverse
    force_y = -0.5 * (up(sxy) - down(sxy) + (right(syy) - left(syy))) * inverse
    laplace_u = up(u) + down(u) + right(u) + left(u) - 4.0 * u
    laplace_v = up(v) + down(v) + right(v) + left(v) - 4.0 * v
    new_u = wet * (
        u
        - LAM_O * grad_x
        + F_CORIOLIS * v
        + LAM_O * force_x
        + NU_H * laplace_u
        + KAPPA_V * (u1 - u)
    )
    new_v = wet * (
        v
        - LAM_O * grad_y
        - F_CORIOLIS * u
        + LAM_O * force_y
        + NU_H * laplace_v
        + KAPPA_V * (v1 - v)
    )

    column = lax.broadcasted_iota(jnp.int32, (128, 128), 0)
    target = lax.broadcasted_iota(jnp.int32, (128, 128), 1)
    to_coarse = jnp.where(target == 64 * parity_ref[0] + (column >> 1), 0.25, 0.0)
    coarse_row = lax.broadcasted_iota(jnp.int32, (32, EXT), 0)
    fine_row = lax.broadcasted_iota(jnp.int32, (32, EXT), 1)
    first_row = 4 * (coarse_row >> 2) + 2 * (coarse_row & 3) + 6
    pair_sum = jnp.where((fine_row == first_row) | (fine_row == first_row + 1), 1.0, 0.0)
    stacked = jnp.concatenate([new_u, new_v, new_depth, wet], axis=0)
    narrowed = jnp.dot(stacked, to_coarse, precision=HIGH, preferred_element_type=F32)
    for index in range(4):
        coarse = jnp.dot(
            pair_sum,
            narrowed[EXT * index : EXT * index + EXT],
            precision=HIGH,
            preferred_element_type=F32,
        )
        for strip in range(8):
            out_ref[strip, 4 * index : 4 * index + 4, :] = coarse[4 * strip : 4 * strip + 4]

    wet_inverse = wet * inverse
    to_right = [u, v, sxy, syy, level, flux_y]
    to_left = [u, v, -sxy, -syy, -level, -flux_y]
    weights = [
        NU_H * wet,
        NU_H * wet,
        0.5 * LAM_O * wet_inverse,
        0.5 * LAM_O * wet_inverse,
        0.5 * LAM_O * wet,
        0.5 * LAM_O * wet,
    ]
    edges = jnp.zeros((EXT, 128), F32)
    for index in range(6):
        edges = jnp.where(lane == index, to_right[index][:, 127:128], edges)
        edges = jnp.where(lane == 8 + index, to_left[index][:, 0:1], edges)
        edges = jnp.where(lane == 16 + index, weights[index][:, 0:1], edges)
        edges = jnp.where(lane == 24 + index, weights[index][:, 127:128], edges)
    for strip in range(8):
        out_ref[strip, 16:24, :] = edges[4 * strip + 6 : 4 * strip + 14]


def surface_step(parity, own, low, high):
    return pl.pallas_call(
        surface_kernel,
        out_shape=jax.ShapeDtypeStruct((8, SENT_ROWS, 128), F32),
        in_specs=[pl.BlockSpec(memory_space=SMEM)] + [pl.BlockSpec(memory_space=VMEM)] * 3,
        out_specs=pl.BlockSpec(memory_space=VMEM),
        compiler_params=params(16),
        cost_estimate=pl.CostEstimate(flops=2000000, bytes_accessed=400000, transcendentals=0),
        name="surface_step",
    )(parity, own, low, high)


def rounded(x):
    return x.astype(BF16).astype(F32)


def strip_fields(arrived_ref, wind_ref):
    sub, lane = iotas()
    even = (sub & 1) == 0
    base = 64 * (sub & 1)
    edge_sums = []
    for row in range(4):
        total = None
        for fine in (2 * row, 2 * row + 1):
            edge = arrived_ref[:, 16 + fine, :]
            from_left = jnp.where(sub == 0, 0.0, sublane_down(edge))
            from_right = jnp.where(sub == 7, 0.0, sublane_up(edge))
            weight = pltpu.roll(edge, 112, 1)
            product = weight * jnp.where(lane < 8, from_left, from_right)
            total = product if total is None else total + product
        edge_sums.append(0.25 * total)

    def tiles(index, row, parts):
        value = arrived_ref[:, 4 * index + row, :]
        edge = edge_sums[row]
        left = sum(edge[:, p : p + 1] for p in parts)
        right = sum(edge[:, 8 + p : 9 + p] for p in parts)
        value = value + jnp.where(lane == base, left, 0.0)
        return value + jnp.where(lane == base + 63, right, 0.0)

    def joined(first, second):
        return jnp.where(even, first + sublane_up(first), second + sublane_down(second))

    u_rows = [tiles(0, row, (0, 2)) for row in range(4)]
    v_rows = [tiles(1, row, (1, 3, 4)) for row in (1, 2)]
    depth_rows = [tiles(2, row, (5,)) for row in (1, 2)]
    wet_rows = [arrived_ref[:, 12 + row, :] for row in (1, 2)]
    current_u = rounded(joined(u_rows[1], u_rows[2]))
    outer_u = rounded(joined(u_rows[0], u_rows[3]))
    current_v = rounded(joined(*v_rows))
    depth = rounded(joined(*depth_rows))
    wet = jnp.where(joined(*wet_rows) > 0.5, 1.0, 0.0)
    wind = wind_ref[...].astype(F32)
    return current_u, outer_u, current_v, depth, wet, wind[0:8], wind[8:16]


def propagate_direction(d, trig_ref, spec_ref, upper_ref, lower_ref, cells, moved_ref, sums):
    even, first_lane, last_lane, col_first, col_last, sign, outer, inner, face_v, edge_v, wet = cells
    along_x = trig_ref[0, d] * sign
    along_y = jnp.full((8, 128), trig_ref[1, d], F32)
    zeroth, second = sums
    for quad in range(NF // 4):
        block = spec_ref[d, 32 * quad : 32 * quad + 32, :].astype(F32)
        above = upper_ref[d, 16 * quad : 16 * quad + 16, :].astype(F32)
        below = lower_ref[d, 16 * quad : 16 * quad + 16, :].astype(F32)
        results = []
        for part in range(4):
            f = 4 * quad + part
            here = block[8 * part : 8 * part + 8]
            pair = slice(8 * (part // 2), 8 * (part // 2) + 8)
            if part % 2 == 0:
                halo = jnp.where(even, sublane_up(above[pair]), sublane_down(below[pair]))
            else:
                halo = jnp.where(even, above[pair], below[pair])
            speed = float(LAM_W * 0.5 / SIGMA[f])
            speed_x = along_x * speed
            through_outer = speed_x + outer
            through_inner = inner - speed_x
            other = swapped(here, even)
            leaving = jnp.minimum(through_outer, 0.0) + jnp.minimum(through_inner, 0.0)
            change = (
                jnp.maximum(through_outer, 0.0) * halo
                + jnp.maximum(through_inner, 0.0) * other
                + leaving * here
            )
            speed_y = along_y * speed
            through_y = speed_y + face_v
            following = jnp.where(col_last, 0.0, next_column(here, first_lane))
            flux = jnp.maximum(through_y, 0.0) * here + jnp.minimum(through_y, 0.0) * following
            entry = jnp.minimum(speed_y + edge_v, 0.0) * here
            flux_before = jnp.where(col_first, entry, previous_column(flux, last_lane))
            moved = wet * (here + change - flux + flux_before)
            zeroth = zeroth + moved
            second = second + moved * float(SIGMA[f] ** 2)
            results.append(moved)
        moved_ref[d, 32 * quad : 32 * quad + 32, :] = jnp.concatenate(results, axis=0).astype(BF16)
    return zeroth, second


def source_direction(d, trig_ref, moved_ref, damp_ref, rel_x, rel_y, breaking, emit):
    plus = lax.rem(d + 2, ND)
    minus = lax.rem(d + ND - 2, ND)
    wind_along = A_IN * (rel_x * trig_ref[0, d] + rel_y * trig_ref[1, d])
    spreads = {-1: None, NF: None}
    values = {}

    def load(quad):
        rows = slice(32 * quad, 32 * quad + 32)
        here = moved_ref[d, rows, :].astype(F32)
        around = moved_ref[plus, rows, :].astype(F32) + moved_ref[minus, rows, :].astype(F32)
        for part in range(4):
            values[4 * quad + part] = here[8 * part : 8 * part + 8]
            spreads[4 * quad + part] = around[8 * part : 8 * part + 8]

    load(0)
    for quad in range(NF // 4):
        if quad + 1 < NF // 4:
            load(quad + 1)
        results = []
        for part in range(4):
            f = 4 * quad + part
            here = values.pop(f)
            growth = jnp.minimum(
                jnp.maximum(wind_along * float(SIGMA[f]) - A_IN, 0.0), 2.0 * A_IN
            )
            summed = (growth + damp_ref[f] - C_NL * here) * here
            if 0 < f < NF - 1:
                summed = summed + (0.25 * C_NL) * spreads[f + 1] * spreads[f - 1]
            results.append(summed * breaking)
        emit(quad, results)


def wave_kernel(last, trig_ref, spec_ref, upper_ref, lower_ref, arrived_ref, wind_ref, *rest):
    if last:
        out_ref, stress_ref, moved_ref, damp_ref = rest
    else:
        out_ref, out_upper_ref, out_lower_ref, moved_ref, damp_ref = rest
    sub, lane = iotas()
    even = (sub & 1) == 0
    first_lane, last_lane = lane == 0, lane == 127
    col_first = first_lane & (sub < 2)
    col_last = last_lane & (sub >= 6)
    current_u, outer_u, current_v, depth, wet, wind_x, wind_y = strip_fields(arrived_ref, wind_ref)
    sign = jnp.where(even, 1.0, -1.0)
    half = 0.5 * LAM_W
    outer = sign * (half * (current_u + outer_u))
    inner = -sign * (half * (current_u + swapped(current_u, even)))
    after_v = jnp.where(col_last, 0.0, next_column(current_v, first_lane))
    face_v = half * (current_v + after_v)
    edge_v = half * current_v
    cells = (
        even,
        first_lane,
        last_lane,
        col_first,
        col_last,
        sign,
        outer,
        inner,
        face_v,
        edge_v,
        wet,
    )
    zeros = jnp.zeros((8, 128), F32)
    zeroth, second = lax.fori_loop(
        0,
        ND,
        lambda d, sums: propagate_direction(
            d, trig_ref, spec_ref, upper_ref, lower_ref, cells, moved_ref, sums
        ),
        (zeros, zeros),
    )
    moment_zero = zeroth * (1.0 / (ND * NF))
    moment_two = second * (1.0 / (ND * NF))
    limit = (GAMMA_BR * depth) * (GAMMA_BR * depth)
    breaking = jnp.where(wet > 0.5, limit / jnp.maximum(16.0 * moment_zero, limit), 0.0)
    for f in range(NF):
        damp_ref[f] = 1.0 - float(C_WC * SIGMA[f] ** 3) * moment_two
    rel_x = wind_x - current_u
    rel_y = wind_y - current_v

    def store(d, quad, results):
        block = jnp.concatenate(results, axis=0).astype(BF16)
        out_ref[d, 32 * quad : 32 * quad + 32, :] = block

    if not last:

        def body(d, carry):
            def emit(quad, results):
                store(d, quad, results)
                up0, lo0 = pack_pair(results[0], results[1], even)
                up1, lo1 = pack_pair(results[2], results[3], even)
                rows = slice(16 * quad, 16 * quad + 16)
                out_upper_ref[d, rows, :] = jnp.concatenate([up0, up1], axis=0).astype(BF16)
                out_lower_ref[d, rows, :] = jnp.concatenate([lo0, lo1], axis=0).astype(BF16)

            source_direction(d, trig_ref, moved_ref, damp_ref, rel_x, rel_y, breaking, emit)
            return carry

        lax.fori_loop(0, ND, body, 0)
    else:

        def body(d, totals):
            energy = [zeros]

            def emit(quad, results):
                store(d, quad, results)
                for part in range(4):
                    scale = float(2.0 * math.pi / ND * 0.5 * SIGMA[4 * quad + part] / NF)
                    energy[0] = energy[0] + results[part] * scale

            source_direction(d, trig_ref, moved_ref, damp_ref, rel_x, rel_y, breaking, emit)
            cos_d, sin_d = trig_ref[0, d], trig_ref[1, d]
            xx, xy, yy = totals
            total = energy[0]
            return (
                xx + total * (cos_d * cos_d),
                xy + total * (cos_d * sin_d),
                yy + total * (sin_d * sin_d),
            )

        totals = lax.fori_loop(0, ND, body, (zeros, zeros, zeros))
        for c in range(3):
            for tile in range(8):
                block = tile // 2
                stress_ref[tile, 2 * c : 2 * c + 2, :] = totals[c][2 * block : 2 * block + 2]


def wave_step(last, trig, spec, upper, lower, arrived, wind):
    full = jax.ShapeDtypeStruct((ND, NF * 8, 128), BF16)
    half = jax.ShapeDtypeStruct((ND, NF * 4, 128), BF16)
    outs = (full, jax.ShapeDtypeStruct((8, 6, 128), F32)) if last else (full, half, half)
    return pl.pallas_call(
        lambda *refs: wave_kernel(last, *refs),
        out_shape=outs,
        in_specs=[pl.BlockSpec(memory_space=SMEM)] + [pl.BlockSpec(memory_space=VMEM)] * 5,
        out_specs=tuple(pl.BlockSpec(memory_space=VMEM) for _ in outs),
        scratch_shapes=[VMEM((ND, NF * 8, 128), BF16), VMEM((NF, 8, 128), F32)],
        compiler_params=params(40),
        cost_estimate=pl.CostEstimate(
            flops=100000000, bytes_accessed=8000000, transcendentals=0
        ),
        name="wave_step",
    )(trig, spec, upper, lower, arrived, wind)


def shifted(array, axis_name, up):
    count = lax.axis_size(axis_name)
    pairs = [(i, i + 1) for i in range(count - 1)]
    if not up:
        pairs = [(target, source) for source, target in pairs]
    return lax.ppermute(array, axis_name, pairs)


def extended(block, sides, width):
    for axis, dim in sides:
        low = shifted(
            lax.slice_in_dim(block, block.shape[dim] - width, None, axis=dim), axis, True
        )
        high = shifted(lax.slice_in_dim(block, 0, width, axis=dim), axis, False)
        block = jnp.concatenate([low, block, high], axis=dim)
    return block


def ocean_update(vel_padded, surface_padded, wet_ocean):
    level_pad = surface_padded[0]
    depth_pad = surface_padded[1] + level_pad
    mean_pad = jnp.mean(vel_padded, axis=1)
    flux_x = depth_pad * mean_pad[0]
    flux_y = depth_pad * mean_pad[1]
    divergence = flux_x[2:, 1:-1] - flux_x[:-2, 1:-1] + flux_y[1:-1, 2:] - flux_y[1:-1, :-2]
    level_now = level_pad[1:-1, 1:-1]
    new_level = level_now - 0.5 * LAM_O * wet_ocean * divergence
    depth_now = depth_pad[1:-1, 1:-1]
    grad_x = 0.5 * (level_pad[2:, 1:-1] - level_pad[:-2, 1:-1])
    grad_y = 0.5 * (level_pad[1:-1, 2:] - level_pad[1:-1, :-2])
    stress_xx = surface_padded[2]
    stress_xy = surface_padded[3]
    stress_yy = surface_padded[4]
    force_x = (
        -0.5
        * (
            stress_xx[2:, 1:-1]
            - stress_xx[:-2, 1:-1]
            + (stress_xy[1:-1, 2:] - stress_xy[1:-1, :-2])
        )
        / depth_now
    )
    force_y = (
        -0.5
        * (
            stress_xy[2:, 1:-1]
            - stress_xy[:-2, 1:-1]
            + (stress_yy[1:-1, 2:] - stress_yy[1:-1, :-2])
        )
        / depth_now
    )
    vel_inner = vel_padded[:, :, 1:-1, 1:-1]
    laplace = (
        vel_padded[:, :, 2:, 1:-1]
        + vel_padded[:, :, :-2, 1:-1]
        + vel_padded[:, :, 1:-1, 2:]
        + vel_padded[:, :, 1:-1, :-2]
        - 4.0 * vel_inner
    )
    upper_nb = jnp.concatenate([vel_inner[:, :1], vel_inner[:, :-1]], axis=1)
    lower_nb = jnp.concatenate([vel_inner[:, 1:], vel_inner[:, -1:]], axis=1)
    vertical = upper_nb + lower_nb - 2.0 * vel_inner
    coriolis = jnp.stack([F_CORIOLIS * vel_inner[1], -F_CORIOLIS * vel_inner[0]])
    pressure = jnp.stack([grad_x, grad_y])[:, None]
    force_xy = jnp.stack([force_x, force_y])[:, None]
    tendency = -LAM_O * pressure + coriolis + LAM_O * force_xy + NU_H * laplace + KAPPA_V * vertical
    new_vel = wet_ocean * (vel_inner + tendency)
    return (new_vel, new_level)


def per_device(ocean_level, ocean_velocity, bathymetry, sea_mask, stress_in, spectra, wind_field):
    levels = ocean_velocity.shape[1]
    ocean_rows, ocean_cols = ocean_level.shape
    both = ("wide", "deep")

    spec = spectra.reshape(ND, NF, 2, 4, 128).transpose(0, 1, 3, 2, 4).reshape(ND, NF * 8, 128)
    wind = wind_field.reshape(2, 2, 4, 128).transpose(0, 2, 1, 3).reshape(16, 128)
    trig = jnp.asarray(TRIG)

    own, low_edge, high_edge = gather_surface(
        ocean_level, ocean_velocity, bathymetry, sea_mask, stress_in
    )
    from_low = shifted(high_edge, "wide", True)
    from_high = shifted(low_edge, "wide", False)
    upper, lower = split_rows(spec)
    halo_low = shifted(upper, both, True)
    halo_high = shifted(lower, both, False)

    parity = (lax.axis_index("deep") & 1).astype(jnp.int32).reshape(1)
    outgoing = surface_step(parity, own, from_low, from_high)
    arrived = lax.all_to_all(outgoing, "deep", split_axis=0, concat_axis=0, tiled=True)

    spec, upper, lower = wave_step(False, trig, spec, halo_low, halo_high, arrived, wind)
    halo_low = shifted(upper, both, True)
    halo_high = shifted(lower, both, False)
    spec, stress = wave_step(True, trig, spec, halo_low, halo_high, arrived, wind)

    stress = lax.all_to_all(stress, "deep", split_axis=0, concat_axis=0, tiled=True)
    stress = stress.reshape(8, 3, 2, 128).transpose(1, 0, 2, 3).reshape(3, 16, 128)
    stress_out = jnp.where(parity[0] == 1, stress[:, :, 64:], stress[:, :, :64])
    spectra_out = (
        spec.reshape(ND, NF, 4, 2, 128).transpose(0, 1, 3, 2, 4).reshape(ND, NF, 2, 512)
    )

    wet_ocean = sea_mask.astype(F32)
    surface = jnp.stack([ocean_level, bathymetry, stress_in[0], stress_in[1], stress_in[2]])
    vel_padded = extended(
        ocean_velocity.reshape(2 * levels, ocean_rows, ocean_cols).astype(BF16),
        (("wide", 1), ("deep", 2)),
        1,
    ).astype(F32)
    surface_padded = extended(surface.astype(BF16), (("wide", 1), ("deep", 2)), 1).astype(F32)
    vel_padded = vel_padded.reshape(2, levels, ocean_rows + 2, ocean_cols + 2)
    velocity_out, level_out = ocean_update(vel_padded, surface_padded, wet_ocean)
    return (level_out, velocity_out, spectra_out, stress_out)


def solution(mesh):
    in_specs = (
        P("wide", "deep"),
        P(None, None, "wide", "deep"),
        P("wide", "deep"),
        P("wide", "deep"),
        P(None, "wide", "deep"),
        P(None, None, ("wide", "deep"), None),
        P(None, ("wide", "deep"), None),
    )
    out_specs = (
        P("wide", "deep"),
        P(None, None, "wide", "deep"),
        P(None, None, ("wide", "deep"), None),
        P(None, "wide", "deep"),
    )
    return jax.shard_map(
        per_device, mesh=mesh, in_specs=in_specs, out_specs=out_specs, check_vma=False
    )
```

```python
import math

import numpy as np

import jax
import jax.numpy as jnp
from jax import lax
from jax.experimental import pallas as pl
from jax.experimental.pallas import tpu as pltpu
from jax.sharding import PartitionSpec as P

LAM_O = 0.2
F_CORIOLIS = 0.1
NU_H = 0.05
KAPPA_V = 0.2
LAM_W = 0.25
GAMMA_BR = 0.73
A_IN = 0.15
C_NL = 0.5
C_WC = 0.002

ND = 36
NF = 36
SIGMA = 0.4 * np.power(1.07, np.arange(NF))
ANGLE = 2.0 * math.pi * np.arange(ND) / ND
TRIG = np.stack([np.cos(ANGLE), np.sin(ANGLE)]).astype(np.float32)

F32 = jnp.float32
BF16 = jnp.bfloat16
VMEM = pltpu.VMEM
SMEM = pltpu.SMEM
HIGH = lax.Precision.HIGHEST


def params(mib):
    return pltpu.CompilerParams(vmem_limit_bytes=mib * 1024 * 1024)


BINS = ND * NF
CELL_ROWS = BINS * 8
PAD = 16
CHUNK = 6


def iotas():
    sub = lax.broadcasted_iota(jnp.int32, (8, 128), 0)
    lane = lax.broadcasted_iota(jnp.int32, (8, 128), 1)
    return sub, lane


def sublane_up(x):
    return pltpu.roll(x, 7, 0)


def sublane_down(x):
    return pltpu.roll(x, 1, 0)


def base_row(d):
    return pl.multiple_of(d * (NF * 8), 8)


def pair_row(ref, start, row):
    return ref[pl.ds(start + row, 8, stride=2), :]


def half_row(d):
    return pl.multiple_of(d * (NF * 4), 16)


HALF_ROWS = BINS * 4


def chunk_copies(source, target, sem):
    def copy(index):
        part = pl.ds(index * CHUNK, CHUNK)
        return pltpu.make_async_copy(source.at[part], target.at[part], sem.at[index])

    return copy


def split_rows_kernel(spec_hbm, wind_ref, upper_ref, lower_ref, held_ref, spec_ref, turn_ref, sem):
    incoming = chunk_copies(spec_hbm, held_ref, sem)
    for index in range(ND // CHUNK):
        incoming(index).start()
    turn_ref[...] = wind_ref[...].astype(F32)
    sides = ((0, lower_ref), (1, upper_ref))
    for row, ref in sides:
        wind = jnp.concatenate([pair_row(turn_ref, 0, row), jnp.zeros((8, 128), F32)], axis=0)
        ref[HALF_ROWS:, :] = wind.astype(BF16)

    def body(d, carry):
        @pl.when(lax.rem(d, CHUNK) == 0)
        def _():
            incoming(lax.div(d, CHUNK)).wait()

        base = base_row(d)
        for quad in range(NF // 4):
            block = held_ref[d, 32 * quad : 32 * quad + 32, :].astype(F32)
            spec_ref[pl.ds(base + 32 * quad, 32), :] = block
        for quad in range(NF // 4):
            start = base + 32 * quad
            for row, ref in sides:
                halves = [pair_row(spec_ref, start + 16 * pair, row) for pair in range(2)]
                packed = jnp.concatenate(halves, axis=0).astype(BF16)
                ref[pl.ds(half_row(d) + 16 * quad, 16), :] = packed
        return carry

    lax.fori_loop(0, ND, body, 0)


def split_rows(spec, wind):
    half = jax.ShapeDtypeStruct((HALF_ROWS + 16, 128), BF16)
    return pl.pallas_call(
        split_rows_kernel,
        out_shape=(half, half),
        in_specs=[pl.BlockSpec(memory_space=pltpu.HBM), pl.BlockSpec(memory_space=VMEM)],
        out_specs=(pl.BlockSpec(memory_space=VMEM),) * 2,
        scratch_shapes=[
            VMEM(spec.shape, BF16),
            VMEM((CELL_ROWS, 128), F32),
            VMEM((16, 128), F32),
            pltpu.SemaphoreType.DMA((ND // CHUNK,)),
        ],
        compiler_params=params(24),
        cost_estimate=pl.CostEstimate(flops=4000000, bytes_accessed=9000000, transcendentals=0),
        name="split_rows",
    )(spec, wind)


FIELDS = 12


def gather_kernel(level_ref, vel_ref, bathy_ref, mask_ref, stress_ref, own_ref, low_ref, high_ref):
    levels = vel_ref.shape[1]
    fields = [
        level_ref[...],
        bathy_ref[...],
        mask_ref[...].astype(F32),
        stress_ref[0],
        stress_ref[1],
        stress_ref[2],
        vel_ref[0, 0],
        vel_ref[1, 0],
        vel_ref[0, 1],
        vel_ref[1, 1],
    ]
    for c in range(2):
        total = vel_ref[c, 0]
        for k in range(1, levels):
            total = total + vel_ref[c, k]
        fields.append(total * (1.0 / levels))
    for index, field in enumerate(fields):
        own_ref[index] = field
        low_ref[index] = field[0:8]
        high_ref[index] = field[24:32]
    blocks = levels // 8
    for c in range(2):
        part = slice(FIELDS + blocks * c, FIELDS + blocks * c + blocks)
        low_ref[part] = vel_ref[c, :, 0, :].reshape(blocks, 8, 128)
        high_ref[part] = vel_ref[c, :, 31, :].reshape(blocks, 8, 128)


def gather_surface(level, vel, bathy, mask, stress):
    rows, cols = level.shape
    edge = jax.ShapeDtypeStruct((FIELDS + vel.shape[1] // 4, 8, cols), F32)
    return pl.pallas_call(
        gather_kernel,
        out_shape=(jax.ShapeDtypeStruct((FIELDS, rows, cols), F32), edge, edge),
        in_specs=[pl.BlockSpec(memory_space=VMEM)] * 5,
        out_specs=(pl.BlockSpec(memory_space=VMEM),) * 3,
        compiler_params=params(56),
        cost_estimate=pl.CostEstimate(flops=400000, bytes_accessed=1700000, transcendentals=0),
        name="gather_surface",
    )(level, vel, bathy, mask, stress)


EXT = 48
ROWS_SENT = 6
EDGE_AT = 4 * ROWS_SENT
COLUMNS_AT = 40
SENT_ROWS = COLUMNS_AT + 32


def surface_kernel(place_ref, own_ref, low_ref, high_ref, first_ref, last_ref, out_ref):
    lane = lax.broadcasted_iota(jnp.int32, (EXT, 128), 1)

    def field(index):
        return jnp.concatenate([low_ref[index], own_ref[index], high_ref[index]], axis=0)

    level, bathy, wet, sxx, sxy, syy, u, v, u1, v1, ubar, vbar = [field(i) for i in range(FIELDS)]

    def down(x):
        return pltpu.roll(x, 1, 0)

    def up(x):
        return pltpu.roll(x, EXT - 1, 0)

    def left(x):
        return jnp.where(lane == 0, 0.0, pltpu.roll(x, 1, 1))

    def right(x):
        return jnp.where(lane == 127, 0.0, pltpu.roll(x, 127, 1))

    depth = bathy + level
    inverse = 1.0 / jnp.where(depth > 0.0, depth, 1.0)
    flux_x = depth * ubar
    flux_y = depth * vbar
    divergence = up(flux_x) - down(flux_x) + right(flux_y) - left(flux_y)
    new_depth = bathy + (level - 0.5 * LAM_O * wet * divergence)
    grad_x = 0.5 * (up(level) - down(level))
    grad_y = 0.5 * (right(level) - left(level))
    force_x = -0.5 * (up(sxx) - down(sxx) + (right(sxy) - left(sxy))) * inverse
    force_y = -0.5 * (up(sxy) - down(sxy) + (right(syy) - left(syy))) * inverse
    laplace_u = up(u) + down(u) + right(u) + left(u) - 4.0 * u
    laplace_v = up(v) + down(v) + right(v) + left(v) - 4.0 * v
    new_u = wet * (
        u
        - LAM_O * grad_x
        + F_CORIOLIS * v
        + LAM_O * force_x
        + NU_H * laplace_u
        + KAPPA_V * (u1 - u)
    )
    new_v = wet * (
        v
        - LAM_O * grad_y
        - F_CORIOLIS * u
        + LAM_O * force_y
        + NU_H * laplace_v
        + KAPPA_V * (v1 - v)
    )

    column = lax.broadcasted_iota(jnp.int32, (128, 128), 0)
    target = lax.broadcasted_iota(jnp.int32, (128, 128), 1)
    to_coarse = jnp.where(target == 64 * (place_ref[0] & 1) + (column >> 1), 0.25, 0.0)
    coarse_row = lax.broadcasted_iota(jnp.int32, (24, EXT), 0)
    fine_row = lax.broadcasted_iota(jnp.int32, (24, EXT), 1)
    pair_sum = jnp.where((fine_row >> 1) == coarse_row, 1.0, 0.0)
    stacked = jnp.concatenate([new_u, new_v, new_depth, wet], axis=0)
    narrowed = jnp.dot(stacked, to_coarse, precision=HIGH, preferred_element_type=F32)
    for index in range(4):
        coarse = jnp.dot(
            pair_sum,
            narrowed[EXT * index : EXT * index + EXT],
            precision=HIGH,
            preferred_element_type=F32,
        )
        for strip in range(8):
            first = 2 * strip + 2
            rows = slice(ROWS_SENT * index, ROWS_SENT * index + ROWS_SENT)
            out_ref[strip, rows, :] = coarse[first : first + ROWS_SENT]

    wet_inverse = wet * inverse
    to_right = [u, v, sxy, syy, level, flux_y]
    to_left = [u, v, -sxy, -syy, -level, -flux_y]
    weights = [
        NU_H * wet,
        NU_H * wet,
        0.5 * LAM_O * wet_inverse,
        0.5 * LAM_O * wet_inverse,
        0.5 * LAM_O * wet,
        0.5 * LAM_O * wet,
    ]
    edges = jnp.zeros((EXT, 128), F32)
    for index in range(6):
        edges = jnp.where(lane == index, to_right[index][:, 127:128], edges)
        edges = jnp.where(lane == 8 + index, to_left[index][:, 0:1], edges)
        edges = jnp.where(lane == 16 + index, weights[index][:, 0:1], edges)
        edges = jnp.where(lane == 24 + index, weights[index][:, 127:128], edges)
    for strip in range(8):
        first = 4 * strip + 4
        rows = 2 * ROWS_SENT
        out_ref[strip, EDGE_AT : EDGE_AT + rows, :] = edges[first : first + rows]
        blank = jnp.zeros((COLUMNS_AT - EDGE_AT - rows, 128), F32)
        out_ref[strip, EDGE_AT + rows : COLUMNS_AT, :] = blank
        columns = jnp.where(place_ref[0] == strip - 1, last_ref[...], 0.0)
        columns = jnp.where(place_ref[0] == strip + 1, first_ref[...], columns)
        out_ref[strip, COLUMNS_AT:, :] = columns


def surface_step(place, *operands):
    return pl.pallas_call(
        surface_kernel,
        out_shape=jax.ShapeDtypeStruct((8, SENT_ROWS, 128), F32),
        in_specs=[pl.BlockSpec(memory_space=SMEM)] + [pl.BlockSpec(memory_space=VMEM)] * 5,
        out_specs=pl.BlockSpec(memory_space=VMEM),
        compiler_params=params(16),
        cost_estimate=pl.CostEstimate(flops=2000000, bytes_accessed=400000, transcendentals=0),
        name="surface_step",
    )(place, *operands)


def rounded(x):
    return x.astype(BF16).astype(F32)


def strip_fields(arrived_ref):
    sub, lane = iotas()
    even = (sub & 1) == 0
    base = 64 * (sub & 1)
    edge_sums = []
    for row in range(ROWS_SENT):
        total = None
        for fine in (2 * row, 2 * row + 1):
            edge = arrived_ref[:, EDGE_AT + fine, :]
            from_left = jnp.where(sub == 0, 0.0, sublane_down(edge))
            from_right = jnp.where(sub == 7, 0.0, sublane_up(edge))
            weight = pltpu.roll(edge, 112, 1)
            product = weight * jnp.where(lane < 8, from_left, from_right)
            total = product if total is None else total + product
        edge_sums.append(0.25 * total)

    def tiles(index, row, parts):
        value = arrived_ref[:, ROWS_SENT * index + row + 2, :]
        if parts:
            edge = edge_sums[row + 2]
            left = sum(edge[:, p : p + 1] for p in parts)
            right = sum(edge[:, 8 + p : 9 + p] for p in parts)
            value = value + jnp.where(lane == base, left, 0.0)
            value = value + jnp.where(lane == base + 63, right, 0.0)
        return value

    def field(index, parts):
        def of_rows(first_row, second_row):
            first = tiles(index, first_row, parts)
            second = tiles(index, second_row, parts)
            return jnp.where(even, first + sublane_up(first), second + sublane_down(second))

        return of_rows

    sums = [field(0, (0, 2)), field(1, (1, 3, 4)), field(2, (5,)), field(3, ())]
    u, v, depth = [lambda a, b, get=get: rounded(get(a, b)) for get in sums[:3]]
    return u, v, depth, lambda a, b: jnp.where(sums[3](a, b) > 0.5, 1.0, 0.0)


def propagate_direction(d, trig_ref, rows_of, faces_x, cells, speed_ref, emit):
    first_lane, last_lane, inside, border, face_v, edge_v, half_wet = cells
    along_x = trig_ref[0, d]
    along_y = trig_ref[1, d] * inside
    along_border = trig_ref[1, d] * border
    for quad in range(NF // 4):
        results = []
        for part, (faces, rows) in enumerate(rows_of(d, quad)):
            speed = speed_ref[2 * quad + part]
            speed_x = along_x * speed
            speed_y = along_y * speed
            speed_border = along_border * speed
            flux_x = []
            for (lower, upper), face in zip(faces, faces_x):
                through = speed_x + face
                flux_x.append(through * jnp.where(through > 0.0, lower, upper))
            moved = []
            for row, (here, beyond, entry, exit) in enumerate(rows):
                through = speed_y + face_v[row]
                following = pltpu.roll(jnp.where(first_lane, beyond, here), 127, 1)
                flux = through * jnp.where(through > 0.0, here, following)
                before = pltpu.roll(jnp.where(last_lane, sublane_down(flux), flux), 1, 1)
                lost = jnp.minimum(speed_border + edge_v[row], 0.0) * here
                change = here + (before - flux) + lost
                if entry is not None:
                    change = change + flux_x[entry]
                if exit is not None:
                    change = change - flux_x[exit]
                moved.append(half_wet[row] * change)
            results.append(moved)
        emit(d, quad, results)


def finish_direction(d, trig_ref, rows_of, faces_x, half_wet, speed_ref, emit):
    along_x = trig_ref[0, d]
    for quad in range(NF // 4):
        results = []
        for part, (below, first, second, above, moved) in enumerate(rows_of(d, quad)):
            speed_x = along_x * speed_ref[2 * quad + part]
            through = speed_x + faces_x[0]
            flux_in = through * jnp.where(through > 0.0, below, first)
            through = speed_x + faces_x[1]
            flux_out = through * jnp.where(through > 0.0, second, above)
            results.append([moved[0] + half_wet[0] * flux_in, moved[1] - half_wet[1] * flux_out])
        emit(d, quad, results)


def source_direction(d, trig_ref, moved_ref, damp_ref, rel_x, rel_y, breaking, emit):
    base = base_row(d)
    plus = base_row(lax.rem(d + 2, ND))
    minus = base_row(lax.rem(d + ND - 2, ND))
    wind_along = A_IN * (rel_x * trig_ref[0, d] + rel_y * trig_ref[1, d])
    spreads = {}

    def spread(f):
        if f not in spreads:
            spreads[f] = moved_ref[pl.ds(plus + 8 * f, 8), :] + moved_ref[pl.ds(minus + 8 * f, 8), :]
        return spreads[f]

    for quad in range(NF // 4):
        results = []
        for part in range(4):
            f = 4 * quad + part
            here = moved_ref[pl.ds(base + 8 * f, 8), :]
            growth = jnp.minimum(jnp.maximum(wind_along * float(SIGMA[f]), A_IN), 3.0 * A_IN)
            summed = (growth + damp_ref[f] - here) * here
            if 0 < f < NF - 1:
                summed = summed + (0.5 * C_NL) * spread(f + 1) * spread(f - 1)
            results.append(summed * breaking)
        emit(quad, results)


def by_row(turn_ref, index, field):
    turn_ref[16 * index : 16 * index + 8] = field
    turn_ref[16 * index + 8 : 16 * index + 16] = field
    return [pair_row(turn_ref, 16 * index, row) for row in range(2)]


def pass_cells(turn_ref, v, wet):
    sub, lane = iotas()
    first_lane, last_lane = lane == 0, lane == 127
    block = sub & 3
    inside = jnp.where(last_lane & (block == 3), 0.0, 1.0)
    border = jnp.where(
        first_lane & (block == 0), 1.0, jnp.where(last_lane & (block == 3), -1.0, 0.0)
    )
    half = 0.5 * LAM_W
    face_v, edge_v = [], []
    for v_row in by_row(turn_ref, 0, v):
        after_v = pltpu.roll(jnp.where(first_lane, sublane_up(v_row), v_row), 127, 1)
        face_v.append(inside * (half * (v_row + after_v)))
        edge_v.append(border * (half * v_row))
    half_wet = [0.5 * wet_row for wet_row in by_row(turn_ref, 1, wet)]
    return first_lane, last_lane, inside, border, face_v, edge_v, half_wet


def set_speeds(speed_ref):
    sub, _ = iotas()
    for pair in range(NF // 2):
        low, high = [float(LAM_W * 0.5 / SIGMA[2 * pair + i]) for i in range(2)]
        speed_ref[pair] = jnp.where(sub < 4, low, high)


def each_direction(body):
    lax.fori_loop(0, ND, lambda d, carry: body(d) or carry, 0)


def summing(moved_ref, sums_ref):
    for f in range(NF):
        sums_ref[f] = jnp.zeros((8, 128), F32)

    def emit(d, quad, results):
        for part, moved in enumerate(results):
            pair = 2 * quad + part
            for row in range(2):
                moved_ref[pl.ds(base_row(d) + 16 * pair + row, 8, stride=2), :] = moved[row]
                sums_ref[2 * pair + row] += moved[row]

    return emit


def packing(refs):
    def emit(d, quad, results):
        for row, ref in enumerate(refs):
            block = jnp.concatenate([moved[row] for moved in results], axis=0)
            ref[pl.ds(half_row(d) + 16 * quad, 16), :] = block.astype(BF16)

    return emit


def source_pass(trig_ref, u, v, depth, wet, wind, scratch, emit, initial=0, combine=None):
    moved_ref, damp_ref, sums_ref, turn_ref = scratch
    sub, _ = iotas()
    zeros = jnp.zeros((8, 128), F32)
    for row in range(2):
        zeroth, second = zeros, zeros
        for pair in range(NF // 2):
            low, high = [float(SIGMA[2 * pair + i] ** 2) for i in range(2)]
            zeroth = zeroth + sums_ref[2 * pair + row]
            second = second + sums_ref[2 * pair + row] * jnp.where(sub < 4, low, high)
        for index, value in ((2, zeroth), (3, second)):
            turn_ref[pl.ds(16 * index + row, 8, stride=2), :] = value + pltpu.roll(value, 4, 0)
    moment_zero = turn_ref[32:40] * (2.0 / BINS)
    moment_two = turn_ref[48:56] * (2.0 / BINS)
    limit = (GAMMA_BR * depth) * (GAMMA_BR * depth)
    breaking = jnp.where(wet > 0.5, 2.0 * limit / jnp.maximum(16.0 * moment_zero, limit), 0.0)
    for f in range(NF):
        damp_ref[f] = (1.0 - A_IN) - float(C_WC * SIGMA[f] ** 3) * moment_two
    rel_x = wind[0] - u
    rel_y = wind[1] - v

    def source(d, carried):
        parts = []
        source_direction(
            d,
            trig_ref,
            moved_ref,
            damp_ref,
            rel_x,
            rel_y,
            breaking,
            lambda quad, results: parts.append(emit(d, quad, results)),
        )
        return combine(d, carried, parts) if combine else carried

    return lax.fori_loop(0, ND, source, initial)


def packed_rows(refs, d, quad):
    blocks = [ref[pl.ds(half_row(d) + 16 * quad, 16), :].astype(F32) for ref in refs]
    return [[block[8 * part : 8 * part + 8] for block in blocks] for part in range(2)]


def wave_scratch():
    return [
        VMEM((CELL_ROWS, 128), F32),
        VMEM((NF, 8, 128), F32),
        VMEM((NF, 8, 128), F32),
        VMEM((64, 128), F32),
        VMEM((NF // 2, 8, 128), F32),
    ]


def first_kernel(
    trig_ref,
    upper_ref,
    lower_ref,
    above_ref,
    below_ref,
    arrived_ref,
    wind_ref,
    spec_lower_ref,
    spec_upper_ref,
    near_above_ref,
    near_below_ref,
    next_lower_ref,
    next_upper_ref,
    spec_ref,
    *scratch,
):
    moved_ref, damp_ref, sums_ref, turn_ref, speed_ref = scratch
    u, v, depth, wet = strip_fields(arrived_ref)
    u_own, u_near = u(0, 1), u(-1, 2)
    own = by_row(turn_ref, 0, u_own)
    near = by_row(turn_ref, 1, u_near)
    half = 0.5 * LAM_W
    face_low = half * (near[0] + own[0])
    face_own = half * (own[0] + own[1])
    face_high = half * (own[1] + near[1])
    wind = wind_ref[...].astype(F32)
    set_speeds(speed_ref)
    v_own, wet_own = v(0, 1), wet(0, 1)
    cells = pass_cells(turn_ref, v_own, wet_own)

    def rows_first(d, quad):
        return [
            (
                [(above, lower), (lower, upper), (upper, below)],
                [(lower, sublane_up(lower), 0, 1), (upper, sublane_up(upper), 1, 2)],
            )
            for above, lower, upper, below in packed_rows(
                (above_ref, lower_ref, upper_ref, below_ref), d, quad
            )
        ]

    emit = summing(moved_ref, sums_ref)
    faces = (face_low, face_own, face_high)
    each_direction(
        lambda d: propagate_direction(d, trig_ref, rows_first, faces, cells, speed_ref, emit)
    )

    def emit_spec(d, quad, results):
        start = base_row(d) + 32 * quad
        spec_ref[pl.ds(start, 32), :] = jnp.concatenate(results, axis=0)
        for row, ref in ((0, spec_lower_ref), (1, spec_upper_ref)):
            halves = [pair_row(spec_ref, start + 16 * pair, row) for pair in range(2)]
            packed = jnp.concatenate(halves, axis=0).astype(BF16)
            ref[pl.ds(half_row(d) + 16 * quad, 16), :] = packed

    source_pass(
        trig_ref,
        u_own,
        v_own,
        depth(0, 1),
        wet_own,
        (wind[0:8], wind[8:16]),
        (moved_ref, damp_ref, sums_ref, turn_ref),
        emit_spec,
    )

    def rows_second(d, quad):
        return [
            (
                [(lower, upper)],
                [(lower, sublane_up(lower), None, 0), (upper, sublane_up(upper), 0, None)],
            )
            for lower, upper in packed_rows((spec_lower_ref, spec_upper_ref), d, quad)
        ]

    emit_next = packing((next_lower_ref, next_upper_ref))
    each_direction(
        lambda d: propagate_direction(
            d, trig_ref, rows_second, (face_own,), cells, speed_ref, emit_next
        )
    )

    cells_near = pass_cells(turn_ref, v(-1, 2), wet(-1, 2))

    def rows_near(d, quad):
        return [
            (
                [(above, lower), (upper, below)],
                [(above, sublane_up(above), None, 0), (below, sublane_up(below), 1, None)],
            )
            for above, lower, upper, below in packed_rows(
                (above_ref, lower_ref, upper_ref, below_ref), d, quad
            )
        ]

    emit_near = packing((near_above_ref, near_below_ref))
    each_direction(
        lambda d: propagate_direction(
            d, trig_ref, rows_near, (face_low, face_high), cells_near, speed_ref, emit_near
        )
    )


def second_kernel(
    trig_ref,
    above_ref,
    below_ref,
    far_above_ref,
    far_below_ref,
    spec_lower_ref,
    spec_upper_ref,
    near_above_ref,
    near_below_ref,
    next_lower_ref,
    next_upper_ref,
    arrived_ref,
    wind_ref,
    out_hbm,
    stress_ref,
    near_ref,
    out_ref,
    sem,
    *scratch,
):
    moved_ref, damp_ref, sums_ref, turn_ref, speed_ref = scratch
    shared = (moved_ref, damp_ref, sums_ref, turn_ref)
    u, v, depth, wet = strip_fields(arrived_ref)
    u_own, u_near = u(0, 1), u(-1, 2)
    own = by_row(turn_ref, 0, u_own)
    near = by_row(turn_ref, 1, u_near)
    far = by_row(turn_ref, 2, u(-2, 3))
    half = 0.5 * LAM_W
    faces_near = (half * (far[0] + near[0]), half * (near[1] + far[1]))
    faces_own = (half * (near[0] + own[0]), half * (own[1] + near[1]))
    for row, ref in ((0, above_ref), (1, below_ref)):
        arrived_wind = ref[HALF_ROWS:, :].astype(F32)[0:8]
        turn_ref[pl.ds(48 + row, 8, stride=2), :] = arrived_wind
    wind_near = (turn_ref[48:56], turn_ref[56:64])
    wind = wind_ref[...].astype(F32)
    wet_own, wet_near = wet(0, 1), wet(-1, 2)
    half_near = [0.5 * row for row in by_row(turn_ref, 0, wet_near)]
    half_own = [0.5 * row for row in by_row(turn_ref, 1, wet_own)]
    set_speeds(speed_ref)

    def rows_near(d, quad):
        refs = (far_above_ref, above_ref, below_ref, far_below_ref, near_above_ref, near_below_ref)
        return [(*rows[:4], rows[4:]) for rows in packed_rows(refs, d, quad)]

    emit = summing(moved_ref, sums_ref)
    each_direction(
        lambda d: finish_direction(d, trig_ref, rows_near, faces_near, half_near, speed_ref, emit)
    )

    def emit_near(d, quad, results):
        near_ref[pl.ds(base_row(d) + 32 * quad, 32), :] = jnp.concatenate(results, axis=0)

    source_pass(
        trig_ref, u_near, v(-1, 2), depth(-1, 2), wet_near, wind_near, shared, emit_near
    )

    def rows_own(d, quad):
        refs = (spec_lower_ref, spec_upper_ref, next_lower_ref, next_upper_ref)
        parts = []
        for part, rows in enumerate(packed_rows(refs, d, quad)):
            start = base_row(d) + 32 * quad + 16 * part
            below, above = [pair_row(near_ref, start, row) for row in range(2)]
            parts.append((below, rows[0], rows[1], above, rows[2:]))
        return parts

    emit = summing(moved_ref, sums_ref)
    each_direction(
        lambda d: finish_direction(d, trig_ref, rows_own, faces_own, half_own, speed_ref, emit)
    )
    outgoing = chunk_copies(out_ref, out_hbm, sem)
    zeros = jnp.zeros((8, 128), F32)

    def emit_own(d, quad, results):
        packed = jnp.concatenate(results, axis=0).astype(BF16)
        out_ref[d, 32 * quad : 32 * quad + 32, :] = packed
        scales = [float(math.pi / ND * SIGMA[4 * quad + part] / NF) for part in range(4)]
        return sum(result * scale for result, scale in zip(results, scales))

    def add_stress(d, totals, parts):
        @pl.when(lax.rem(d, CHUNK) == CHUNK - 1)
        def _():
            outgoing(lax.div(d, CHUNK)).start()

        total = sum(parts)
        cos_d, sin_d = trig_ref[0, d], trig_ref[1, d]
        xx, xy, yy = totals
        return (
            xx + total * (cos_d * cos_d),
            xy + total * (cos_d * sin_d),
            yy + total * (sin_d * sin_d),
        )

    totals = source_pass(
        trig_ref,
        u_own,
        v(0, 1),
        depth(0, 1),
        wet_own,
        (wind[0:8], wind[8:16]),
        shared,
        emit_own,
        (zeros, zeros, zeros),
        add_stress,
    )
    for c in range(3):
        for tile in range(8):
            part = tile // 2
            stress_ref[tile, 2 * c : 2 * c + 2, :] = totals[c][2 * part : 2 * part + 2]
    for index in range(ND // CHUNK):
        outgoing(index).wait()


def first_step(trig, *operands):
    here = pl.BlockSpec(memory_space=VMEM)
    return pl.pallas_call(
        first_kernel,
        out_shape=(jax.ShapeDtypeStruct((HALF_ROWS, 128), BF16),) * 6,
        in_specs=[pl.BlockSpec(memory_space=SMEM)] + [here] * len(operands),
        out_specs=(here,) * 6,
        scratch_shapes=[VMEM((CELL_ROWS, 128), F32)] + wave_scratch(),
        compiler_params=params(32),
        cost_estimate=pl.CostEstimate(
            flops=100000000, bytes_accessed=60000000, transcendentals=0
        ),
        name="first_wave_step",
    )(trig, *operands)


def second_step(trig, *operands):
    here = pl.BlockSpec(memory_space=VMEM)
    full = jax.ShapeDtypeStruct((ND, NF * 8, 128), BF16)
    return pl.pallas_call(
        second_kernel,
        out_shape=(full, jax.ShapeDtypeStruct((8, 6, 128), F32)),
        in_specs=[pl.BlockSpec(memory_space=SMEM)] + [here] * len(operands),
        out_specs=(pl.BlockSpec(memory_space=pl.ANY), here),
        scratch_shapes=[
            VMEM((CELL_ROWS, 128), F32),
            VMEM(full.shape, BF16),
            pltpu.SemaphoreType.DMA((ND // CHUNK,)),
        ]
        + wave_scratch(),
        compiler_params=params(36),
        cost_estimate=pl.CostEstimate(
            flops=200000000, bytes_accessed=40000000, transcendentals=0
        ),
        name="second_wave_step",
    )(trig, *operands)


def columns_kernel(vel_ref, own_ref, first_ref, last_ref):
    lane = lax.broadcasted_iota(jnp.int32, (32, 128), 1)
    levels = vel_ref.shape[1]
    planes = [vel_ref[c, k] for c in range(2) for k in range(levels)]
    planes += [own_ref[0], own_ref[4], own_ref[5], (own_ref[0] + own_ref[1]) * own_ref[11]]
    first = jnp.zeros((32, 128), F32)
    last = jnp.zeros((32, 128), F32)
    for index, plane in enumerate(planes):
        here = lane == index
        first = jnp.where(here, pltpu.roll(plane, index, 1), first)
        last = jnp.where(here, pltpu.roll(plane, (index + 1) % 128, 1), last)
    first_ref[...] = first
    last_ref[...] = last


def edge_columns(vel, own):
    edge = jax.ShapeDtypeStruct((32, 128), F32)
    return pl.pallas_call(
        columns_kernel,
        out_shape=(edge, edge),
        in_specs=[pl.BlockSpec(memory_space=VMEM)] * 2,
        out_specs=(pl.BlockSpec(memory_space=VMEM),) * 2,
        compiler_params=params(16),
        cost_estimate=pl.CostEstimate(flops=2000000, bytes_accessed=1700000, transcendentals=0),
        name="edge_columns",
    )(vel, own)


def ocean_kernel(place_ref, vel_ref, own_ref, low_ref, high_ref, arrived_ref, out_ref, level_ref):
    row = lax.broadcasted_iota(jnp.int32, (32, 128), 0)
    lane = lax.broadcasted_iota(jnp.int32, (32, 128), 1)
    first_row, last_row = row == 0, row == 31
    first_lane, last_lane = lane == 0, lane == 127
    levels = vel_ref.shape[1]
    place = place_ref[0]
    before = arrived_ref[jnp.maximum(place - 1, 0), COLUMNS_AT:, :]
    before = jnp.where(place > 0, before, 0.0)
    after = arrived_ref[jnp.minimum(place + 1, 7), COLUMNS_AT:, :]
    after = jnp.where(place < 7, after, 0.0)

    def down(x, edge):
        return jnp.where(first_row, edge, pltpu.roll(x, 1, 0))

    def up(x, edge):
        return jnp.where(last_row, edge, pltpu.roll(x, 31, 0))

    def left(x, index):
        return jnp.where(first_lane, before[:, index : index + 1], pltpu.roll(x, 1, 1))

    def right(x, index):
        return jnp.where(last_lane, after[:, index : index + 1], pltpu.roll(x, 127, 1))

    def edge_rows(index):
        return low_ref[index, 7:8, :], high_ref[index, 0:1, :]

    level, bathy, wet, sxx, sxy, syy = [own_ref[i] for i in range(6)]
    ubar, vbar = own_ref[10], own_ref[11]
    edges = [edge_rows(i) for i in range(FIELDS)]
    plane_count = 2 * levels
    depth = bathy + level
    flux_x = depth * ubar
    flux_low = (edges[0][0] + edges[1][0]) * edges[10][0]
    flux_high = (edges[0][1] + edges[1][1]) * edges[10][1]
    flux_y = depth * vbar
    divergence = (
        up(flux_x, flux_high)
        - down(flux_x, flux_low)
        + right(flux_y, plane_count + 3)
        - left(flux_y, plane_count + 3)
    )
    level_ref[...] = level - 0.5 * LAM_O * wet * divergence
    inverse = 1.0 / depth
    grad_x = 0.5 * (up(level, edges[0][1]) - down(level, edges[0][0]))
    grad_y = 0.5 * (right(level, plane_count) - left(level, plane_count))
    xx_x = up(sxx, edges[3][1]) - down(sxx, edges[3][0])
    xy_x = up(sxy, edges[4][1]) - down(sxy, edges[4][0])
    xy_y = right(sxy, plane_count + 1) - left(sxy, plane_count + 1)
    yy_y = right(syy, plane_count + 2) - left(syy, plane_count + 2)
    base = (
        -LAM_O * grad_x - 0.5 * LAM_O * (xx_x + xy_y) * inverse,
        -LAM_O * grad_y - 0.5 * LAM_O * (xy_x + yy_y) * inverse,
    )
    turn = (F_CORIOLIS, -F_CORIOLIS)
    for k in range(levels):
        for c in range(2):
            plane = c * levels + k
            here = vel_ref[c, k]
            other = vel_ref[1 - c, k]
            above = vel_ref[c, max(k - 1, 0)]
            below = vel_ref[c, min(k + 1, levels - 1)]
            block, place = FIELDS + plane // 8, plane % 8
            low = low_ref[block, place : place + 1, :]
            high = high_ref[block, place : place + 1, :]
            around = up(here, high) + down(here, low) + right(here, plane) + left(here, plane)
            tendency = (
                base[c]
                + turn[c] * other
                + NU_H * (around - 4.0 * here)
                + KAPPA_V * (above + below - 2.0 * here)
            )
            out_ref[c, k] = wet * (here + tendency)


def ocean_step(place, vel, *operands):
    return pl.pallas_call(
        ocean_kernel,
        out_shape=(
            jax.ShapeDtypeStruct(vel.shape, F32),
            jax.ShapeDtypeStruct((32, 128), F32),
        ),
        in_specs=[pl.BlockSpec(memory_space=SMEM)] + [pl.BlockSpec(memory_space=VMEM)] * 5,
        out_specs=(pl.BlockSpec(memory_space=VMEM),) * 2,
        compiler_params=params(16),
        cost_estimate=pl.CostEstimate(flops=10000000, bytes_accessed=3000000, transcendentals=0),
        name="ocean_step",
    )(place, vel, *operands)


def shifted(array, axis_name, up):
    count = lax.axis_size(axis_name)
    pairs = [(i, i + 1) for i in range(count - 1)]
    if not up:
        pairs = [(target, source) for source, target in pairs]
    return lax.ppermute(array, axis_name, pairs)


def after(value, *others):
    return lax.optimization_barrier((value,) + others)[0]


def per_device(ocean_level, ocean_velocity, bathymetry, sea_mask, stress_in, spectra, wind_field):
    both = ("wide", "deep")
    spec = spectra.reshape(ND, NF, 2, 4, 128).transpose(0, 1, 3, 2, 4).reshape(ND, NF * 8, 128)
    wind = wind_field.reshape(2, 2, 4, 128).transpose(0, 2, 1, 3).reshape(16, 128)
    trig = jnp.asarray(TRIG)

    own, low_edge, high_edge = gather_surface(
        ocean_level, ocean_velocity, bathymetry, sea_mask, stress_in
    )
    from_low = shifted(high_edge, "wide", True)
    from_high = shifted(low_edge, "wide", False)
    upper, lower = split_rows(after(spec, own), wind)
    first, last = edge_columns(ocean_velocity, own)
    place = lax.axis_index("deep").astype(jnp.int32).reshape(1)
    outgoing = surface_step(place, after(own, upper), from_low, from_high, first, last)
    arrived = lax.all_to_all(outgoing, "deep", split_axis=0, concat_axis=0, tiled=True)

    above = shifted(after(upper, arrived), both, True)
    below = shifted(after(lower, arrived), both, False)
    far_above = shifted(after(lower, arrived), both, True)
    far_below = shifted(after(upper, arrived), both, False)
    velocity_out, level_out = ocean_step(
        place, ocean_velocity, own, from_low, from_high, arrived
    )
    partial = first_step(trig, upper, lower, above, below, after(arrived, level_out), wind)
    spec, stress = second_step(
        trig, above, below, far_above, far_below, *partial, arrived, wind
    )
    stress = lax.all_to_all(stress, "deep", split_axis=0, concat_axis=0, tiled=True)
    stress = stress.reshape(8, 3, 2, 128).transpose(1, 0, 2, 3).reshape(3, 16, 128)
    stress_out = jnp.where((place[0] & 1) == 1, stress[:, :, 64:], stress[:, :, :64])
    spectra_out = (
        spec.reshape(ND, NF, 4, 2, 128).transpose(0, 1, 3, 2, 4).reshape(ND, NF, 2, 512)
    )
    return (level_out, velocity_out, spectra_out, stress_out)


def solution(mesh):
    in_specs = (
        P("wide", "deep"),
        P(None, None, "wide", "deep"),
        P("wide", "deep"),
        P("wide", "deep"),
        P(None, "wide", "deep"),
        P(None, None, ("wide", "deep"), None),
        P(None, ("wide", "deep"), None),
    )
    out_specs = (
        P("wide", "deep"),
        P(None, None, "wide", "deep"),
        P(None, None, ("wide", "deep"), None),
        P(None, "wide", "deep"),
    )
    return jax.shard_map(
        per_device, mesh=mesh, in_specs=in_specs, out_specs=out_specs, check_vma=False
    )
```

```python
import math

import numpy as np

import jax
import jax.numpy as jnp
from jax import lax
from jax.experimental import pallas as pl
from jax.experimental.pallas import tpu as pltpu
from jax.sharding import PartitionSpec as P

LAM_O = 0.2
F_CORIOLIS = 0.1
NU_H = 0.05
KAPPA_V = 0.2
LAM_W = 0.25
GAMMA_BR = 0.73
A_IN = 0.15
C_NL = 0.5
C_WC = 0.002

ND = 36
NF = 36
SIGMA = 0.4 * np.power(1.07, np.arange(NF))
ANGLE = 2.0 * math.pi * np.arange(ND) / ND
TRIG = np.stack([np.cos(ANGLE), np.sin(ANGLE)]).astype(np.float32)

F32 = jnp.float32
BF16 = jnp.bfloat16
VMEM = pltpu.VMEM
SMEM = pltpu.SMEM
HIGH = lax.Precision.HIGHEST


def params(mib):
    return pltpu.CompilerParams(vmem_limit_bytes=mib * 1024 * 1024)


BINS = ND * NF
CELL_ROWS = BINS * 8
PAD = 16
CHUNK = 6


def iotas():
    sub = lax.broadcasted_iota(jnp.int32, (8, 128), 0)
    lane = lax.broadcasted_iota(jnp.int32, (8, 128), 1)
    return sub, lane


def sublane_up(x):
    return pltpu.roll(x, 7, 0)


def sublane_down(x):
    return pltpu.roll(x, 1, 0)


def base_row(d):
    return pl.multiple_of(d * (NF * 8), 8)


def pair_row(ref, start, row):
    return ref[pl.ds(start + row, 8, stride=2), :]


def half_row(d):
    return pl.multiple_of(d * (NF * 4), 16)


HALF_ROWS = BINS * 4


def chunk_copies(source, target, sem):
    def copy(index):
        part = pl.ds(index * CHUNK, CHUNK)
        return pltpu.make_async_copy(source.at[part], target.at[part], sem.at[index])

    return copy


def split_rows_kernel(spec_hbm, wind_ref, upper_ref, lower_ref, held_ref, spec_ref, turn_ref, sem):
    incoming = chunk_copies(spec_hbm, held_ref, sem)
    for index in range(ND // CHUNK):
        incoming(index).start()
    turn_ref[...] = wind_ref[...].astype(F32)
    sides = ((0, lower_ref), (1, upper_ref))
    for row, ref in sides:
        wind = jnp.concatenate([pair_row(turn_ref, 0, row), jnp.zeros((8, 128), F32)], axis=0)
        ref[HALF_ROWS:, :] = wind.astype(BF16)

    def body(d, carry):
        @pl.when(lax.rem(d, CHUNK) == 0)
        def _():
            incoming(lax.div(d, CHUNK)).wait()

        base = base_row(d)
        for quad in range(NF // 4):
            block = held_ref[d, 32 * quad : 32 * quad + 32, :].astype(F32)
            spec_ref[pl.ds(base + 32 * quad, 32), :] = block
        for quad in range(NF // 4):
            start = base + 32 * quad
            for row, ref in sides:
                halves = [pair_row(spec_ref, start + 16 * pair, row) for pair in range(2)]
                packed = jnp.concatenate(halves, axis=0).astype(BF16)
                ref[pl.ds(half_row(d) + 16 * quad, 16), :] = packed
        return carry

    lax.fori_loop(0, ND, body, 0)


def split_rows(spec, wind):
    half = jax.ShapeDtypeStruct((HALF_ROWS + 16, 128), BF16)
    return pl.pallas_call(
        split_rows_kernel,
        out_shape=(half, half),
        in_specs=[pl.BlockSpec(memory_space=pltpu.HBM), pl.BlockSpec(memory_space=VMEM)],
        out_specs=(pl.BlockSpec(memory_space=VMEM),) * 2,
        scratch_shapes=[
            VMEM(spec.shape, BF16),
            VMEM((CELL_ROWS, 128), F32),
            VMEM((16, 128), F32),
            pltpu.SemaphoreType.DMA((ND // CHUNK,)),
        ],
        compiler_params=params(56),
        cost_estimate=pl.CostEstimate(flops=4000000, bytes_accessed=9000000, transcendentals=0),
        name="split_rows",
    )(spec, wind)


FIELDS = 12


def edge_columns(planes):
    lane = lax.broadcasted_iota(jnp.int32, (32, 128), 1)
    first = jnp.zeros((32, 128), F32)
    last = jnp.zeros((32, 128), F32)
    for index, plane in enumerate(planes):
        here = lane == index
        first = jnp.where(here, pltpu.roll(plane, index, 1), first)
        last = jnp.where(here, pltpu.roll(plane, (index + 1) % 128, 1), last)
    return first, last


def gather_kernel(
    level_ref,
    vel_ref,
    bathy_ref,
    mask_ref,
    stress_ref,
    own_ref,
    low_ref,
    high_ref,
    first_ref,
    last_ref,
):
    levels = vel_ref.shape[1]
    fields = [
        level_ref[...],
        bathy_ref[...],
        mask_ref[...].astype(F32),
        stress_ref[0],
        stress_ref[1],
        stress_ref[2],
        vel_ref[0, 0],
        vel_ref[1, 0],
        vel_ref[0, 1],
        vel_ref[1, 1],
    ]
    for c in range(2):
        total = vel_ref[c, 0]
        for k in range(1, levels):
            total = total + vel_ref[c, k]
        fields.append(total * (1.0 / levels))
    for index, field in enumerate(fields):
        own_ref[index] = field
        low_ref[index] = field[0:8]
        high_ref[index] = field[24:32]
    blocks = levels // 8
    for c in range(2):
        part = slice(FIELDS + blocks * c, FIELDS + blocks * c + blocks)
        low_ref[part] = vel_ref[c, :, 0, :].reshape(blocks, 8, 128)
        high_ref[part] = vel_ref[c, :, 31, :].reshape(blocks, 8, 128)
    planes = [vel_ref[c, k] for c in range(2) for k in range(levels)]
    planes += [fields[0], fields[4], fields[5], (fields[0] + fields[1]) * fields[11]]
    first_ref[...], last_ref[...] = edge_columns(planes)


def gather_surface(level, vel, bathy, mask, stress):
    rows, cols = level.shape
    edge = jax.ShapeDtypeStruct((FIELDS + vel.shape[1] // 4, 8, cols), F32)
    column = jax.ShapeDtypeStruct((rows, cols), F32)
    return pl.pallas_call(
        gather_kernel,
        out_shape=(jax.ShapeDtypeStruct((FIELDS, rows, cols), F32), edge, edge, column, column),
        in_specs=[pl.BlockSpec(memory_space=VMEM)] * 5,
        out_specs=(pl.BlockSpec(memory_space=VMEM),) * 5,
        compiler_params=params(56),
        cost_estimate=pl.CostEstimate(flops=400000, bytes_accessed=1700000, transcendentals=0),
        name="gather_surface",
    )(level, vel, bathy, mask, stress)


EXT = 48
ROWS_SENT = 6
EDGE_AT = 4 * ROWS_SENT
COLUMNS_AT = 40
SENT_ROWS = COLUMNS_AT + 32


def surface_kernel(place_ref, own_ref, low_ref, high_ref, first_ref, last_ref, out_ref):
    lane = lax.broadcasted_iota(jnp.int32, (EXT, 128), 1)

    def field(index):
        return jnp.concatenate([low_ref[index], own_ref[index], high_ref[index]], axis=0)

    level, bathy, wet, sxx, sxy, syy, u, v, u1, v1, ubar, vbar = [field(i) for i in range(FIELDS)]

    def down(x):
        return pltpu.roll(x, 1, 0)

    def up(x):
        return pltpu.roll(x, EXT - 1, 0)

    def left(x):
        return jnp.where(lane == 0, 0.0, pltpu.roll(x, 1, 1))

    def right(x):
        return jnp.where(lane == 127, 0.0, pltpu.roll(x, 127, 1))

    depth = bathy + level
    inverse = 1.0 / jnp.where(depth > 0.0, depth, 1.0)
    flux_x = depth * ubar
    flux_y = depth * vbar
    divergence = up(flux_x) - down(flux_x) + right(flux_y) - left(flux_y)
    new_depth = bathy + (level - 0.5 * LAM_O * wet * divergence)
    grad_x = 0.5 * (up(level) - down(level))
    grad_y = 0.5 * (right(level) - left(level))
    force_x = -0.5 * (up(sxx) - down(sxx) + (right(sxy) - left(sxy))) * inverse
    force_y = -0.5 * (up(sxy) - down(sxy) + (right(syy) - left(syy))) * inverse
    laplace_u = up(u) + down(u) + right(u) + left(u) - 4.0 * u
    laplace_v = up(v) + down(v) + right(v) + left(v) - 4.0 * v
    new_u = wet * (
        u
        - LAM_O * grad_x
        + F_CORIOLIS * v
        + LAM_O * force_x
        + NU_H * laplace_u
        + KAPPA_V * (u1 - u)
    )
    new_v = wet * (
        v
        - LAM_O * grad_y
        - F_CORIOLIS * u
        + LAM_O * force_y
        + NU_H * laplace_v
        + KAPPA_V * (v1 - v)
    )

    column = lax.broadcasted_iota(jnp.int32, (128, 128), 0)
    target = lax.broadcasted_iota(jnp.int32, (128, 128), 1)
    to_coarse = jnp.where(target == 64 * (place_ref[0] & 1) + (column >> 1), 0.25, 0.0)
    coarse_row = lax.broadcasted_iota(jnp.int32, (24, EXT), 0)
    fine_row = lax.broadcasted_iota(jnp.int32, (24, EXT), 1)
    pair_sum = jnp.where((fine_row >> 1) == coarse_row, 1.0, 0.0)
    stacked = jnp.concatenate([new_u, new_v, new_depth, wet], axis=0)
    narrowed = jnp.dot(stacked, to_coarse, precision=HIGH, preferred_element_type=F32)
    for index in range(4):
        coarse = jnp.dot(
            pair_sum,
            narrowed[EXT * index : EXT * index + EXT],
            precision=HIGH,
            preferred_element_type=F32,
        )
        for strip in range(8):
            first = 2 * strip + 2
            rows = slice(ROWS_SENT * index, ROWS_SENT * index + ROWS_SENT)
            out_ref[strip, rows, :] = coarse[first : first + ROWS_SENT]

    wet_inverse = wet * inverse
    to_right = [u, v, sxy, syy, level, flux_y]
    to_left = [u, v, -sxy, -syy, -level, -flux_y]
    weights = [
        NU_H * wet,
        NU_H * wet,
        0.5 * LAM_O * wet_inverse,
        0.5 * LAM_O * wet_inverse,
        0.5 * LAM_O * wet,
        0.5 * LAM_O * wet,
    ]
    edges = jnp.zeros((EXT, 128), F32)
    for index in range(6):
        edges = jnp.where(lane == index, to_right[index][:, 127:128], edges)
        edges = jnp.where(lane == 8 + index, to_left[index][:, 0:1], edges)
        edges = jnp.where(lane == 16 + index, weights[index][:, 0:1], edges)
        edges = jnp.where(lane == 24 + index, weights[index][:, 127:128], edges)
    for strip in range(8):
        first = 4 * strip + 4
        rows = 2 * ROWS_SENT
        out_ref[strip, EDGE_AT : EDGE_AT + rows, :] = edges[first : first + rows]
        blank = jnp.zeros((COLUMNS_AT - EDGE_AT - rows, 128), F32)
        out_ref[strip, EDGE_AT + rows : COLUMNS_AT, :] = blank
        columns = jnp.where(place_ref[0] == strip - 1, last_ref[...], 0.0)
        columns = jnp.where(place_ref[0] == strip + 1, first_ref[...], columns)
        out_ref[strip, COLUMNS_AT:, :] = columns


def surface_step(place, *operands):
    return pl.pallas_call(
        surface_kernel,
        out_shape=jax.ShapeDtypeStruct((8, SENT_ROWS, 128), F32),
        in_specs=[pl.BlockSpec(memory_space=SMEM)] + [pl.BlockSpec(memory_space=VMEM)] * 5,
        out_specs=pl.BlockSpec(memory_space=VMEM),
        compiler_params=params(16),
        cost_estimate=pl.CostEstimate(flops=2000000, bytes_accessed=400000, transcendentals=0),
        name="surface_step",
    )(place, *operands)


def rounded(x):
    return x.astype(BF16).astype(F32)


def strip_fields(arrived_ref):
    sub, lane = iotas()
    even = (sub & 1) == 0
    base = 64 * (sub & 1)
    edge_sums = []
    for row in range(ROWS_SENT):
        total = None
        for fine in (2 * row, 2 * row + 1):
            edge = arrived_ref[:, EDGE_AT + fine, :]
            from_left = jnp.where(sub == 0, 0.0, sublane_down(edge))
            from_right = jnp.where(sub == 7, 0.0, sublane_up(edge))
            weight = pltpu.roll(edge, 112, 1)
            product = weight * jnp.where(lane < 8, from_left, from_right)
            total = product if total is None else total + product
        edge_sums.append(0.25 * total)

    def tiles(index, row, parts):
        value = arrived_ref[:, ROWS_SENT * index + row + 2, :]
        if parts:
            edge = edge_sums[row + 2]
            left = sum(edge[:, p : p + 1] for p in parts)
            right = sum(edge[:, 8 + p : 9 + p] for p in parts)
            value = value + jnp.where(lane == base, left, 0.0)
            value = value + jnp.where(lane == base + 63, right, 0.0)
        return value

    def field(index, parts):
        def of_rows(first_row, second_row):
            first = tiles(index, first_row, parts)
            second = tiles(index, second_row, parts)
            return jnp.where(even, first + sublane_up(first), second + sublane_down(second))

        return of_rows

    sums = [field(0, (0, 2)), field(1, (1, 3, 4)), field(2, (5,)), field(3, ())]
    u, v, depth = [lambda a, b, get=get: rounded(get(a, b)) for get in sums[:3]]
    return u, v, depth, lambda a, b: jnp.where(sums[3](a, b) > 0.5, 1.0, 0.0)


def propagate_direction(d, trig_ref, rows_of, faces_x, cells, speed_ref, emit):
    first_lane, last_lane, inside, border, face_v, edge_v, half_wet = cells
    along_x = trig_ref[0, d]
    along_y = trig_ref[1, d] * inside
    along_border = trig_ref[1, d] * border
    for quad in range(NF // 4):
        results = []
        for part, (faces, rows) in enumerate(rows_of(d, quad)):
            speed = speed_ref[2 * quad + part]
            speed_x = along_x * speed
            speed_y = along_y * speed
            speed_border = along_border * speed
            flux_x = []
            for (lower, upper), face in zip(faces, faces_x):
                through = speed_x + face
                flux_x.append(through * jnp.where(through > 0.0, lower, upper))
            moved = []
            for row, (here, beyond, entry, exit) in enumerate(rows):
                through = speed_y + face_v[row]
                following = pltpu.roll(jnp.where(first_lane, beyond, here), 127, 1)
                flux = through * jnp.where(through > 0.0, here, following)
                before = pltpu.roll(jnp.where(last_lane, sublane_down(flux), flux), 1, 1)
                lost = jnp.minimum(speed_border + edge_v[row], 0.0) * here
                change = here + (before - flux) + lost
                if entry is not None:
                    change = change + flux_x[entry]
                if exit is not None:
                    change = change - flux_x[exit]
                moved.append(half_wet[row] * change)
            results.append(moved)
        emit(d, quad, results)


def finish_direction(d, trig_ref, rows_of, faces_x, half_wet, speed_ref, emit):
    along_x = trig_ref[0, d]
    for quad in range(NF // 4):
        results = []
        for part, (below, first, second, above, moved) in enumerate(rows_of(d, quad)):
            speed_x = along_x * speed_ref[2 * quad + part]
            through = speed_x + faces_x[0]
            flux_in = through * jnp.where(through > 0.0, below, first)
            through = speed_x + faces_x[1]
            flux_out = through * jnp.where(through > 0.0, second, above)
            results.append([moved[0] + half_wet[0] * flux_in, moved[1] - half_wet[1] * flux_out])
        emit(d, quad, results)


def source_direction(d, trig_ref, moved_ref, damp_ref, rel_x, rel_y, breaking, emit):
    base = base_row(d)
    plus = base_row(lax.rem(d + 2, ND))
    minus = base_row(lax.rem(d + ND - 2, ND))
    wind_along = A_IN * (rel_x * trig_ref[0, d] + rel_y * trig_ref[1, d])
    spreads = {}

    def spread(f):
        if f not in spreads:
            spreads[f] = moved_ref[pl.ds(plus + 8 * f, 8), :] + moved_ref[pl.ds(minus + 8 * f, 8), :]
        return spreads[f]

    for quad in range(NF // 4):
        results = []
        for part in range(4):
            f = 4 * quad + part
            here = moved_ref[pl.ds(base + 8 * f, 8), :]
            growth = jnp.minimum(jnp.maximum(wind_along * float(SIGMA[f]), A_IN), 3.0 * A_IN)
            summed = (growth + damp_ref[f] - here) * here
            if 0 < f < NF - 1:
                summed = summed + (0.5 * C_NL) * spread(f + 1) * spread(f - 1)
            results.append(summed * breaking)
        emit(quad, results)


def by_row(turn_ref, index, field):
    turn_ref[16 * index : 16 * index + 8] = field
    turn_ref[16 * index + 8 : 16 * index + 16] = field
    return [pair_row(turn_ref, 16 * index, row) for row in range(2)]


def pass_cells(turn_ref, v, wet):
    sub, lane = iotas()
    first_lane, last_lane = lane == 0, lane == 127
    block = sub & 3
    inside = jnp.where(last_lane & (block == 3), 0.0, 1.0)
    border = jnp.where(
        first_lane & (block == 0), 1.0, jnp.where(last_lane & (block == 3), -1.0, 0.0)
    )
    half = 0.5 * LAM_W
    face_v, edge_v = [], []
    for v_row in by_row(turn_ref, 0, v):
        after_v = pltpu.roll(jnp.where(first_lane, sublane_up(v_row), v_row), 127, 1)
        face_v.append(inside * (half * (v_row + after_v)))
        edge_v.append(border * (half * v_row))
    half_wet = [0.5 * wet_row for wet_row in by_row(turn_ref, 1, wet)]
    return first_lane, last_lane, inside, border, face_v, edge_v, half_wet


def set_speeds(speed_ref):
    sub, _ = iotas()
    for pair in range(NF // 2):
        low, high = [float(LAM_W * 0.5 / SIGMA[2 * pair + i]) for i in range(2)]
        speed_ref[pair] = jnp.where(sub < 4, low, high)


def each_direction(body):
    lax.fori_loop(0, ND, lambda d, carry: body(d) or carry, 0)


def summing(moved_ref, sums_ref):
    for f in range(NF):
        sums_ref[f] = jnp.zeros((8, 128), F32)

    def emit(d, quad, results):
        for part, moved in enumerate(results):
            pair = 2 * quad + part
            for row in range(2):
                moved_ref[pl.ds(base_row(d) + 16 * pair + row, 8, stride=2), :] = moved[row]
                sums_ref[2 * pair + row] += moved[row]

    return emit


def packing(refs):
    def emit(d, quad, results):
        for row, ref in enumerate(refs):
            block = jnp.concatenate([moved[row] for moved in results], axis=0)
            ref[pl.ds(half_row(d) + 16 * quad, 16), :] = block.astype(BF16)

    return emit


def source_pass(trig_ref, u, v, depth, wet, wind, scratch, emit, initial=0, combine=None):
    moved_ref, damp_ref, sums_ref, turn_ref = scratch
    sub, _ = iotas()
    zeros = jnp.zeros((8, 128), F32)
    for row in range(2):
        zeroth, second = zeros, zeros
        for pair in range(NF // 2):
            low, high = [float(SIGMA[2 * pair + i] ** 2) for i in range(2)]
            zeroth = zeroth + sums_ref[2 * pair + row]
            second = second + sums_ref[2 * pair + row] * jnp.where(sub < 4, low, high)
        for index, value in ((2, zeroth), (3, second)):
            turn_ref[pl.ds(16 * index + row, 8, stride=2), :] = value + pltpu.roll(value, 4, 0)
    moment_zero = turn_ref[32:40] * (2.0 / BINS)
    moment_two = turn_ref[48:56] * (2.0 / BINS)
    limit = (GAMMA_BR * depth) * (GAMMA_BR * depth)
    breaking = jnp.where(wet > 0.5, 2.0 * limit / jnp.maximum(16.0 * moment_zero, limit), 0.0)
    for f in range(NF):
        damp_ref[f] = (1.0 - A_IN) - float(C_WC * SIGMA[f] ** 3) * moment_two
    rel_x = wind[0] - u
    rel_y = wind[1] - v

    def source(d, carried):
        parts = []
        source_direction(
            d,
            trig_ref,
            moved_ref,
            damp_ref,
            rel_x,
            rel_y,
            breaking,
            lambda quad, results: parts.append(emit(d, quad, results)),
        )
        return combine(d, carried, parts) if combine else carried

    return lax.fori_loop(0, ND, source, initial)


def packed_rows(refs, d, quad):
    blocks = [ref[pl.ds(half_row(d) + 16 * quad, 16), :].astype(F32) for ref in refs]
    return [[block[8 * part : 8 * part + 8] for block in blocks] for part in range(2)]


def wave_scratch():
    return [
        VMEM((CELL_ROWS, 128), F32),
        VMEM((NF, 8, 128), F32),
        VMEM((NF, 8, 128), F32),
        VMEM((64, 128), F32),
        VMEM((NF // 2, 8, 128), F32),
    ]


def first_kernel(
    trig_ref,
    upper_ref,
    lower_ref,
    above_ref,
    below_ref,
    arrived_ref,
    wind_ref,
    spec_lower_ref,
    spec_upper_ref,
    near_above_ref,
    near_below_ref,
    next_lower_ref,
    next_upper_ref,
    spec_ref,
    *scratch,
):
    moved_ref, damp_ref, sums_ref, turn_ref, speed_ref = scratch
    u, v, depth, wet = strip_fields(arrived_ref)
    u_own, u_near = u(0, 1), u(-1, 2)
    own = by_row(turn_ref, 0, u_own)
    near = by_row(turn_ref, 1, u_near)
    half = 0.5 * LAM_W
    face_low = half * (near[0] + own[0])
    face_own = half * (own[0] + own[1])
    face_high = half * (own[1] + near[1])
    wind = wind_ref[...].astype(F32)
    set_speeds(speed_ref)
    v_own, wet_own = v(0, 1), wet(0, 1)
    cells = pass_cells(turn_ref, v_own, wet_own)

    def rows_first(d, quad):
        return [
            (
                [(above, lower), (lower, upper), (upper, below)],
                [(lower, sublane_up(lower), 0, 1), (upper, sublane_up(upper), 1, 2)],
            )
            for above, lower, upper, below in packed_rows(
                (above_ref, lower_ref, upper_ref, below_ref), d, quad
            )
        ]

    emit = summing(moved_ref, sums_ref)
    faces = (face_low, face_own, face_high)
    each_direction(
        lambda d: propagate_direction(d, trig_ref, rows_first, faces, cells, speed_ref, emit)
    )

    def emit_spec(d, quad, results):
        start = base_row(d) + 32 * quad
        spec_ref[pl.ds(start, 32), :] = jnp.concatenate(results, axis=0)
        for row, ref in ((0, spec_lower_ref), (1, spec_upper_ref)):
            halves = [pair_row(spec_ref, start + 16 * pair, row) for pair in range(2)]
            packed = jnp.concatenate(halves, axis=0).astype(BF16)
            ref[pl.ds(half_row(d) + 16 * quad, 16), :] = packed

    source_pass(
        trig_ref,
        u_own,
        v_own,
        depth(0, 1),
        wet_own,
        (wind[0:8], wind[8:16]),
        (moved_ref, damp_ref, sums_ref, turn_ref),
        emit_spec,
    )

    def rows_second(d, quad):
        return [
            (
                [(lower, upper)],
                [(lower, sublane_up(lower), None, 0), (upper, sublane_up(upper), 0, None)],
            )
            for lower, upper in packed_rows((spec_lower_ref, spec_upper_ref), d, quad)
        ]

    emit_next = packing((next_lower_ref, next_upper_ref))
    each_direction(
        lambda d: propagate_direction(
            d, trig_ref, rows_second, (face_own,), cells, speed_ref, emit_next
        )
    )

    cells_near = pass_cells(turn_ref, v(-1, 2), wet(-1, 2))

    def rows_near(d, quad):
        return [
            (
                [(above, lower), (upper, below)],
                [(above, sublane_up(above), None, 0), (below, sublane_up(below), 1, None)],
            )
            for above, lower, upper, below in packed_rows(
                (above_ref, lower_ref, upper_ref, below_ref), d, quad
            )
        ]

    emit_near = packing((near_above_ref, near_below_ref))
    each_direction(
        lambda d: propagate_direction(
            d, trig_ref, rows_near, (face_low, face_high), cells_near, speed_ref, emit_near
        )
    )


def second_kernel(
    trig_ref,
    above_ref,
    below_ref,
    far_above_ref,
    far_below_ref,
    spec_lower_ref,
    spec_upper_ref,
    near_above_ref,
    near_below_ref,
    next_lower_ref,
    next_upper_ref,
    arrived_ref,
    wind_ref,
    out_hbm,
    stress_ref,
    near_ref,
    out_ref,
    sem,
    *scratch,
):
    moved_ref, damp_ref, sums_ref, turn_ref, speed_ref = scratch
    shared = (moved_ref, damp_ref, sums_ref, turn_ref)
    u, v, depth, wet = strip_fields(arrived_ref)
    u_own, u_near = u(0, 1), u(-1, 2)
    own = by_row(turn_ref, 0, u_own)
    near = by_row(turn_ref, 1, u_near)
    far = by_row(turn_ref, 2, u(-2, 3))
    half = 0.5 * LAM_W
    faces_near = (half * (far[0] + near[0]), half * (near[1] + far[1]))
    faces_own = (half * (near[0] + own[0]), half * (own[1] + near[1]))
    for row, ref in ((0, above_ref), (1, below_ref)):
        arrived_wind = ref[HALF_ROWS:, :].astype(F32)[0:8]
        turn_ref[pl.ds(48 + row, 8, stride=2), :] = arrived_wind
    wind_near = (turn_ref[48:56], turn_ref[56:64])
    wind = wind_ref[...].astype(F32)
    wet_own, wet_near = wet(0, 1), wet(-1, 2)
    half_near = [0.5 * row for row in by_row(turn_ref, 0, wet_near)]
    half_own = [0.5 * row for row in by_row(turn_ref, 1, wet_own)]
    set_speeds(speed_ref)

    def rows_near(d, quad):
        refs = (far_above_ref, above_ref, below_ref, far_below_ref, near_above_ref, near_below_ref)
        return [(*rows[:4], rows[4:]) for rows in packed_rows(refs, d, quad)]

    emit = summing(moved_ref, sums_ref)
    each_direction(
        lambda d: finish_direction(d, trig_ref, rows_near, faces_near, half_near, speed_ref, emit)
    )

    def emit_near(d, quad, results):
        near_ref[pl.ds(base_row(d) + 32 * quad, 32), :] = jnp.concatenate(results, axis=0)

    source_pass(
        trig_ref, u_near, v(-1, 2), depth(-1, 2), wet_near, wind_near, shared, emit_near
    )

    def rows_own(d, quad):
        refs = (spec_lower_ref, spec_upper_ref, next_lower_ref, next_upper_ref)
        parts = []
        for part, rows in enumerate(packed_rows(refs, d, quad)):
            start = base_row(d) + 32 * quad + 16 * part
            below, above = [pair_row(near_ref, start, row) for row in range(2)]
            parts.append((below, rows[0], rows[1], above, rows[2:]))
        return parts

    emit = summing(moved_ref, sums_ref)
    each_direction(
        lambda d: finish_direction(d, trig_ref, rows_own, faces_own, half_own, speed_ref, emit)
    )
    outgoing = chunk_copies(out_ref, out_hbm, sem)
    zeros = jnp.zeros((8, 128), F32)

    def emit_own(d, quad, results):
        packed = jnp.concatenate(results, axis=0).astype(BF16)
        out_ref[d, 32 * quad : 32 * quad + 32, :] = packed
        scales = [float(math.pi / ND * SIGMA[4 * quad + part] / NF) for part in range(4)]
        return sum(result * scale for result, scale in zip(results, scales))

    def add_stress(d, totals, parts):
        @pl.when(lax.rem(d, CHUNK) == CHUNK - 1)
        def _():
            outgoing(lax.div(d, CHUNK)).start()

        total = sum(parts)
        cos_d, sin_d = trig_ref[0, d], trig_ref[1, d]
        xx, xy, yy = totals
        return (
            xx + total * (cos_d * cos_d),
            xy + total * (cos_d * sin_d),
            yy + total * (sin_d * sin_d),
        )

    totals = source_pass(
        trig_ref,
        u_own,
        v(0, 1),
        depth(0, 1),
        wet_own,
        (wind[0:8], wind[8:16]),
        shared,
        emit_own,
        (zeros, zeros, zeros),
        add_stress,
    )
    for c in range(3):
        for tile in range(8):
            part = tile // 2
            stress_ref[tile, 2 * c : 2 * c + 2, :] = totals[c][2 * part : 2 * part + 2]
    for index in range(ND // CHUNK):
        outgoing(index).wait()


def first_step(trig, *operands):
    here = pl.BlockSpec(memory_space=VMEM)
    return pl.pallas_call(
        first_kernel,
        out_shape=(jax.ShapeDtypeStruct((HALF_ROWS, 128), BF16),) * 6,
        in_specs=[pl.BlockSpec(memory_space=SMEM)] + [here] * len(operands),
        out_specs=(here,) * 6,
        scratch_shapes=[VMEM((CELL_ROWS, 128), F32)] + wave_scratch(),
        compiler_params=params(32),
        cost_estimate=pl.CostEstimate(
            flops=100000000, bytes_accessed=60000000, transcendentals=0
        ),
        name="first_wave_step",
    )(trig, *operands)


def second_step(trig, *operands):
    here = pl.BlockSpec(memory_space=VMEM)
    full = jax.ShapeDtypeStruct((ND, NF * 8, 128), BF16)
    return pl.pallas_call(
        second_kernel,
        out_shape=(full, jax.ShapeDtypeStruct((8, 6, 128), F32)),
        in_specs=[pl.BlockSpec(memory_space=SMEM)] + [here] * len(operands),
        out_specs=(pl.BlockSpec(memory_space=pl.ANY), here),
        scratch_shapes=[
            VMEM((CELL_ROWS, 128), F32),
            VMEM(full.shape, BF16),
            pltpu.SemaphoreType.DMA((ND // CHUNK,)),
        ]
        + wave_scratch(),
        compiler_params=params(36),
        cost_estimate=pl.CostEstimate(
            flops=200000000, bytes_accessed=40000000, transcendentals=0
        ),
        name="second_wave_step",
    )(trig, *operands)


def ocean_kernel(place_ref, vel_ref, own_ref, low_ref, high_ref, arrived_ref, out_ref, level_ref):
    row = lax.broadcasted_iota(jnp.int32, (32, 128), 0)
    lane = lax.broadcasted_iota(jnp.int32, (32, 128), 1)
    first_row, last_row = row == 0, row == 31
    first_lane, last_lane = lane == 0, lane == 127
    levels = vel_ref.shape[1]
    place = place_ref[0]
    before = arrived_ref[jnp.maximum(place - 1, 0), COLUMNS_AT:, :]
    before = jnp.where(place > 0, before, 0.0)
    after = arrived_ref[jnp.minimum(place + 1, 7), COLUMNS_AT:, :]
    after = jnp.where(place < 7, after, 0.0)

    def down(x, edge):
        return jnp.where(first_row, edge, pltpu.roll(x, 1, 0))

    def up(x, edge):
        return jnp.where(last_row, edge, pltpu.roll(x, 31, 0))

    def left(x, index):
        return jnp.where(first_lane, before[:, index : index + 1], pltpu.roll(x, 1, 1))

    def right(x, index):
        return jnp.where(last_lane, after[:, index : index + 1], pltpu.roll(x, 127, 1))

    def edge_rows(index):
        return low_ref[index, 7:8, :], high_ref[index, 0:1, :]

    level, bathy, wet, sxx, sxy, syy = [own_ref[i] for i in range(6)]
    ubar, vbar = own_ref[10], own_ref[11]
    edges = [edge_rows(i) for i in range(FIELDS)]
    plane_count = 2 * levels
    depth = bathy + level
    flux_x = depth * ubar
    flux_low = (edges[0][0] + edges[1][0]) * edges[10][0]
    flux_high = (edges[0][1] + edges[1][1]) * edges[10][1]
    flux_y = depth * vbar
    divergence = (
        up(flux_x, flux_high)
        - down(flux_x, flux_low)
        + right(flux_y, plane_count + 3)
        - left(flux_y, plane_count + 3)
    )
    level_ref[...] = level - 0.5 * LAM_O * wet * divergence
    inverse = 1.0 / depth
    grad_x = 0.5 * (up(level, edges[0][1]) - down(level, edges[0][0]))
    grad_y = 0.5 * (right(level, plane_count) - left(level, plane_count))
    xx_x = up(sxx, edges[3][1]) - down(sxx, edges[3][0])
    xy_x = up(sxy, edges[4][1]) - down(sxy, edges[4][0])
    xy_y = right(sxy, plane_count + 1) - left(sxy, plane_count + 1)
    yy_y = right(syy, plane_count + 2) - left(syy, plane_count + 2)
    base = (
        -LAM_O * grad_x - 0.5 * LAM_O * (xx_x + xy_y) * inverse,
        -LAM_O * grad_y - 0.5 * LAM_O * (xy_x + yy_y) * inverse,
    )
    turn = (F_CORIOLIS, -F_CORIOLIS)
    for k in range(levels):
        for c in range(2):
            plane = c * levels + k
            here = vel_ref[c, k]
            other = vel_ref[1 - c, k]
            above = vel_ref[c, max(k - 1, 0)]
            below = vel_ref[c, min(k + 1, levels - 1)]
            block, place = FIELDS + plane // 8, plane % 8
            low = low_ref[block, place : place + 1, :]
            high = high_ref[block, place : place + 1, :]
            around = up(here, high) + down(here, low) + right(here, plane) + left(here, plane)
            tendency = (
                base[c]
                + turn[c] * other
                + NU_H * (around - 4.0 * here)
                + KAPPA_V * (above + below - 2.0 * here)
            )
            out_ref[c, k] = wet * (here + tendency)


def ocean_step(place, vel, *operands):
    return pl.pallas_call(
        ocean_kernel,
        out_shape=(
            jax.ShapeDtypeStruct(vel.shape, F32),
            jax.ShapeDtypeStruct((32, 128), F32),
        ),
        in_specs=[pl.BlockSpec(memory_space=SMEM)] + [pl.BlockSpec(memory_space=VMEM)] * 5,
        out_specs=(pl.BlockSpec(memory_space=VMEM),) * 2,
        compiler_params=params(16),
        cost_estimate=pl.CostEstimate(flops=10000000, bytes_accessed=3000000, transcendentals=0),
        name="ocean_step",
    )(place, vel, *operands)


def shifted(array, axis_name, up):
    count = lax.axis_size(axis_name)
    pairs = [(i, i + 1) for i in range(count - 1)]
    if not up:
        pairs = [(target, source) for source, target in pairs]
    return lax.ppermute(array, axis_name, pairs)


def after(value, *others):
    return lax.optimization_barrier((value,) + others)[0]


def per_device(ocean_level, ocean_velocity, bathymetry, sea_mask, stress_in, spectra, wind_field):
    both = ("wide", "deep")
    spec = spectra.reshape(ND, NF, 2, 4, 128).transpose(0, 1, 3, 2, 4).reshape(ND, NF * 8, 128)
    wind = wind_field.reshape(2, 2, 4, 128).transpose(0, 2, 1, 3).reshape(16, 128)
    trig = jnp.asarray(TRIG)

    own, low_edge, high_edge, first, last = gather_surface(
        ocean_level, ocean_velocity, bathymetry, sea_mask, stress_in
    )
    from_low = shifted(high_edge, "wide", True)
    from_high = shifted(low_edge, "wide", False)
    upper, lower = split_rows(after(spec, own), wind)
    place = lax.axis_index("deep").astype(jnp.int32).reshape(1)
    outgoing = surface_step(place, after(own, upper), from_low, from_high, first, last)
    arrived = lax.all_to_all(outgoing, "deep", split_axis=0, concat_axis=0, tiled=True)

    above = shifted(after(upper, from_low, from_high), both, True)
    below = shifted(after(lower, from_low, from_high), both, False)
    far_above = shifted(after(lower, arrived), both, True)
    far_below = shifted(after(upper, arrived), both, False)
    velocity_out, level_out = ocean_step(
        place, ocean_velocity, own, from_low, from_high, arrived
    )
    partial = first_step(trig, upper, lower, above, below, after(arrived, level_out), wind)
    spec, stress = second_step(
        trig, above, below, far_above, far_below, *partial, arrived, wind
    )
    stress = lax.all_to_all(stress, "deep", split_axis=0, concat_axis=0, tiled=True)
    stress = stress.reshape(8, 3, 2, 128).transpose(1, 0, 2, 3).reshape(3, 16, 128)
    stress_out = jnp.where((place[0] & 1) == 1, stress[:, :, 64:], stress[:, :, :64])
    spectra_out = (
        spec.reshape(ND, NF, 4, 2, 128).transpose(0, 1, 3, 2, 4).reshape(ND, NF, 2, 512)
    )
    return (level_out, velocity_out, spectra_out, stress_out)


def solution(mesh):
    in_specs = (
        P("wide", "deep"),
        P(None, None, "wide", "deep"),
        P("wide", "deep"),
        P("wide", "deep"),
        P(None, "wide", "deep"),
        P(None, None, ("wide", "deep"), None),
        P(None, ("wide", "deep"), None),
    )
    out_specs = (
        P("wide", "deep"),
        P(None, None, "wide", "deep"),
        P(None, None, ("wide", "deep"), None),
        P(None, "wide", "deep"),
    )
    return jax.shard_map(
        per_device, mesh=mesh, in_specs=in_specs, out_specs=out_specs, check_vma=False
    )
```

```python
import math

import numpy as np

import jax
import jax.numpy as jnp
from jax import lax
from jax.experimental import pallas as pl
from jax.experimental.pallas import tpu as pltpu
from jax.sharding import PartitionSpec as P

LAM_O = 0.2
F_CORIOLIS = 0.1
NU_H = 0.05
KAPPA_V = 0.2
LAM_W = 0.25
GAMMA_BR = 0.73
A_IN = 0.15
C_NL = 0.5
C_WC = 0.002

ND = 36
NF = 36
SIGMA = 0.4 * np.power(1.07, np.arange(NF))
ANGLE = 2.0 * math.pi * np.arange(ND) / ND
TRIG = np.stack([np.cos(ANGLE), np.sin(ANGLE)]).astype(np.float32)

F32 = jnp.float32
BF16 = jnp.bfloat16
VMEM = pltpu.VMEM
SMEM = pltpu.SMEM
HIGH = lax.Precision.HIGHEST


def params(mib):
    return pltpu.CompilerParams(vmem_limit_bytes=mib * 1024 * 1024)


BINS = ND * NF
CELL_ROWS = BINS * 8
PAD = 16
CHUNK = 6


def iotas():
    sub = lax.broadcasted_iota(jnp.int32, (8, 128), 0)
    lane = lax.broadcasted_iota(jnp.int32, (8, 128), 1)
    return sub, lane


def sublane_up(x):
    return pltpu.roll(x, 7, 0)


def sublane_down(x):
    return pltpu.roll(x, 1, 0)


def base_row(d):
    return pl.multiple_of(d * (NF * 8), 8)


def pair_row(ref, start, row):
    return ref[pl.ds(start + row, 8, stride=2), :]


def half_row(d):
    return pl.multiple_of(d * (NF * 4), 16)


HALF_ROWS = BINS * 4


def chunk_copies(source, target, sem):
    def copy(index):
        part = pl.ds(index * CHUNK, CHUNK)
        return pltpu.make_async_copy(source.at[part], target.at[part], sem.at[index])

    return copy


def split_rows_kernel(spec_hbm, wind_ref, upper_ref, lower_ref, held_ref, spec_ref, turn_ref, sem):
    incoming = chunk_copies(spec_hbm, held_ref, sem)
    for index in range(ND // CHUNK):
        incoming(index).start()
    turn_ref[...] = wind_ref[...].astype(F32)
    sides = ((0, lower_ref), (1, upper_ref))
    for row, ref in sides:
        wind = jnp.concatenate([pair_row(turn_ref, 0, row), jnp.zeros((8, 128), F32)], axis=0)
        ref[HALF_ROWS:, :] = wind.astype(BF16)

    def body(d, carry):
        @pl.when(lax.rem(d, CHUNK) == 0)
        def _():
            incoming(lax.div(d, CHUNK)).wait()

        base = base_row(d)
        for quad in range(NF // 4):
            block = held_ref[d, 32 * quad : 32 * quad + 32, :].astype(F32)
            spec_ref[pl.ds(base + 32 * quad, 32), :] = block
        for quad in range(NF // 4):
            start = base + 32 * quad
            for row, ref in sides:
                halves = [pair_row(spec_ref, start + 16 * pair, row) for pair in range(2)]
                packed = jnp.concatenate(halves, axis=0).astype(BF16)
                ref[pl.ds(half_row(d) + 16 * quad, 16), :] = packed
        return carry

    lax.fori_loop(0, ND, body, 0)


def split_rows(spec, wind):
    half = jax.ShapeDtypeStruct((HALF_ROWS + 16, 128), BF16)
    return pl.pallas_call(
        split_rows_kernel,
        out_shape=(half, half),
        in_specs=[pl.BlockSpec(memory_space=pltpu.HBM), pl.BlockSpec(memory_space=VMEM)],
        out_specs=(pl.BlockSpec(memory_space=VMEM),) * 2,
        scratch_shapes=[
            VMEM(spec.shape, BF16),
            VMEM((CELL_ROWS, 128), F32),
            VMEM((16, 128), F32),
            pltpu.SemaphoreType.DMA((ND // CHUNK,)),
        ],
        compiler_params=params(56),
        cost_estimate=pl.CostEstimate(flops=4000000, bytes_accessed=9000000, transcendentals=0),
        name="split_rows",
    )(spec, wind)


FIELDS = 12


def edge_columns(planes):
    lane = lax.broadcasted_iota(jnp.int32, (32, 128), 1)
    first = jnp.zeros((32, 128), F32)
    last = jnp.zeros((32, 128), F32)
    for index, plane in enumerate(planes):
        here = lane == index
        first = jnp.where(here, pltpu.roll(plane, index, 1), first)
        last = jnp.where(here, pltpu.roll(plane, (index + 1) % 128, 1), last)
    return first, last


def gather_kernel(
    level_ref,
    vel_ref,
    bathy_ref,
    mask_ref,
    stress_ref,
    own_ref,
    low_ref,
    high_ref,
    first_ref,
    last_ref,
):
    levels = vel_ref.shape[1]
    fields = [
        level_ref[...],
        bathy_ref[...],
        mask_ref[...].astype(F32),
        stress_ref[0],
        stress_ref[1],
        stress_ref[2],
        vel_ref[0, 0],
        vel_ref[1, 0],
        vel_ref[0, 1],
        vel_ref[1, 1],
    ]
    for c in range(2):
        total = vel_ref[c, 0]
        for k in range(1, levels):
            total = total + vel_ref[c, k]
        fields.append(total * (1.0 / levels))
    for index, field in enumerate(fields):
        own_ref[index] = field
        low_ref[index] = field[0:8]
        high_ref[index] = field[24:32]
    blocks = levels // 8
    for c in range(2):
        part = slice(FIELDS + blocks * c, FIELDS + blocks * c + blocks)
        low_ref[part] = vel_ref[c, :, 0, :].reshape(blocks, 8, 128)
        high_ref[part] = vel_ref[c, :, 31, :].reshape(blocks, 8, 128)
    planes = [vel_ref[c, k] for c in range(2) for k in range(levels)]
    planes += [fields[0], fields[4], fields[5], (fields[0] + fields[1]) * fields[11]]
    first_ref[...], last_ref[...] = edge_columns(planes)


def gather_surface(level, vel, bathy, mask, stress):
    rows, cols = level.shape
    edge = jax.ShapeDtypeStruct((FIELDS + vel.shape[1] // 4, 8, cols), F32)
    column = jax.ShapeDtypeStruct((rows, cols), F32)
    return pl.pallas_call(
        gather_kernel,
        out_shape=(jax.ShapeDtypeStruct((FIELDS, rows, cols), F32), edge, edge, column, column),
        in_specs=[pl.BlockSpec(memory_space=VMEM)] * 5,
        out_specs=(pl.BlockSpec(memory_space=VMEM),) * 5,
        compiler_params=params(56),
        cost_estimate=pl.CostEstimate(flops=400000, bytes_accessed=1700000, transcendentals=0),
        name="gather_surface",
    )(level, vel, bathy, mask, stress)


EXT = 48
ROWS_SENT = 6
EDGE_AT = 4 * ROWS_SENT
COLUMNS_AT = 40
SENT_ROWS = COLUMNS_AT + 32


def surface_kernel(place_ref, own_ref, low_ref, high_ref, first_ref, last_ref, out_ref):
    lane = lax.broadcasted_iota(jnp.int32, (EXT, 128), 1)

    def field(index):
        return jnp.concatenate([low_ref[index], own_ref[index], high_ref[index]], axis=0)

    level, bathy, wet, sxx, sxy, syy, u, v, u1, v1, ubar, vbar = [field(i) for i in range(FIELDS)]

    def down(x):
        return pltpu.roll(x, 1, 0)

    def up(x):
        return pltpu.roll(x, EXT - 1, 0)

    def left(x):
        return jnp.where(lane == 0, 0.0, pltpu.roll(x, 1, 1))

    def right(x):
        return jnp.where(lane == 127, 0.0, pltpu.roll(x, 127, 1))

    depth = bathy + level
    inverse = 1.0 / jnp.where(depth > 0.0, depth, 1.0)
    flux_x = depth * ubar
    flux_y = depth * vbar
    divergence = up(flux_x) - down(flux_x) + right(flux_y) - left(flux_y)
    new_depth = bathy + (level - 0.5 * LAM_O * wet * divergence)
    grad_x = 0.5 * (up(level) - down(level))
    grad_y = 0.5 * (right(level) - left(level))
    force_x = -0.5 * (up(sxx) - down(sxx) + (right(sxy) - left(sxy))) * inverse
    force_y = -0.5 * (up(sxy) - down(sxy) + (right(syy) - left(syy))) * inverse
    laplace_u = up(u) + down(u) + right(u) + left(u) - 4.0 * u
    laplace_v = up(v) + down(v) + right(v) + left(v) - 4.0 * v
    new_u = wet * (
        u
        - LAM_O * grad_x
        + F_CORIOLIS * v
        + LAM_O * force_x
        + NU_H * laplace_u
        + KAPPA_V * (u1 - u)
    )
    new_v = wet * (
        v
        - LAM_O * grad_y
        - F_CORIOLIS * u
        + LAM_O * force_y
        + NU_H * laplace_v
        + KAPPA_V * (v1 - v)
    )

    column = lax.broadcasted_iota(jnp.int32, (128, 128), 0)
    target = lax.broadcasted_iota(jnp.int32, (128, 128), 1)
    to_coarse = jnp.where(target == 64 * (place_ref[0] & 1) + (column >> 1), 0.25, 0.0)
    coarse_row = lax.broadcasted_iota(jnp.int32, (24, EXT), 0)
    fine_row = lax.broadcasted_iota(jnp.int32, (24, EXT), 1)
    pair_sum = jnp.where((fine_row >> 1) == coarse_row, 1.0, 0.0)
    stacked = jnp.concatenate([new_u, new_v, new_depth, wet], axis=0)
    narrowed = jnp.dot(stacked, to_coarse, precision=HIGH, preferred_element_type=F32)
    for index in range(4):
        coarse = jnp.dot(
            pair_sum,
            narrowed[EXT * index : EXT * index + EXT],
            precision=HIGH,
            preferred_element_type=F32,
        )
        for strip in range(8):
            first = 2 * strip + 2
            rows = slice(ROWS_SENT * index, ROWS_SENT * index + ROWS_SENT)
            out_ref[strip, rows, :] = coarse[first : first + ROWS_SENT]

    wet_inverse = wet * inverse
    to_right = [u, v, sxy, syy, level, flux_y]
    to_left = [u, v, -sxy, -syy, -level, -flux_y]
    weights = [
        NU_H * wet,
        NU_H * wet,
        0.5 * LAM_O * wet_inverse,
        0.5 * LAM_O * wet_inverse,
        0.5 * LAM_O * wet,
        0.5 * LAM_O * wet,
    ]
    edges = jnp.zeros((EXT, 128), F32)
    for index in range(6):
        edges = jnp.where(lane == index, to_right[index][:, 127:128], edges)
        edges = jnp.where(lane == 8 + index, to_left[index][:, 0:1], edges)
        edges = jnp.where(lane == 16 + index, weights[index][:, 0:1], edges)
        edges = jnp.where(lane == 24 + index, weights[index][:, 127:128], edges)
    for strip in range(8):
        first = 4 * strip + 4
        rows = 2 * ROWS_SENT
        out_ref[strip, EDGE_AT : EDGE_AT + rows, :] = edges[first : first + rows]
        blank = jnp.zeros((COLUMNS_AT - EDGE_AT - rows, 128), F32)
        out_ref[strip, EDGE_AT + rows : COLUMNS_AT, :] = blank
        columns = jnp.where(place_ref[0] == strip - 1, last_ref[...], 0.0)
        columns = jnp.where(place_ref[0] == strip + 1, first_ref[...], columns)
        out_ref[strip, COLUMNS_AT:, :] = columns


def surface_step(place, *operands):
    return pl.pallas_call(
        surface_kernel,
        out_shape=jax.ShapeDtypeStruct((8, SENT_ROWS, 128), F32),
        in_specs=[pl.BlockSpec(memory_space=SMEM)] + [pl.BlockSpec(memory_space=VMEM)] * 5,
        out_specs=pl.BlockSpec(memory_space=VMEM),
        compiler_params=params(16),
        cost_estimate=pl.CostEstimate(flops=2000000, bytes_accessed=400000, transcendentals=0),
        name="surface_step",
    )(place, *operands)


def rounded(x):
    return x.astype(BF16).astype(F32)


def strip_fields(arrived_ref):
    sub, lane = iotas()
    even = (sub & 1) == 0
    base = 64 * (sub & 1)
    edge_sums = []
    for row in range(ROWS_SENT):
        total = None
        for fine in (2 * row, 2 * row + 1):
            edge = arrived_ref[:, EDGE_AT + fine, :]
            from_left = jnp.where(sub == 0, 0.0, sublane_down(edge))
            from_right = jnp.where(sub == 7, 0.0, sublane_up(edge))
            weight = pltpu.roll(edge, 112, 1)
            product = weight * jnp.where(lane < 8, from_left, from_right)
            total = product if total is None else total + product
        edge_sums.append(0.25 * total)

    def tiles(index, row, parts):
        value = arrived_ref[:, ROWS_SENT * index + row + 2, :]
        if parts:
            edge = edge_sums[row + 2]
            left = sum(edge[:, p : p + 1] for p in parts)
            right = sum(edge[:, 8 + p : 9 + p] for p in parts)
            value = value + jnp.where(lane == base, left, 0.0)
            value = value + jnp.where(lane == base + 63, right, 0.0)
        return value

    def field(index, parts):
        def of_rows(first_row, second_row):
            first = tiles(index, first_row, parts)
            second = tiles(index, second_row, parts)
            return jnp.where(even, first + sublane_up(first), second + sublane_down(second))

        return of_rows

    sums = [field(0, (0, 2)), field(1, (1, 3, 4)), field(2, (5,)), field(3, ())]
    u, v, depth = [lambda a, b, get=get: rounded(get(a, b)) for get in sums[:3]]
    return u, v, depth, lambda a, b: jnp.where(sums[3](a, b) > 0.5, 1.0, 0.0)


def propagate_direction(d, trig_ref, rows_of, faces_x, cells, speed_ref, emit):
    first_lane, last_lane, inside, border, face_v, edge_v, half_wet = cells
    along_x = trig_ref[0, d]
    along_y = trig_ref[1, d] * inside
    along_border = trig_ref[1, d] * border
    for quad in range(NF // 4):
        results = []
        for part, (faces, rows) in enumerate(rows_of(d, quad)):
            speed = speed_ref[2 * quad + part]
            speed_x = along_x * speed
            speed_y = along_y * speed
            speed_border = along_border * speed
            flux_x = []
            for (lower, upper), face in zip(faces, faces_x):
                through = speed_x + face
                flux_x.append(through * jnp.where(through > 0.0, lower, upper))
            moved = []
            for row, (here, beyond, entry, exit) in enumerate(rows):
                through = speed_y + face_v[row]
                following = pltpu.roll(jnp.where(first_lane, beyond, here), 127, 1)
                flux = through * jnp.where(through > 0.0, here, following)
                before = pltpu.roll(jnp.where(last_lane, sublane_down(flux), flux), 1, 1)
                lost = jnp.minimum(speed_border + edge_v[row], 0.0) * here
                change = here + (before - flux) + lost
                if entry is not None:
                    change = change + flux_x[entry]
                if exit is not None:
                    change = change - flux_x[exit]
                moved.append(half_wet[row] * change)
            results.append(moved)
        emit(d, quad, results)


def finish_direction(d, trig_ref, rows_of, faces_x, half_wet, speed_ref, emit):
    along_x = trig_ref[0, d]
    for quad in range(NF // 4):
        results = []
        for part, (below, first, second, above, moved) in enumerate(rows_of(d, quad)):
            speed_x = along_x * speed_ref[2 * quad + part]
            through = speed_x + faces_x[0]
            flux_in = through * jnp.where(through > 0.0, below, first)
            through = speed_x + faces_x[1]
            flux_out = through * jnp.where(through > 0.0, second, above)
            results.append([moved[0] + half_wet[0] * flux_in, moved[1] - half_wet[1] * flux_out])
        emit(d, quad, results)


def source_direction(d, trig_ref, moved_ref, damp_ref, rel_x, rel_y, breaking, emit):
    base = base_row(d)
    plus = base_row(lax.rem(d + 2, ND))
    minus = base_row(lax.rem(d + ND - 2, ND))
    wind_along = A_IN * (rel_x * trig_ref[0, d] + rel_y * trig_ref[1, d])
    spreads = {}

    def spread(f):
        if f not in spreads:
            spreads[f] = moved_ref[pl.ds(plus + 8 * f, 8), :] + moved_ref[pl.ds(minus + 8 * f, 8), :]
        return spreads[f]

    for quad in range(NF // 4):
        results = []
        for part in range(4):
            f = 4 * quad + part
            here = moved_ref[pl.ds(base + 8 * f, 8), :]
            growth = jnp.minimum(jnp.maximum(wind_along * float(SIGMA[f]), A_IN), 3.0 * A_IN)
            summed = (growth + damp_ref[f] - here) * here
            if 0 < f < NF - 1:
                summed = summed + (0.5 * C_NL) * spread(f + 1) * spread(f - 1)
            results.append(summed * breaking)
        emit(quad, results)


def by_row(turn_ref, index, field):
    turn_ref[16 * index : 16 * index + 8] = field
    turn_ref[16 * index + 8 : 16 * index + 16] = field
    return [pair_row(turn_ref, 16 * index, row) for row in range(2)]


def pass_cells(turn_ref, v, wet):
    sub, lane = iotas()
    first_lane, last_lane = lane == 0, lane == 127
    block = sub & 3
    inside = jnp.where(last_lane & (block == 3), 0.0, 1.0)
    border = jnp.where(
        first_lane & (block == 0), 1.0, jnp.where(last_lane & (block == 3), -1.0, 0.0)
    )
    half = 0.5 * LAM_W
    face_v, edge_v = [], []
    for v_row in by_row(turn_ref, 0, v):
        after_v = pltpu.roll(jnp.where(first_lane, sublane_up(v_row), v_row), 127, 1)
        face_v.append(inside * (half * (v_row + after_v)))
        edge_v.append(border * (half * v_row))
    half_wet = [0.5 * wet_row for wet_row in by_row(turn_ref, 1, wet)]
    return first_lane, last_lane, inside, border, face_v, edge_v, half_wet


def set_speeds(speed_ref):
    sub, _ = iotas()
    for pair in range(NF // 2):
        low, high = [float(LAM_W * 0.5 / SIGMA[2 * pair + i]) for i in range(2)]
        speed_ref[pair] = jnp.where(sub < 4, low, high)


def each_direction(body):
    lax.fori_loop(0, ND, lambda d, carry: body(d) or carry, 0)


def summing(moved_ref, sums_ref):
    for f in range(NF):
        sums_ref[f] = jnp.zeros((8, 128), F32)

    def emit(d, quad, results):
        for part, moved in enumerate(results):
            pair = 2 * quad + part
            for row in range(2):
                moved_ref[pl.ds(base_row(d) + 16 * pair + row, 8, stride=2), :] = moved[row]
                sums_ref[2 * pair + row] += moved[row]

    return emit


def packing(refs):
    def emit(d, quad, results):
        for row, ref in enumerate(refs):
            block = jnp.concatenate([moved[row] for moved in results], axis=0)
            ref[pl.ds(half_row(d) + 16 * quad, 16), :] = block.astype(BF16)

    return emit


def source_pass(trig_ref, u, v, depth, wet, wind, scratch, emit, initial=0, combine=None):
    moved_ref, damp_ref, sums_ref, turn_ref = scratch
    sub, _ = iotas()
    zeros = jnp.zeros((8, 128), F32)
    for row in range(2):
        zeroth, second = zeros, zeros
        for pair in range(NF // 2):
            low, high = [float(SIGMA[2 * pair + i] ** 2) for i in range(2)]
            zeroth = zeroth + sums_ref[2 * pair + row]
            second = second + sums_ref[2 * pair + row] * jnp.where(sub < 4, low, high)
        for index, value in ((2, zeroth), (3, second)):
            turn_ref[pl.ds(16 * index + row, 8, stride=2), :] = value + pltpu.roll(value, 4, 0)
    moment_zero = turn_ref[32:40] * (2.0 / BINS)
    moment_two = turn_ref[48:56] * (2.0 / BINS)
    limit = (GAMMA_BR * depth) * (GAMMA_BR * depth)
    breaking = jnp.where(wet > 0.5, 2.0 * limit / jnp.maximum(16.0 * moment_zero, limit), 0.0)
    for f in range(NF):
        damp_ref[f] = (1.0 - A_IN) - float(C_WC * SIGMA[f] ** 3) * moment_two
    rel_x = wind[0] - u
    rel_y = wind[1] - v

    def source(d, carried):
        parts = []
        source_direction(
            d,
            trig_ref,
            moved_ref,
            damp_ref,
            rel_x,
            rel_y,
            breaking,
            lambda quad, results: parts.append(emit(d, quad, results)),
        )
        return combine(d, carried, parts) if combine else carried

    return lax.fori_loop(0, ND, source, initial)


def packed_rows(refs, d, quad):
    blocks = [ref[pl.ds(half_row(d) + 16 * quad, 16), :].astype(F32) for ref in refs]
    return [[block[8 * part : 8 * part + 8] for block in blocks] for part in range(2)]


def wave_scratch():
    return [
        VMEM((CELL_ROWS, 128), F32),
        VMEM((NF, 8, 128), F32),
        VMEM((NF, 8, 128), F32),
        VMEM((64, 128), F32),
        VMEM((NF // 2, 8, 128), F32),
    ]


def inner_rows(refs, d, quad):
    return [
        (
            [(lower, upper)],
            [(lower, sublane_up(lower), None, 0), (upper, sublane_up(upper), 0, None)],
        )
        for lower, upper in packed_rows(refs, d, quad)
    ]


def begin_kernel(
    trig_ref, upper_ref, lower_ref, arrived_ref, part_lower_ref, part_upper_ref, turn_ref, speed_ref
):
    u, v, _, wet = strip_fields(arrived_ref)
    own = by_row(turn_ref, 0, u(0, 1))
    face_own = (0.5 * LAM_W) * (own[0] + own[1])
    set_speeds(speed_ref)
    cells = pass_cells(turn_ref, v(0, 1), wet(0, 1))

    def rows_own(d, quad):
        return inner_rows((lower_ref, upper_ref), d, quad)

    emit = packing((part_lower_ref, part_upper_ref))
    each_direction(
        lambda d: propagate_direction(d, trig_ref, rows_own, (face_own,), cells, speed_ref, emit)
    )


def begin_step(trig, *operands):
    here = pl.BlockSpec(memory_space=VMEM)
    return pl.pallas_call(
        begin_kernel,
        out_shape=(jax.ShapeDtypeStruct((HALF_ROWS, 128), BF16),) * 2,
        in_specs=[pl.BlockSpec(memory_space=SMEM)] + [here] * len(operands),
        out_specs=(here,) * 2,
        scratch_shapes=wave_scratch()[-2:],
        compiler_params=params(16),
        cost_estimate=pl.CostEstimate(
            flops=100000000, bytes_accessed=20000000, transcendentals=0
        ),
        name="begin_wave_step",
    )(trig, *operands)


KEPT = 20


def first_kernel(
    trig_ref,
    upper_ref,
    lower_ref,
    above_ref,
    below_ref,
    part_lower_ref,
    part_upper_ref,
    arrived_ref,
    wind_ref,
    spec_lower_ref,
    spec_upper_ref,
    near_above_ref,
    near_below_ref,
    next_lower_ref,
    next_upper_ref,
    above_out_ref,
    below_out_ref,
    fields_ref,
    spec_ref,
    *scratch,
):
    moved_ref, damp_ref, sums_ref, turn_ref, speed_ref = scratch
    u, v, depth, wet = strip_fields(arrived_ref)
    u_own, u_near = u(0, 1), u(-1, 2)
    own = by_row(turn_ref, 0, u_own)
    near = by_row(turn_ref, 1, u_near)
    half = 0.5 * LAM_W
    face_low = half * (near[0] + own[0])
    face_own = half * (own[0] + own[1])
    face_high = half * (own[1] + near[1])
    wind = wind_ref[...].astype(F32)
    set_speeds(speed_ref)
    v_own, wet_own = v(0, 1), wet(0, 1)
    cells = pass_cells(turn_ref, v_own, wet_own)

    above_out_ref[...] = above_ref[0:HALF_ROWS, :]
    below_out_ref[...] = below_ref[0:HALF_ROWS, :]
    far = by_row(turn_ref, 2, u(-2, 3))
    wet_near = wet(-1, 2)
    for row, ref in ((0, above_ref), (1, below_ref)):
        arrived_wind = ref[HALF_ROWS:, :].astype(F32)[0:8]
        turn_ref[pl.ds(48 + row, 8, stride=2), :] = arrived_wind
    kept = [half * (far[0] + near[0]), half * (near[1] + far[1]), face_low, face_high]
    kept += [u_near, v(-1, 2), depth(-1, 2), wet_near, turn_ref[48:56], turn_ref[56:64]]
    kept += [u_own, v_own, depth(0, 1), wet_own, wind[0:8], wind[8:16]]
    kept += [0.5 * row for field in (wet_near, wet_own) for row in by_row(turn_ref, 0, field)]
    for index, field in enumerate(kept):
        fields_ref[index] = field

    def rows_first(d, quad):
        refs = (above_ref, lower_ref, upper_ref, below_ref, part_lower_ref, part_upper_ref)
        return [(*rows[:4], rows[4:]) for rows in packed_rows(refs, d, quad)]

    emit = summing(moved_ref, sums_ref)
    faces = (face_low, face_high)
    half_own = cells[-1]
    each_direction(
        lambda d: finish_direction(d, trig_ref, rows_first, faces, half_own, speed_ref, emit)
    )

    def emit_spec(d, quad, results):
        start = base_row(d) + 32 * quad
        spec_ref[pl.ds(start, 32), :] = jnp.concatenate(results, axis=0)
        for row, ref in ((0, spec_lower_ref), (1, spec_upper_ref)):
            halves = [pair_row(spec_ref, start + 16 * pair, row) for pair in range(2)]
            packed = jnp.concatenate(halves, axis=0).astype(BF16)
            ref[pl.ds(half_row(d) + 16 * quad, 16), :] = packed

    source_pass(
        trig_ref,
        u_own,
        v_own,
        depth(0, 1),
        wet_own,
        (wind[0:8], wind[8:16]),
        (moved_ref, damp_ref, sums_ref, turn_ref),
        emit_spec,
    )

    def rows_second(d, quad):
        return inner_rows((spec_lower_ref, spec_upper_ref), d, quad)

    emit_next = packing((next_lower_ref, next_upper_ref))
    each_direction(
        lambda d: propagate_direction(
            d, trig_ref, rows_second, (face_own,), cells, speed_ref, emit_next
        )
    )

    cells_near = pass_cells(turn_ref, v(-1, 2), wet(-1, 2))

    def rows_near(d, quad):
        return [
            (
                [(above, lower), (upper, below)],
                [(above, sublane_up(above), None, 0), (below, sublane_up(below), 1, None)],
            )
            for above, lower, upper, below in packed_rows(
                (above_ref, lower_ref, upper_ref, below_ref), d, quad
            )
        ]

    emit_near = packing((near_above_ref, near_below_ref))
    each_direction(
        lambda d: propagate_direction(
            d, trig_ref, rows_near, (face_low, face_high), cells_near, speed_ref, emit_near
        )
    )


def second_kernel(
    trig_ref,
    far_above_ref,
    far_below_ref,
    spec_lower_ref,
    spec_upper_ref,
    near_above_ref,
    near_below_ref,
    next_lower_ref,
    next_upper_ref,
    above_ref,
    below_ref,
    fields_ref,
    out_hbm,
    stress_ref,
    near_ref,
    out_ref,
    sem,
    *scratch,
):
    moved_ref, damp_ref, sums_ref, turn_ref, speed_ref = scratch
    shared = (moved_ref, damp_ref, sums_ref, turn_ref)
    kept = [fields_ref[index] for index in range(KEPT)]
    faces_near, faces_own = kept[0:2], kept[2:4]
    half_near, half_own = kept[16:18], kept[18:20]
    set_speeds(speed_ref)

    def rows_near(d, quad):
        refs = (far_above_ref, above_ref, below_ref, far_below_ref, near_above_ref, near_below_ref)
        return [(*rows[:4], rows[4:]) for rows in packed_rows(refs, d, quad)]

    emit = summing(moved_ref, sums_ref)
    each_direction(
        lambda d: finish_direction(d, trig_ref, rows_near, faces_near, half_near, speed_ref, emit)
    )

    def emit_near(d, quad, results):
        near_ref[pl.ds(base_row(d) + 32 * quad, 32), :] = jnp.concatenate(results, axis=0)

    source_pass(trig_ref, *kept[4:8], kept[8:10], shared, emit_near)

    def rows_own(d, quad):
        refs = (spec_lower_ref, spec_upper_ref, next_lower_ref, next_upper_ref)
        parts = []
        for part, rows in enumerate(packed_rows(refs, d, quad)):
            start = base_row(d) + 32 * quad + 16 * part
            below, above = [pair_row(near_ref, start, row) for row in range(2)]
            parts.append((below, rows[0], rows[1], above, rows[2:]))
        return parts

    emit = summing(moved_ref, sums_ref)
    each_direction(
        lambda d: finish_direction(d, trig_ref, rows_own, faces_own, half_own, speed_ref, emit)
    )
    outgoing = chunk_copies(out_ref, out_hbm, sem)
    zeros = jnp.zeros((8, 128), F32)

    def emit_own(d, quad, results):
        packed = jnp.concatenate(results, axis=0).astype(BF16)
        out_ref[d, 32 * quad : 32 * quad + 32, :] = packed
        scales = [float(math.pi / ND * SIGMA[4 * quad + part] / NF) for part in range(4)]
        return sum(result * scale for result, scale in zip(results, scales))

    def add_stress(d, totals, parts):
        @pl.when(lax.rem(d, CHUNK) == CHUNK - 1)
        def _():
            outgoing(lax.div(d, CHUNK)).start()

        total = sum(parts)
        cos_d, sin_d = trig_ref[0, d], trig_ref[1, d]
        xx, xy, yy = totals
        return (
            xx + total * (cos_d * cos_d),
            xy + total * (cos_d * sin_d),
            yy + total * (sin_d * sin_d),
        )

    totals = source_pass(
        trig_ref,
        *kept[10:14],
        kept[14:16],
        shared,
        emit_own,
        (zeros, zeros, zeros),
        add_stress,
    )
    for c in range(3):
        for tile in range(8):
            part = tile // 2
            stress_ref[tile, 2 * c : 2 * c + 2, :] = totals[c][2 * part : 2 * part + 2]
    for index in range(ND // CHUNK):
        outgoing(index).wait()


def first_step(trig, *operands):
    here = pl.BlockSpec(memory_space=VMEM)
    return pl.pallas_call(
        first_kernel,
        out_shape=(jax.ShapeDtypeStruct((HALF_ROWS, 128), BF16),) * 8
        + (jax.ShapeDtypeStruct((KEPT, 8, 128), F32),),
        in_specs=[pl.BlockSpec(memory_space=SMEM)] + [here] * len(operands),
        out_specs=(here,) * 9,
        scratch_shapes=[VMEM((CELL_ROWS, 128), F32)] + wave_scratch(),
        compiler_params=params(32),
        cost_estimate=pl.CostEstimate(
            flops=100000000, bytes_accessed=60000000, transcendentals=0
        ),
        name="first_wave_step",
    )(trig, *operands)


def second_step(trig, *operands):
    here = pl.BlockSpec(memory_space=VMEM)
    full = jax.ShapeDtypeStruct((ND, NF * 8, 128), BF16)
    return pl.pallas_call(
        second_kernel,
        out_shape=(full, jax.ShapeDtypeStruct((8, 6, 128), F32)),
        in_specs=[pl.BlockSpec(memory_space=SMEM)] + [here] * len(operands),
        out_specs=(pl.BlockSpec(memory_space=pl.ANY), here),
        scratch_shapes=[
            VMEM((CELL_ROWS, 128), F32),
            VMEM(full.shape, BF16),
            pltpu.SemaphoreType.DMA((ND // CHUNK,)),
        ]
        + wave_scratch(),
        compiler_params=params(36),
        cost_estimate=pl.CostEstimate(
            flops=200000000, bytes_accessed=40000000, transcendentals=0
        ),
        name="second_wave_step",
    )(trig, *operands)


def ocean_kernel(place_ref, vel_ref, own_ref, low_ref, high_ref, arrived_ref, out_ref, level_ref):
    row = lax.broadcasted_iota(jnp.int32, (32, 128), 0)
    lane = lax.broadcasted_iota(jnp.int32, (32, 128), 1)
    first_row, last_row = row == 0, row == 31
    first_lane, last_lane = lane == 0, lane == 127
    levels = vel_ref.shape[1]
    place = place_ref[0]
    before = arrived_ref[jnp.maximum(place - 1, 0), COLUMNS_AT:, :]
    before = jnp.where(place > 0, before, 0.0)
    after = arrived_ref[jnp.minimum(place + 1, 7), COLUMNS_AT:, :]
    after = jnp.where(place < 7, after, 0.0)

    def down(x, edge):
        return jnp.where(first_row, edge, pltpu.roll(x, 1, 0))

    def up(x, edge):
        return jnp.where(last_row, edge, pltpu.roll(x, 31, 0))

    def left(x, index):
        return jnp.where(first_lane, before[:, index : index + 1], pltpu.roll(x, 1, 1))

    def right(x, index):
        return jnp.where(last_lane, after[:, index : index + 1], pltpu.roll(x, 127, 1))

    def edge_rows(index):
        return low_ref[index, 7:8, :], high_ref[index, 0:1, :]

    level, bathy, wet, sxx, sxy, syy = [own_ref[i] for i in range(6)]
    ubar, vbar = own_ref[10], own_ref[11]
    edges = [edge_rows(i) for i in range(FIELDS)]
    plane_count = 2 * levels
    depth = bathy + level
    flux_x = depth * ubar
    flux_low = (edges[0][0] + edges[1][0]) * edges[10][0]
    flux_high = (edges[0][1] + edges[1][1]) * edges[10][1]
    flux_y = depth * vbar
    divergence = (
        up(flux_x, flux_high)
        - down(flux_x, flux_low)
        + right(flux_y, plane_count + 3)
        - left(flux_y, plane_count + 3)
    )
    level_ref[...] = level - 0.5 * LAM_O * wet * divergence
    inverse = 1.0 / depth
    grad_x = 0.5 * (up(level, edges[0][1]) - down(level, edges[0][0]))
    grad_y = 0.5 * (right(level, plane_count) - left(level, plane_count))
    xx_x = up(sxx, edges[3][1]) - down(sxx, edges[3][0])
    xy_x = up(sxy, edges[4][1]) - down(sxy, edges[4][0])
    xy_y = right(sxy, plane_count + 1) - left(sxy, plane_count + 1)
    yy_y = right(syy, plane_count + 2) - left(syy, plane_count + 2)
    base = (
        -LAM_O * grad_x - 0.5 * LAM_O * (xx_x + xy_y) * inverse,
        -LAM_O * grad_y - 0.5 * LAM_O * (xy_x + yy_y) * inverse,
    )
    turn = (F_CORIOLIS, -F_CORIOLIS)
    for k in range(levels):
        for c in range(2):
            plane = c * levels + k
            here = vel_ref[c, k]
            other = vel_ref[1 - c, k]
            above = vel_ref[c, max(k - 1, 0)]
            below = vel_ref[c, min(k + 1, levels - 1)]
            block, place = FIELDS + plane // 8, plane % 8
            low = low_ref[block, place : place + 1, :]
            high = high_ref[block, place : place + 1, :]
            around = up(here, high) + down(here, low) + right(here, plane) + left(here, plane)
            tendency = (
                base[c]
                + turn[c] * other
                + NU_H * (around - 4.0 * here)
                + KAPPA_V * (above + below - 2.0 * here)
            )
            out_ref[c, k] = wet * (here + tendency)


def ocean_step(place, vel, *operands):
    return pl.pallas_call(
        ocean_kernel,
        out_shape=(
            jax.ShapeDtypeStruct(vel.shape, F32),
            jax.ShapeDtypeStruct((32, 128), F32),
        ),
        in_specs=[pl.BlockSpec(memory_space=SMEM)] + [pl.BlockSpec(memory_space=VMEM)] * 5,
        out_specs=(pl.BlockSpec(memory_space=VMEM),) * 2,
        compiler_params=params(16),
        cost_estimate=pl.CostEstimate(flops=10000000, bytes_accessed=3000000, transcendentals=0),
        name="ocean_step",
    )(place, vel, *operands)


def shifted(array, axis_name, up):
    count = lax.axis_size(axis_name)
    pairs = [(i, i + 1) for i in range(count - 1)]
    if not up:
        pairs = [(target, source) for source, target in pairs]
    return lax.ppermute(array, axis_name, pairs)


def after(value, *others):
    return lax.optimization_barrier((value,) + others)[0]


def per_device(ocean_level, ocean_velocity, bathymetry, sea_mask, stress_in, spectra, wind_field):
    both = ("wide", "deep")
    spec = spectra.reshape(ND, NF, 2, 4, 128).transpose(0, 1, 3, 2, 4).reshape(ND, NF * 8, 128)
    wind = wind_field.reshape(2, 2, 4, 128).transpose(0, 2, 1, 3).reshape(16, 128)
    trig = jnp.asarray(TRIG)

    own, low_edge, high_edge, first, last = gather_surface(
        ocean_level, ocean_velocity, bathymetry, sea_mask, stress_in
    )
    from_low = shifted(high_edge, "wide", True)
    from_high = shifted(low_edge, "wide", False)
    upper, lower = split_rows(after(spec, own), wind)
    place = lax.axis_index("deep").astype(jnp.int32).reshape(1)
    outgoing = surface_step(place, after(own, upper), from_low, from_high, first, last)
    arrived = lax.all_to_all(outgoing, "deep", split_axis=0, concat_axis=0, tiled=True)

    above = shifted(after(upper, from_low, from_high), both, True)
    below = shifted(after(lower, from_low, from_high), both, False)
    far_above = shifted(after(lower, arrived), both, True)
    far_below = shifted(after(upper, arrived), both, False)
    velocity_out, level_out = ocean_step(
        place, ocean_velocity, own, from_low, from_high, arrived
    )
    begun = begin_step(trig, upper, lower, arrived)
    partial = first_step(
        trig, upper, lower, above, below, *begun, after(arrived, level_out), wind
    )
    spec, stress = second_step(trig, far_above, far_below, *partial)
    stress = lax.all_to_all(stress, "deep", split_axis=0, concat_axis=0, tiled=True)
    stress = stress.reshape(8, 3, 2, 128).transpose(1, 0, 2, 3).reshape(3, 16, 128)
    stress_out = jnp.where((place[0] & 1) == 1, stress[:, :, 64:], stress[:, :, :64])
    spectra_out = (
        spec.reshape(ND, NF, 4, 2, 128).transpose(0, 1, 3, 2, 4).reshape(ND, NF, 2, 512)
    )
    return (level_out, velocity_out, spectra_out, stress_out)


def solution(mesh):
    in_specs = (
        P("wide", "deep"),
        P(None, None, "wide", "deep"),
        P("wide", "deep"),
        P("wide", "deep"),
        P(None, "wide", "deep"),
        P(None, None, ("wide", "deep"), None),
        P(None, ("wide", "deep"), None),
    )
    out_specs = (
        P("wide", "deep"),
        P(None, None, "wide", "deep"),
        P(None, None, ("wide", "deep"), None),
        P(None, "wide", "deep"),
    )
    return jax.shard_map(
        per_device, mesh=mesh, in_specs=in_specs, out_specs=out_specs, check_vma=False
    )
```

```python
import math

import numpy as np

import jax
import jax.numpy as jnp
from jax import lax
from jax.experimental import pallas as pl
from jax.experimental.pallas import tpu as pltpu
from jax.sharding import PartitionSpec as P

LAM_O = 0.2
F_CORIOLIS = 0.1
NU_H = 0.05
KAPPA_V = 0.2
LAM_W = 0.25
GAMMA_BR = 0.73
A_IN = 0.15
C_NL = 0.5
C_WC = 0.002

ND = 36
NF = 36
SIGMA = 0.4 * np.power(1.07, np.arange(NF))
ANGLE = 2.0 * math.pi * np.arange(ND) / ND
TRIG = np.stack([np.cos(ANGLE), np.sin(ANGLE)]).astype(np.float32)

F32 = jnp.float32
BF16 = jnp.bfloat16
VMEM = pltpu.VMEM
SMEM = pltpu.SMEM
HIGH = lax.Precision.HIGHEST


def params(mib):
    return pltpu.CompilerParams(vmem_limit_bytes=mib * 1024 * 1024)


BINS = ND * NF
CELL_ROWS = BINS * 8
PAD = 16
CHUNK = 6


def iotas():
    sub = lax.broadcasted_iota(jnp.int32, (8, 128), 0)
    lane = lax.broadcasted_iota(jnp.int32, (8, 128), 1)
    return sub, lane


def sublane_up(x):
    return pltpu.roll(x, 7, 0)


def sublane_down(x):
    return pltpu.roll(x, 1, 0)


def base_row(d):
    return pl.multiple_of(d * (NF * 8), 8)


def pair_row(ref, start, row):
    return ref[pl.ds(start + row, 8, stride=2), :]


def half_row(d):
    return pl.multiple_of(d * (NF * 4), 16)


HALF_ROWS = BINS * 4


def chunk_copies(source, target, sem):
    def copy(index):
        part = pl.ds(index * CHUNK, CHUNK)
        return pltpu.make_async_copy(source.at[part], target.at[part], sem.at[index])

    return copy


def split_rows_kernel(spec_hbm, wind_ref, upper_ref, lower_ref, held_ref, spec_ref, turn_ref, sem):
    incoming = chunk_copies(spec_hbm, held_ref, sem)
    for index in range(ND // CHUNK):
        incoming(index).start()
    turn_ref[0:16, :] = wind_ref[...].astype(F32)
    sides = ((0, lower_ref), (1, upper_ref))
    for row, ref in sides:
        wind = jnp.concatenate([pair_row(turn_ref, 0, row), jnp.zeros((8, 128), F32)], axis=0)
        ref[HALF_ROWS:, :] = wind.astype(BF16)

    def body(d, carry):
        @pl.when(lax.rem(d, CHUNK) == 0)
        def _():
            incoming(lax.div(d, CHUNK)).wait()

        base = base_row(d)
        for quad in range(NF // 4):
            block = held_ref[d, 32 * quad : 32 * quad + 32, :].astype(F32)
            spec_ref[pl.ds(base + 32 * quad, 32), :] = block
        for quad in range(NF // 4):
            start = base + 32 * quad
            for row, ref in sides:
                halves = [pair_row(spec_ref, start + 16 * pair, row) for pair in range(2)]
                packed = jnp.concatenate(halves, axis=0).astype(BF16)
                ref[pl.ds(half_row(d) + 16 * quad, 16), :] = packed
        return carry

    lax.fori_loop(0, ND, body, 0)


def split_rows(spec, wind):
    half = jax.ShapeDtypeStruct((HALF_ROWS + 16, 128), BF16)
    return pl.pallas_call(
        split_rows_kernel,
        out_shape=(half, half),
        in_specs=[pl.BlockSpec(memory_space=pltpu.HBM), pl.BlockSpec(memory_space=VMEM)],
        out_specs=(pl.BlockSpec(memory_space=VMEM),) * 2,
        scratch_shapes=[
            VMEM(spec.shape, BF16),
            VMEM((CELL_ROWS + PAD, 128), F32),
            VMEM((16 + PAD, 128), F32),
            pltpu.SemaphoreType.DMA((ND // CHUNK,)),
        ],
        compiler_params=params(56),
        cost_estimate=pl.CostEstimate(flops=4000000, bytes_accessed=9000000, transcendentals=0),
        name="split_rows",
    )(spec, wind)


FIELDS = 12


def edge_columns(planes):
    lane = lax.broadcasted_iota(jnp.int32, (32, 128), 1)
    first = jnp.zeros((32, 128), F32)
    last = jnp.zeros((32, 128), F32)
    for index, plane in enumerate(planes):
        here = lane == index
        first = jnp.where(here, pltpu.roll(plane, index, 1), first)
        last = jnp.where(here, pltpu.roll(plane, (index + 1) % 128, 1), last)
    return first, last


def gather_kernel(
    level_ref,
    vel_ref,
    bathy_ref,
    mask_ref,
    stress_ref,
    own_ref,
    low_ref,
    high_ref,
    first_ref,
    last_ref,
):
    levels = vel_ref.shape[1]
    fields = [
        level_ref[...],
        bathy_ref[...],
        mask_ref[...].astype(F32),
        stress_ref[0],
        stress_ref[1],
        stress_ref[2],
        vel_ref[0, 0],
        vel_ref[1, 0],
        vel_ref[0, 1],
        vel_ref[1, 1],
    ]
    for c in range(2):
        total = vel_ref[c, 0]
        for k in range(1, levels):
            total = total + vel_ref[c, k]
        fields.append(total * (1.0 / levels))
    for index, field in enumerate(fields):
        own_ref[index] = field
        low_ref[index] = field[0:8]
        high_ref[index] = field[24:32]
    blocks = levels // 8
    for c in range(2):
        part = slice(FIELDS + blocks * c, FIELDS + blocks * c + blocks)
        low_ref[part] = vel_ref[c, :, 0, :].reshape(blocks, 8, 128)
        high_ref[part] = vel_ref[c, :, 31, :].reshape(blocks, 8, 128)
    planes = [vel_ref[c, k] for c in range(2) for k in range(levels)]
    planes += [fields[0], fields[4], fields[5], (fields[0] + fields[1]) * fields[11]]
    first_ref[...], last_ref[...] = edge_columns(planes)


def gather_surface(level, vel, bathy, mask, stress):
    rows, cols = level.shape
    edge = jax.ShapeDtypeStruct((FIELDS + vel.shape[1] // 4, 8, cols), F32)
    column = jax.ShapeDtypeStruct((rows, cols), F32)
    return pl.pallas_call(
        gather_kernel,
        out_shape=(jax.ShapeDtypeStruct((FIELDS, rows, cols), F32), edge, edge, column, column),
        in_specs=[pl.BlockSpec(memory_space=VMEM)] * 5,
        out_specs=(pl.BlockSpec(memory_space=VMEM),) * 5,
        compiler_params=params(56),
        cost_estimate=pl.CostEstimate(flops=400000, bytes_accessed=1700000, transcendentals=0),
        name="gather_surface",
    )(level, vel, bathy, mask, stress)


EXT = 48
ROWS_SENT = 6
EDGE_AT = 4 * ROWS_SENT
COLUMNS_AT = 40
SENT_ROWS = COLUMNS_AT + 32


def surface_kernel(place_ref, own_ref, low_ref, high_ref, first_ref, last_ref, out_ref):
    lane = lax.broadcasted_iota(jnp.int32, (EXT, 128), 1)

    def field(index):
        return jnp.concatenate([low_ref[index], own_ref[index], high_ref[index]], axis=0)

    level, bathy, wet, sxx, sxy, syy, u, v, u1, v1, ubar, vbar = [field(i) for i in range(FIELDS)]

    def down(x):
        return pltpu.roll(x, 1, 0)

    def up(x):
        return pltpu.roll(x, EXT - 1, 0)

    def left(x):
        return jnp.where(lane == 0, 0.0, pltpu.roll(x, 1, 1))

    def right(x):
        return jnp.where(lane == 127, 0.0, pltpu.roll(x, 127, 1))

    depth = bathy + level
    inverse = 1.0 / jnp.where(depth > 0.0, depth, 1.0)
    flux_x = depth * ubar
    flux_y = depth * vbar
    divergence = up(flux_x) - down(flux_x) + right(flux_y) - left(flux_y)
    new_depth = bathy + (level - 0.5 * LAM_O * wet * divergence)
    grad_x = 0.5 * (up(level) - down(level))
    grad_y = 0.5 * (right(level) - left(level))
    force_x = -0.5 * (up(sxx) - down(sxx) + (right(sxy) - left(sxy))) * inverse
    force_y = -0.5 * (up(sxy) - down(sxy) + (right(syy) - left(syy))) * inverse
    laplace_u = up(u) + down(u) + right(u) + left(u) - 4.0 * u
    laplace_v = up(v) + down(v) + right(v) + left(v) - 4.0 * v
    new_u = wet * (
        u
        - LAM_O * grad_x
        + F_CORIOLIS * v
        + LAM_O * force_x
        + NU_H * laplace_u
        + KAPPA_V * (u1 - u)
    )
    new_v = wet * (
        v
        - LAM_O * grad_y
        - F_CORIOLIS * u
        + LAM_O * force_y
        + NU_H * laplace_v
        + KAPPA_V * (v1 - v)
    )

    column = lax.broadcasted_iota(jnp.int32, (128, 128), 0)
    target = lax.broadcasted_iota(jnp.int32, (128, 128), 1)
    to_coarse = jnp.where(target == 64 * (place_ref[0] & 1) + (column >> 1), 0.25, 0.0)
    coarse_row = lax.broadcasted_iota(jnp.int32, (24, EXT), 0)
    fine_row = lax.broadcasted_iota(jnp.int32, (24, EXT), 1)
    pair_sum = jnp.where((fine_row >> 1) == coarse_row, 1.0, 0.0)
    stacked = jnp.concatenate([new_u, new_v, new_depth, wet], axis=0)
    narrowed = jnp.dot(stacked, to_coarse, precision=HIGH, preferred_element_type=F32)
    for index in range(4):
        coarse = jnp.dot(
            pair_sum,
            narrowed[EXT * index : EXT * index + EXT],
            precision=HIGH,
            preferred_element_type=F32,
        )
        for strip in range(8):
            first = 2 * strip + 2
            rows = slice(ROWS_SENT * index, ROWS_SENT * index + ROWS_SENT)
            out_ref[strip, rows, :] = coarse[first : first + ROWS_SENT]

    wet_inverse = wet * inverse
    to_right = [u, v, sxy, syy, level, flux_y]
    to_left = [u, v, -sxy, -syy, -level, -flux_y]
    weights = [
        NU_H * wet,
        NU_H * wet,
        0.5 * LAM_O * wet_inverse,
        0.5 * LAM_O * wet_inverse,
        0.5 * LAM_O * wet,
        0.5 * LAM_O * wet,
    ]
    edges = jnp.zeros((EXT, 128), F32)
    for index in range(6):
        edges = jnp.where(lane == index, to_right[index][:, 127:128], edges)
        edges = jnp.where(lane == 8 + index, to_left[index][:, 0:1], edges)
        edges = jnp.where(lane == 16 + index, weights[index][:, 0:1], edges)
        edges = jnp.where(lane == 24 + index, weights[index][:, 127:128], edges)
    for strip in range(8):
        first = 4 * strip + 4
        rows = 2 * ROWS_SENT
        out_ref[strip, EDGE_AT : EDGE_AT + rows, :] = edges[first : first + rows]
        blank = jnp.zeros((COLUMNS_AT - EDGE_AT - rows, 128), F32)
        out_ref[strip, EDGE_AT + rows : COLUMNS_AT, :] = blank
        columns = jnp.where(place_ref[0] == strip - 1, last_ref[...], 0.0)
        columns = jnp.where(place_ref[0] == strip + 1, first_ref[...], columns)
        out_ref[strip, COLUMNS_AT:, :] = columns


def surface_step(place, *operands):
    return pl.pallas_call(
        surface_kernel,
        out_shape=jax.ShapeDtypeStruct((8, SENT_ROWS, 128), F32),
        in_specs=[pl.BlockSpec(memory_space=SMEM)] + [pl.BlockSpec(memory_space=VMEM)] * 5,
        out_specs=pl.BlockSpec(memory_space=VMEM),
        compiler_params=params(16),
        cost_estimate=pl.CostEstimate(flops=2000000, bytes_accessed=400000, transcendentals=0),
        name="surface_step",
    )(place, *operands)


def rounded(x):
    return x.astype(BF16).astype(F32)


def strip_fields(arrived_ref):
    sub, lane = iotas()
    even = (sub & 1) == 0
    base = 64 * (sub & 1)
    edge_sums = []
    for row in range(ROWS_SENT):
        total = None
        for fine in (2 * row, 2 * row + 1):
            edge = arrived_ref[:, EDGE_AT + fine, :]
            from_left = jnp.where(sub == 0, 0.0, sublane_down(edge))
            from_right = jnp.where(sub == 7, 0.0, sublane_up(edge))
            weight = pltpu.roll(edge, 112, 1)
            product = weight * jnp.where(lane < 8, from_left, from_right)
            total = product if total is None else total + product
        edge_sums.append(0.25 * total)

    def tiles(index, row, parts):
        value = arrived_ref[:, ROWS_SENT * index + row + 2, :]
        if parts:
            edge = edge_sums[row + 2]
            left = sum(edge[:, p : p + 1] for p in parts)
            right = sum(edge[:, 8 + p : 9 + p] for p in parts)
            value = value + jnp.where(lane == base, left, 0.0)
            value = value + jnp.where(lane == base + 63, right, 0.0)
        return value

    def field(index, parts):
        def of_rows(first_row, second_row):
            first = tiles(index, first_row, parts)
            second = tiles(index, second_row, parts)
            return jnp.where(even, first + sublane_up(first), second + sublane_down(second))

        return of_rows

    sums = [field(0, (0, 2)), field(1, (1, 3, 4)), field(2, (5,)), field(3, ())]
    u, v, depth = [lambda a, b, get=get: rounded(get(a, b)) for get in sums[:3]]
    return u, v, depth, lambda a, b: jnp.where(sums[3](a, b) > 0.5, 1.0, 0.0)


def propagate_direction(d, trig_ref, rows_of, faces_x, cells, speed_ref, emit):
    first_lane, last_lane, inside, border, face_v, edge_v, half_wet = cells
    along_x = trig_ref[0, d]
    along_y = trig_ref[1, d] * inside
    along_border = trig_ref[1, d] * border
    for quad in range(NF // 4):
        results = []
        for part, (faces, rows) in enumerate(rows_of(d, quad)):
            speed = speed_ref[2 * quad + part]
            speed_x = along_x * speed
            speed_y = along_y * speed
            speed_border = along_border * speed
            flux_x = []
            for (lower, upper), face in zip(faces, faces_x):
                through = speed_x + face
                flux_x.append(through * jnp.where(through > 0.0, lower, upper))
            moved = []
            for row, (here, beyond, entry, exit) in enumerate(rows):
                through = speed_y + face_v[row]
                following = pltpu.roll(jnp.where(first_lane, beyond, here), 127, 1)
                flux = through * jnp.where(through > 0.0, here, following)
                before = pltpu.roll(jnp.where(last_lane, sublane_down(flux), flux), 1, 1)
                lost = jnp.minimum(speed_border + edge_v[row], 0.0) * here
                change = here + (before - flux) + lost
                if entry is not None:
                    change = change + flux_x[entry]
                if exit is not None:
                    change = change - flux_x[exit]
                moved.append(half_wet[row] * change)
            results.append(moved)
        emit(d, quad, results)


def finish_direction(d, trig_ref, rows_of, faces_x, half_wet, speed_ref, emit):
    along_x = trig_ref[0, d]
    for quad in range(NF // 4):
        results = []
        for part, (below, first, second, above, moved) in enumerate(rows_of(d, quad)):
            speed_x = along_x * speed_ref[2 * quad + part]
            through = speed_x + faces_x[0]
            flux_in = through * jnp.where(through > 0.0, below, first)
            through = speed_x + faces_x[1]
            flux_out = through * jnp.where(through > 0.0, second, above)
            results.append([moved[0] + half_wet[0] * flux_in, moved[1] - half_wet[1] * flux_out])
        emit(d, quad, results)


def source_direction(d, trig_ref, moved_ref, damp_ref, rel_x, rel_y, breaking, emit):
    base = base_row(d)
    plus = base_row(lax.rem(d + 2, ND))
    minus = base_row(lax.rem(d + ND - 2, ND))
    wind_along = A_IN * (rel_x * trig_ref[0, d] + rel_y * trig_ref[1, d])
    spreads = {}

    def spread(f):
        if f not in spreads:
            spreads[f] = moved_ref[pl.ds(plus + 8 * f, 8), :] + moved_ref[pl.ds(minus + 8 * f, 8), :]
        return spreads[f]

    for quad in range(NF // 4):
        results = []
        for part in range(4):
            f = 4 * quad + part
            here = moved_ref[pl.ds(base + 8 * f, 8), :]
            growth = jnp.minimum(jnp.maximum(wind_along * float(SIGMA[f]), A_IN), 3.0 * A_IN)
            summed = (growth + damp_ref[f] - here) * here
            if 0 < f < NF - 1:
                summed = summed + (0.5 * C_NL) * spread(f + 1) * spread(f - 1)
            results.append(summed * breaking)
        emit(quad, results)


def by_row(turn_ref, index, field):
    turn_ref[16 * index : 16 * index + 8] = field
    turn_ref[16 * index + 8 : 16 * index + 16] = field
    return [pair_row(turn_ref, 16 * index, row) for row in range(2)]


def pass_cells(turn_ref, v, wet):
    sub, lane = iotas()
    first_lane, last_lane = lane == 0, lane == 127
    block = sub & 3
    inside = jnp.where(last_lane & (block == 3), 0.0, 1.0)
    border = jnp.where(
        first_lane & (block == 0), 1.0, jnp.where(last_lane & (block == 3), -1.0, 0.0)
    )
    half = 0.5 * LAM_W
    face_v, edge_v = [], []
    for v_row in by_row(turn_ref, 0, v):
        after_v = pltpu.roll(jnp.where(first_lane, sublane_up(v_row), v_row), 127, 1)
        face_v.append(inside * (half * (v_row + after_v)))
        edge_v.append(border * (half * v_row))
    half_wet = [0.5 * wet_row for wet_row in by_row(turn_ref, 1, wet)]
    return first_lane, last_lane, inside, border, face_v, edge_v, half_wet


def set_speeds(speed_ref):
    sub, _ = iotas()
    for pair in range(NF // 2):
        low, high = [float(LAM_W * 0.5 / SIGMA[2 * pair + i]) for i in range(2)]
        speed_ref[pair] = jnp.where(sub < 4, low, high)


def each_direction(body):
    lax.fori_loop(0, ND, lambda d, carry: body(d) or carry, 0)


def summing(moved_ref, sums_ref):
    for f in range(NF):
        sums_ref[f] = jnp.zeros((8, 128), F32)

    def emit(d, quad, results):
        for part, moved in enumerate(results):
            pair = 2 * quad + part
            for row in range(2):
                moved_ref[pl.ds(base_row(d) + 16 * pair + row, 8, stride=2), :] = moved[row]
                sums_ref[2 * pair + row] += moved[row]

    return emit


def packing(refs):
    def emit(d, quad, results):
        for row, ref in enumerate(refs):
            block = jnp.concatenate([moved[row] for moved in results], axis=0)
            ref[pl.ds(half_row(d) + 16 * quad, 16), :] = block.astype(BF16)

    return emit


def source_pass(trig_ref, u, v, depth, wet, wind, scratch, emit, initial=0, combine=None):
    moved_ref, damp_ref, sums_ref, turn_ref = scratch
    sub, _ = iotas()
    zeros = jnp.zeros((8, 128), F32)
    for row in range(2):
        zeroth, second = zeros, zeros
        for pair in range(NF // 2):
            low, high = [float(SIGMA[2 * pair + i] ** 2) for i in range(2)]
            zeroth = zeroth + sums_ref[2 * pair + row]
            second = second + sums_ref[2 * pair + row] * jnp.where(sub < 4, low, high)
        for index, value in ((2, zeroth), (3, second)):
            turn_ref[pl.ds(16 * index + row, 8, stride=2), :] = value + pltpu.roll(value, 4, 0)
    moment_zero = turn_ref[32:40] * (2.0 / BINS)
    moment_two = turn_ref[48:56] * (2.0 / BINS)
    limit = (GAMMA_BR * depth) * (GAMMA_BR * depth)
    breaking = jnp.where(wet > 0.5, 2.0 * limit / jnp.maximum(16.0 * moment_zero, limit), 0.0)
    for f in range(NF):
        damp_ref[f] = (1.0 - A_IN) - float(C_WC * SIGMA[f] ** 3) * moment_two
    rel_x = wind[0] - u
    rel_y = wind[1] - v

    def source(d, carried):
        parts = []
        source_direction(
            d,
            trig_ref,
            moved_ref,
            damp_ref,
            rel_x,
            rel_y,
            breaking,
            lambda quad, results: parts.append(emit(d, quad, results)),
        )
        return combine(d, carried, parts) if combine else carried

    return lax.fori_loop(0, ND, source, initial)


def packed_rows(refs, d, quad):
    blocks = [ref[pl.ds(half_row(d) + 16 * quad, 16), :].astype(F32) for ref in refs]
    return [[block[8 * part : 8 * part + 8] for block in blocks] for part in range(2)]


def wave_scratch():
    return [
        VMEM((CELL_ROWS + PAD, 128), F32),
        VMEM((NF, 8, 128), F32),
        VMEM((NF, 8, 128), F32),
        VMEM((64 + PAD, 128), F32),
        VMEM((NF // 2, 8, 128), F32),
    ]


def inner_rows(refs, d, quad):
    return [
        (
            [(lower, upper)],
            [(lower, sublane_up(lower), None, 0), (upper, sublane_up(upper), 0, None)],
        )
        for lower, upper in packed_rows(refs, d, quad)
    ]


def begin_kernel(
    trig_ref, upper_ref, lower_ref, arrived_ref, part_lower_ref, part_upper_ref, turn_ref, speed_ref
):
    u, v, _, wet = strip_fields(arrived_ref)
    own = by_row(turn_ref, 0, u(0, 1))
    face_own = (0.5 * LAM_W) * (own[0] + own[1])
    set_speeds(speed_ref)
    cells = pass_cells(turn_ref, v(0, 1), wet(0, 1))

    def rows_own(d, quad):
        return inner_rows((lower_ref, upper_ref), d, quad)

    emit = packing((part_lower_ref, part_upper_ref))
    each_direction(
        lambda d: propagate_direction(d, trig_ref, rows_own, (face_own,), cells, speed_ref, emit)
    )


def begin_step(trig, *operands):
    here = pl.BlockSpec(memory_space=VMEM)
    return pl.pallas_call(
        begin_kernel,
        out_shape=(jax.ShapeDtypeStruct((HALF_ROWS, 128), BF16),) * 2,
        in_specs=[pl.BlockSpec(memory_space=SMEM)] + [here] * len(operands),
        out_specs=(here,) * 2,
        scratch_shapes=wave_scratch()[-2:],
        compiler_params=params(16),
        cost_estimate=pl.CostEstimate(
            flops=100000000, bytes_accessed=20000000, transcendentals=0
        ),
        name="begin_wave_step",
    )(trig, *operands)


KEPT = 20


def first_kernel(
    trig_ref,
    upper_ref,
    lower_ref,
    above_ref,
    below_ref,
    part_lower_ref,
    part_upper_ref,
    arrived_ref,
    wind_ref,
    spec_lower_ref,
    spec_upper_ref,
    near_above_ref,
    near_below_ref,
    next_lower_ref,
    next_upper_ref,
    above_out_ref,
    below_out_ref,
    fields_ref,
    spec_ref,
    *scratch,
):
    moved_ref, damp_ref, sums_ref, turn_ref, speed_ref = scratch
    u, v, depth, wet = strip_fields(arrived_ref)
    u_own, u_near = u(0, 1), u(-1, 2)
    own = by_row(turn_ref, 0, u_own)
    near = by_row(turn_ref, 1, u_near)
    half = 0.5 * LAM_W
    face_low = half * (near[0] + own[0])
    face_own = half * (own[0] + own[1])
    face_high = half * (own[1] + near[1])
    wind = wind_ref[...].astype(F32)
    set_speeds(speed_ref)
    v_own, wet_own = v(0, 1), wet(0, 1)
    cells = pass_cells(turn_ref, v_own, wet_own)

    above_out_ref[...] = above_ref[0:HALF_ROWS, :]
    below_out_ref[...] = below_ref[0:HALF_ROWS, :]
    far = by_row(turn_ref, 2, u(-2, 3))
    wet_near = wet(-1, 2)
    for row, ref in ((0, above_ref), (1, below_ref)):
        arrived_wind = ref[HALF_ROWS:, :].astype(F32)[0:8]
        turn_ref[pl.ds(48 + row, 8, stride=2), :] = arrived_wind
    kept = [half * (far[0] + near[0]), half * (near[1] + far[1]), face_low, face_high]
    kept += [u_near, v(-1, 2), depth(-1, 2), wet_near, turn_ref[48:56], turn_ref[56:64]]
    kept += [u_own, v_own, depth(0, 1), wet_own, wind[0:8], wind[8:16]]
    kept += [0.5 * row for field in (wet_near, wet_own) for row in by_row(turn_ref, 0, field)]
    for index, field in enumerate(kept):
        fields_ref[index] = field

    def rows_first(d, quad):
        refs = (above_ref, lower_ref, upper_ref, below_ref, part_lower_ref, part_upper_ref)
        return [(*rows[:4], rows[4:]) for rows in packed_rows(refs, d, quad)]

    emit = summing(moved_ref, sums_ref)
    faces = (face_low, face_high)
    half_own = cells[-1]
    each_direction(
        lambda d: finish_direction(d, trig_ref, rows_first, faces, half_own, speed_ref, emit)
    )

    def emit_spec(d, quad, results):
        start = base_row(d) + 32 * quad
        spec_ref[pl.ds(start, 32), :] = jnp.concatenate(results, axis=0)
        for row, ref in ((0, spec_lower_ref), (1, spec_upper_ref)):
            halves = [pair_row(spec_ref, start + 16 * pair, row) for pair in range(2)]
            packed = jnp.concatenate(halves, axis=0).astype(BF16)
            ref[pl.ds(half_row(d) + 16 * quad, 16), :] = packed

    source_pass(
        trig_ref,
        u_own,
        v_own,
        depth(0, 1),
        wet_own,
        (wind[0:8], wind[8:16]),
        (moved_ref, damp_ref, sums_ref, turn_ref),
        emit_spec,
    )

    def rows_second(d, quad):
        return inner_rows((spec_lower_ref, spec_upper_ref), d, quad)

    emit_next = packing((next_lower_ref, next_upper_ref))
    each_direction(
        lambda d: propagate_direction(
            d, trig_ref, rows_second, (face_own,), cells, speed_ref, emit_next
        )
    )

    cells_near = pass_cells(turn_ref, v(-1, 2), wet(-1, 2))

    def rows_near(d, quad):
        return [
            (
                [(above, lower), (upper, below)],
                [(above, sublane_up(above), None, 0), (below, sublane_up(below), 1, None)],
            )
            for above, lower, upper, below in packed_rows(
                (above_ref, lower_ref, upper_ref, below_ref), d, quad
            )
        ]

    emit_near = packing((near_above_ref, near_below_ref))
    each_direction(
        lambda d: propagate_direction(
            d, trig_ref, rows_near, (face_low, face_high), cells_near, speed_ref, emit_near
        )
    )


def second_kernel(
    trig_ref,
    far_above_ref,
    far_below_ref,
    spec_lower_ref,
    spec_upper_ref,
    near_above_ref,
    near_below_ref,
    next_lower_ref,
    next_upper_ref,
    above_ref,
    below_ref,
    fields_ref,
    out_hbm,
    stress_ref,
    near_ref,
    out_ref,
    sem,
    *scratch,
):
    moved_ref, damp_ref, sums_ref, turn_ref, speed_ref = scratch
    shared = (moved_ref, damp_ref, sums_ref, turn_ref)
    kept = [fields_ref[index] for index in range(KEPT)]
    faces_near, faces_own = kept[0:2], kept[2:4]
    half_near, half_own = kept[16:18], kept[18:20]
    set_speeds(speed_ref)

    def rows_near(d, quad):
        refs = (far_above_ref, above_ref, below_ref, far_below_ref, near_above_ref, near_below_ref)
        return [(*rows[:4], rows[4:]) for rows in packed_rows(refs, d, quad)]

    emit = summing(moved_ref, sums_ref)
    each_direction(
        lambda d: finish_direction(d, trig_ref, rows_near, faces_near, half_near, speed_ref, emit)
    )

    def emit_near(d, quad, results):
        near_ref[pl.ds(base_row(d) + 32 * quad, 32), :] = jnp.concatenate(results, axis=0)

    source_pass(trig_ref, *kept[4:8], kept[8:10], shared, emit_near)

    def rows_own(d, quad):
        refs = (spec_lower_ref, spec_upper_ref, next_lower_ref, next_upper_ref)
        parts = []
        for part, rows in enumerate(packed_rows(refs, d, quad)):
            start = base_row(d) + 32 * quad + 16 * part
            below, above = [pair_row(near_ref, start, row) for row in range(2)]
            parts.append((below, rows[0], rows[1], above, rows[2:]))
        return parts

    emit = summing(moved_ref, sums_ref)
    each_direction(
        lambda d: finish_direction(d, trig_ref, rows_own, faces_own, half_own, speed_ref, emit)
    )
    outgoing = chunk_copies(out_ref, out_hbm, sem)
    zeros = jnp.zeros((8, 128), F32)

    def emit_own(d, quad, results):
        packed = jnp.concatenate(results, axis=0).astype(BF16)
        out_ref[d, 32 * quad : 32 * quad + 32, :] = packed
        scales = [float(math.pi / ND * SIGMA[4 * quad + part] / NF) for part in range(4)]
        return sum(result * scale for result, scale in zip(results, scales))

    def add_stress(d, totals, parts):
        @pl.when(lax.rem(d, CHUNK) == CHUNK - 1)
        def _():
            outgoing(lax.div(d, CHUNK)).start()

        total = sum(parts)
        cos_d, sin_d = trig_ref[0, d], trig_ref[1, d]
        xx, xy, yy = totals
        return (
            xx + total * (cos_d * cos_d),
            xy + total * (cos_d * sin_d),
            yy + total * (sin_d * sin_d),
        )

    totals = source_pass(
        trig_ref,
        *kept[10:14],
        kept[14:16],
        shared,
        emit_own,
        (zeros, zeros, zeros),
        add_stress,
    )
    for c in range(3):
        for tile in range(8):
            part = tile // 2
            stress_ref[tile, 2 * c : 2 * c + 2, :] = totals[c][2 * part : 2 * part + 2]
    for index in range(ND // CHUNK):
        outgoing(index).wait()


def first_step(trig, *operands):
    here = pl.BlockSpec(memory_space=VMEM)
    return pl.pallas_call(
        first_kernel,
        out_shape=(jax.ShapeDtypeStruct((HALF_ROWS, 128), BF16),) * 8
        + (jax.ShapeDtypeStruct((KEPT, 8, 128), F32),),
        in_specs=[pl.BlockSpec(memory_space=SMEM)] + [here] * len(operands),
        out_specs=(here,) * 9,
        scratch_shapes=[VMEM((CELL_ROWS + PAD, 128), F32)] + wave_scratch(),
        compiler_params=params(32),
        cost_estimate=pl.CostEstimate(
            flops=100000000, bytes_accessed=60000000, transcendentals=0
        ),
        name="first_wave_step",
    )(trig, *operands)


def second_step(trig, *operands):
    here = pl.BlockSpec(memory_space=VMEM)
    full = jax.ShapeDtypeStruct((ND, NF * 8, 128), BF16)
    return pl.pallas_call(
        second_kernel,
        out_shape=(full, jax.ShapeDtypeStruct((8, 6, 128), F32)),
        in_specs=[pl.BlockSpec(memory_space=SMEM)] + [here] * len(operands),
        out_specs=(pl.BlockSpec(memory_space=pl.ANY), here),
        scratch_shapes=[
            VMEM((CELL_ROWS + PAD, 128), F32),
            VMEM(full.shape, BF16),
            pltpu.SemaphoreType.DMA((ND // CHUNK,)),
        ]
        + wave_scratch(),
        compiler_params=params(36),
        cost_estimate=pl.CostEstimate(
            flops=200000000, bytes_accessed=40000000, transcendentals=0
        ),
        name="second_wave_step",
    )(trig, *operands)


def ocean_kernel(place_ref, vel_ref, own_ref, low_ref, high_ref, arrived_ref, out_ref, level_ref):
    row = lax.broadcasted_iota(jnp.int32, (32, 128), 0)
    lane = lax.broadcasted_iota(jnp.int32, (32, 128), 1)
    first_row, last_row = row == 0, row == 31
    first_lane, last_lane = lane == 0, lane == 127
    levels = vel_ref.shape[1]
    place = place_ref[0]
    before = arrived_ref[jnp.maximum(place - 1, 0), COLUMNS_AT:, :]
    before = jnp.where(place > 0, before, 0.0)
    after = arrived_ref[jnp.minimum(place + 1, 7), COLUMNS_AT:, :]
    after = jnp.where(place < 7, after, 0.0)

    def down(x, edge):
        return jnp.where(first_row, edge, pltpu.roll(x, 1, 0))

    def up(x, edge):
        return jnp.where(last_row, edge, pltpu.roll(x, 31, 0))

    def left(x, index):
        return jnp.where(first_lane, before[:, index : index + 1], pltpu.roll(x, 1, 1))

    def right(x, index):
        return jnp.where(last_lane, after[:, index : index + 1], pltpu.roll(x, 127, 1))

    def edge_rows(index):
        return low_ref[index, 7:8, :], high_ref[index, 0:1, :]

    level, bathy, wet, sxx, sxy, syy = [own_ref[i] for i in range(6)]
    ubar, vbar = own_ref[10], own_ref[11]
    edges = [edge_rows(i) for i in range(FIELDS)]
    plane_count = 2 * levels
    depth = bathy + level
    flux_x = depth * ubar
    flux_low = (edges[0][0] + edges[1][0]) * edges[10][0]
    flux_high = (edges[0][1] + edges[1][1]) * edges[10][1]
    flux_y = depth * vbar
    divergence = (
        up(flux_x, flux_high)
        - down(flux_x, flux_low)
        + right(flux_y, plane_count + 3)
        - left(flux_y, plane_count + 3)
    )
    level_ref[...] = level - 0.5 * LAM_O * wet * divergence
    inverse = 1.0 / depth
    grad_x = 0.5 * (up(level, edges[0][1]) - down(level, edges[0][0]))
    grad_y = 0.5 * (right(level, plane_count) - left(level, plane_count))
    xx_x = up(sxx, edges[3][1]) - down(sxx, edges[3][0])
    xy_x = up(sxy, edges[4][1]) - down(sxy, edges[4][0])
    xy_y = right(sxy, plane_count + 1) - left(sxy, plane_count + 1)
    yy_y = right(syy, plane_count + 2) - left(syy, plane_count + 2)
    base = (
        -LAM_O * grad_x - 0.5 * LAM_O * (xx_x + xy_y) * inverse,
        -LAM_O * grad_y - 0.5 * LAM_O * (xy_x + yy_y) * inverse,
    )
    turn = (F_CORIOLIS, -F_CORIOLIS)
    for k in range(levels):
        for c in range(2):
            plane = c * levels + k
            here = vel_ref[c, k]
            other = vel_ref[1 - c, k]
            above = vel_ref[c, max(k - 1, 0)]
            below = vel_ref[c, min(k + 1, levels - 1)]
            block, place = FIELDS + plane // 8, plane % 8
            low = low_ref[block, place : place + 1, :]
            high = high_ref[block, place : place + 1, :]
            around = up(here, high) + down(here, low) + right(here, plane) + left(here, plane)
            tendency = (
                base[c]
                + turn[c] * other
                + NU_H * (around - 4.0 * here)
                + KAPPA_V * (above + below - 2.0 * here)
            )
            out_ref[c, k] = wet * (here + tendency)


def ocean_step(place, vel, *operands):
    return pl.pallas_call(
        ocean_kernel,
        out_shape=(
            jax.ShapeDtypeStruct(vel.shape, F32),
            jax.ShapeDtypeStruct((32, 128), F32),
        ),
        in_specs=[pl.BlockSpec(memory_space=SMEM)] + [pl.BlockSpec(memory_space=VMEM)] * 5,
        out_specs=(pl.BlockSpec(memory_space=VMEM),) * 2,
        compiler_params=params(16),
        cost_estimate=pl.CostEstimate(flops=10000000, bytes_accessed=3000000, transcendentals=0),
        name="ocean_step",
    )(place, vel, *operands)


def shifted(array, axis_name, up):
    count = lax.axis_size(axis_name)
    pairs = [(i, i + 1) for i in range(count - 1)]
    if not up:
        pairs = [(target, source) for source, target in pairs]
    return lax.ppermute(array, axis_name, pairs)


def after(value, *others):
    return lax.optimization_barrier((value,) + others)[0]


def per_device(ocean_level, ocean_velocity, bathymetry, sea_mask, stress_in, spectra, wind_field):
    both = ("wide", "deep")
    spec = spectra.reshape(ND, NF, 2, 4, 128).transpose(0, 1, 3, 2, 4).reshape(ND, NF * 8, 128)
    wind = wind_field.reshape(2, 2, 4, 128).transpose(0, 2, 1, 3).reshape(16, 128)
    trig = jnp.asarray(TRIG)

    own, low_edge, high_edge, first, last = gather_surface(
        ocean_level, ocean_velocity, bathymetry, sea_mask, stress_in
    )
    from_low = shifted(high_edge, "wide", True)
    from_high = shifted(low_edge, "wide", False)
    upper, lower = split_rows(after(spec, own), wind)
    place = lax.axis_index("deep").astype(jnp.int32).reshape(1)
    outgoing = surface_step(place, after(own, upper), from_low, from_high, first, last)
    arrived = lax.all_to_all(outgoing, "deep", split_axis=0, concat_axis=0, tiled=True)

    above = shifted(after(upper, from_low, from_high), both, True)
    below = shifted(after(lower, from_low, from_high), both, False)
    far_above = shifted(after(lower, arrived), both, True)
    far_below = shifted(after(upper, arrived), both, False)
    velocity_out, level_out = ocean_step(
        place, ocean_velocity, own, from_low, from_high, arrived
    )
    begun = begin_step(trig, upper, lower, arrived)
    partial = first_step(
        trig, upper, lower, above, below, *begun, after(arrived, level_out), wind
    )
    spec, stress = second_step(trig, far_above, far_below, *partial)
    stress = lax.all_to_all(stress, "deep", split_axis=0, concat_axis=0, tiled=True)
    stress = stress.reshape(8, 3, 2, 128).transpose(1, 0, 2, 3).reshape(3, 16, 128)
    stress_out = jnp.where((place[0] & 1) == 1, stress[:, :, 64:], stress[:, :, :64])
    spectra_out = (
        spec.reshape(ND, NF, 4, 2, 128).transpose(0, 1, 3, 2, 4).reshape(ND, NF, 2, 512)
    )
    return (level_out, velocity_out, spectra_out, stress_out)


def solution(mesh):
    in_specs = (
        P("wide", "deep"),
        P(None, None, "wide", "deep"),
        P("wide", "deep"),
        P("wide", "deep"),
        P(None, "wide", "deep"),
        P(None, None, ("wide", "deep"), None),
        P(None, ("wide", "deep"), None),
    )
    out_specs = (
        P("wide", "deep"),
        P(None, None, "wide", "deep"),
        P(None, None, ("wide", "deep"), None),
        P(None, "wide", "deep"),
    )
    return jax.shard_map(
        per_device, mesh=mesh, in_specs=in_specs, out_specs=out_specs, check_vma=False
    )
```

```python
import math

import numpy as np

import jax
import jax.numpy as jnp
from jax import lax
from jax.experimental import pallas as pl
from jax.experimental.pallas import tpu as pltpu
from jax.sharding import PartitionSpec as P

LAM_O = 0.2
F_CORIOLIS = 0.1
NU_H = 0.05
KAPPA_V = 0.2
LAM_W = 0.25
GAMMA_BR = 0.73
A_IN = 0.15
C_NL = 0.5
C_WC = 0.002

ND = 36
NF = 36
SIGMA = 0.4 * np.power(1.07, np.arange(NF))
ANGLE = 2.0 * math.pi * np.arange(ND) / ND
TRIG = np.stack([np.cos(ANGLE), np.sin(ANGLE)]).astype(np.float32)

F32 = jnp.float32
BF16 = jnp.bfloat16
VMEM = pltpu.VMEM
SMEM = pltpu.SMEM
HIGH = lax.Precision.HIGHEST


def params(mib):
    return pltpu.CompilerParams(vmem_limit_bytes=mib * 1024 * 1024)


BINS = ND * NF
CELL_ROWS = BINS * 8
PAD = 16
CHUNK = 6


def iotas():
    sub = lax.broadcasted_iota(jnp.int32, (8, 128), 0)
    lane = lax.broadcasted_iota(jnp.int32, (8, 128), 1)
    return sub, lane


def sublane_up(x):
    return pltpu.roll(x, 7, 0)


def sublane_down(x):
    return pltpu.roll(x, 1, 0)


def base_row(d):
    return pl.multiple_of(d * (NF * 8), 8)


def pair_row(ref, start, row):
    return ref[pl.ds(start + row, 8, stride=2), :]


def half_row(d):
    return pl.multiple_of(d * (NF * 4), 16)


HALF_ROWS = BINS * 4


def chunk_copies(source, target, sem):
    def copy(index):
        part = pl.ds(index * CHUNK, CHUNK)
        return pltpu.make_async_copy(source.at[part], target.at[part], sem.at[index])

    return copy


def split_rows_kernel(
    spec_hbm,
    wind_ref,
    upper_hbm,
    lower_hbm,
    held_ref,
    spec_ref,
    turn_ref,
    upper_ref,
    lower_ref,
    sem,
    out_sem,
):
    incoming = chunk_copies(spec_hbm, held_ref, sem)
    chunks = ND // CHUNK

    def outgoing(side, index):
        source, target = ((lower_ref, lower_hbm), (upper_ref, upper_hbm))[side]
        start = pl.multiple_of(index * (CHUNK * NF * 4), 16)
        part = pl.ds(start, CHUNK * NF * 4)
        return pltpu.make_async_copy(source.at[part], target.at[part], out_sem.at[side, index])

    def outgoing_wind(side):
        source, target = ((lower_ref, lower_hbm), (upper_ref, upper_hbm))[side]
        part = pl.ds(HALF_ROWS, 16)
        return pltpu.make_async_copy(source.at[part], target.at[part], out_sem.at[side, chunks])

    for index in range(ND // CHUNK):
        incoming(index).start()
    turn_ref[0:16, :] = wind_ref[...].astype(F32)
    sides = ((0, lower_ref), (1, upper_ref))
    for row, ref in sides:
        wind = jnp.concatenate([pair_row(turn_ref, 0, row), jnp.zeros((8, 128), F32)], axis=0)
        ref[HALF_ROWS:, :] = wind.astype(BF16)
        outgoing_wind(row).start()

    def body(d, carry):
        @pl.when(lax.rem(d, CHUNK) == 0)
        def _():
            incoming(lax.div(d, CHUNK)).wait()

        base = base_row(d)
        for quad in range(NF // 4):
            block = held_ref[d, 32 * quad : 32 * quad + 32, :].astype(F32)
            spec_ref[pl.ds(base + 32 * quad, 32), :] = block
        for quad in range(NF // 4):
            start = base + 32 * quad
            for row, ref in sides:
                halves = [pair_row(spec_ref, start + 16 * pair, row) for pair in range(2)]
                packed = jnp.concatenate(halves, axis=0).astype(BF16)
                ref[pl.ds(half_row(d) + 16 * quad, 16), :] = packed

        @pl.when(lax.rem(d, CHUNK) == CHUNK - 1)
        def _():
            for side in range(2):
                outgoing(side, lax.div(d, CHUNK)).start()

        return carry

    lax.fori_loop(0, ND, body, 0)
    for side in range(2):
        outgoing_wind(side).wait()
        for index in range(chunks):
            outgoing(side, index).wait()


def split_rows(spec, wind):
    half = jax.ShapeDtypeStruct((HALF_ROWS + 16, 128), BF16)
    return pl.pallas_call(
        split_rows_kernel,
        out_shape=(half, half),
        in_specs=[pl.BlockSpec(memory_space=pltpu.HBM), pl.BlockSpec(memory_space=VMEM)],
        out_specs=(pl.BlockSpec(memory_space=pl.ANY),) * 2,
        scratch_shapes=[
            VMEM(spec.shape, BF16),
            VMEM((CELL_ROWS + PAD, 128), F32),
            VMEM((16 + PAD, 128), F32),
            VMEM(half.shape, BF16),
            VMEM(half.shape, BF16),
            pltpu.SemaphoreType.DMA((ND // CHUNK,)),
            pltpu.SemaphoreType.DMA((2, ND // CHUNK + 1)),
        ],
        compiler_params=params(56),
        cost_estimate=pl.CostEstimate(flops=4000000, bytes_accessed=9000000, transcendentals=0),
        name="split_rows",
    )(spec, wind)


FIELDS = 12


def edge_columns(planes):
    lane = lax.broadcasted_iota(jnp.int32, (32, 128), 1)
    first = jnp.zeros((32, 128), F32)
    last = jnp.zeros((32, 128), F32)
    for index, plane in enumerate(planes):
        here = lane == index
        first = jnp.where(here, pltpu.roll(plane, index, 1), first)
        last = jnp.where(here, pltpu.roll(plane, (index + 1) % 128, 1), last)
    return first, last


def gather_kernel(
    level_ref,
    vel_ref,
    bathy_ref,
    mask_ref,
    stress_ref,
    own_hbm,
    low_hbm,
    high_hbm,
    first_ref,
    last_ref,
    own_ref,
    low_ref,
    high_ref,
    sem,
):
    levels = vel_ref.shape[1]
    fields = [
        level_ref[...],
        bathy_ref[...],
        mask_ref[...].astype(F32),
        stress_ref[0],
        stress_ref[1],
        stress_ref[2],
        vel_ref[0, 0],
        vel_ref[1, 0],
        vel_ref[0, 1],
        vel_ref[1, 1],
    ]
    for c in range(2):
        total = vel_ref[c, 0]
        for k in range(1, levels):
            total = total + vel_ref[c, k]
        fields.append(total * (1.0 / levels))
    for index, field in enumerate(fields):
        own_ref[index] = field
        low_ref[index] = field[0:8]
        high_ref[index] = field[24:32]
    blocks = levels // 8
    for c in range(2):
        part = slice(FIELDS + blocks * c, FIELDS + blocks * c + blocks)
        low_ref[part] = vel_ref[c, :, 0, :].reshape(blocks, 8, 128)
        high_ref[part] = vel_ref[c, :, 31, :].reshape(blocks, 8, 128)
    pairs = ((own_ref, own_hbm), (low_ref, low_hbm), (high_ref, high_hbm))
    copies = [pltpu.make_async_copy(*pair, sem.at[i]) for i, pair in enumerate(pairs)]
    for copy in copies:
        copy.start()
    planes = [vel_ref[c, k] for c in range(2) for k in range(levels)]
    planes += [fields[0], fields[4], fields[5], (fields[0] + fields[1]) * fields[11]]
    first_ref[...], last_ref[...] = edge_columns(planes)
    for copy in copies:
        copy.wait()


def gather_surface(level, vel, bathy, mask, stress):
    rows, cols = level.shape
    edge = jax.ShapeDtypeStruct((FIELDS + vel.shape[1] // 4, 8, cols), F32)
    column = jax.ShapeDtypeStruct((rows, cols), F32)
    return pl.pallas_call(
        gather_kernel,
        out_shape=(jax.ShapeDtypeStruct((FIELDS, rows, cols), F32), edge, edge, column, column),
        in_specs=[pl.BlockSpec(memory_space=VMEM)] * 5,
        out_specs=(pl.BlockSpec(memory_space=pl.ANY),) * 3
        + (pl.BlockSpec(memory_space=VMEM),) * 2,
        scratch_shapes=[
            VMEM((FIELDS, rows, cols), F32),
            VMEM(edge.shape, F32),
            VMEM(edge.shape, F32),
            pltpu.SemaphoreType.DMA((3,)),
        ],
        compiler_params=params(56),
        cost_estimate=pl.CostEstimate(flops=400000, bytes_accessed=1700000, transcendentals=0),
        name="gather_surface",
    )(level, vel, bathy, mask, stress)


EXT = 48
ROWS_SENT = 6
EDGE_AT = 4 * ROWS_SENT
COLUMNS_AT = 40
SENT_ROWS = COLUMNS_AT + 32


def surface_kernel(place_ref, own_ref, low_ref, high_ref, first_ref, last_ref, out_ref):
    lane = lax.broadcasted_iota(jnp.int32, (EXT, 128), 1)

    def field(index):
        return jnp.concatenate([low_ref[index], own_ref[index], high_ref[index]], axis=0)

    level, bathy, wet, sxx, sxy, syy, u, v, u1, v1, ubar, vbar = [field(i) for i in range(FIELDS)]

    def down(x):
        return pltpu.roll(x, 1, 0)

    def up(x):
        return pltpu.roll(x, EXT - 1, 0)

    def left(x):
        return jnp.where(lane == 0, 0.0, pltpu.roll(x, 1, 1))

    def right(x):
        return jnp.where(lane == 127, 0.0, pltpu.roll(x, 127, 1))

    depth = bathy + level
    inverse = 1.0 / jnp.where(depth > 0.0, depth, 1.0)
    flux_x = depth * ubar
    flux_y = depth * vbar
    divergence = up(flux_x) - down(flux_x) + right(flux_y) - left(flux_y)
    new_depth = bathy + (level - 0.5 * LAM_O * wet * divergence)
    grad_x = 0.5 * (up(level) - down(level))
    grad_y = 0.5 * (right(level) - left(level))
    force_x = -0.5 * (up(sxx) - down(sxx) + (right(sxy) - left(sxy))) * inverse
    force_y = -0.5 * (up(sxy) - down(sxy) + (right(syy) - left(syy))) * inverse
    laplace_u = up(u) + down(u) + right(u) + left(u) - 4.0 * u
    laplace_v = up(v) + down(v) + right(v) + left(v) - 4.0 * v
    new_u = wet * (
        u
        - LAM_O * grad_x
        + F_CORIOLIS * v
        + LAM_O * force_x
        + NU_H * laplace_u
        + KAPPA_V * (u1 - u)
    )
    new_v = wet * (
        v
        - LAM_O * grad_y
        - F_CORIOLIS * u
        + LAM_O * force_y
        + NU_H * laplace_v
        + KAPPA_V * (v1 - v)
    )

    column = lax.broadcasted_iota(jnp.int32, (128, 128), 0)
    target = lax.broadcasted_iota(jnp.int32, (128, 128), 1)
    to_coarse = jnp.where(target == 64 * (place_ref[0] & 1) + (column >> 1), 0.25, 0.0)
    coarse_row = lax.broadcasted_iota(jnp.int32, (24, EXT), 0)
    fine_row = lax.broadcasted_iota(jnp.int32, (24, EXT), 1)
    pair_sum = jnp.where((fine_row >> 1) == coarse_row, 1.0, 0.0)
    stacked = jnp.concatenate([new_u, new_v, new_depth, wet], axis=0)
    narrowed = jnp.dot(stacked, to_coarse, precision=HIGH, preferred_element_type=F32)
    for index in range(4):
        coarse = jnp.dot(
            pair_sum,
            narrowed[EXT * index : EXT * index + EXT],
            precision=HIGH,
            preferred_element_type=F32,
        )
        for strip in range(8):
            first = 2 * strip + 2
            rows = slice(ROWS_SENT * index, ROWS_SENT * index + ROWS_SENT)
            out_ref[strip, rows, :] = coarse[first : first + ROWS_SENT]

    wet_inverse = wet * inverse
    to_right = [u, v, sxy, syy, level, flux_y]
    to_left = [u, v, -sxy, -syy, -level, -flux_y]
    weights = [
        NU_H * wet,
        NU_H * wet,
        0.5 * LAM_O * wet_inverse,
        0.5 * LAM_O * wet_inverse,
        0.5 * LAM_O * wet,
        0.5 * LAM_O * wet,
    ]
    edges = jnp.zeros((EXT, 128), F32)
    for index in range(6):
        edges = jnp.where(lane == index, to_right[index][:, 127:128], edges)
        edges = jnp.where(lane == 8 + index, to_left[index][:, 0:1], edges)
        edges = jnp.where(lane == 16 + index, weights[index][:, 0:1], edges)
        edges = jnp.where(lane == 24 + index, weights[index][:, 127:128], edges)
    for strip in range(8):
        first = 4 * strip + 4
        rows = 2 * ROWS_SENT
        out_ref[strip, EDGE_AT : EDGE_AT + rows, :] = edges[first : first + rows]
        blank = jnp.zeros((COLUMNS_AT - EDGE_AT - rows, 128), F32)
        out_ref[strip, EDGE_AT + rows : COLUMNS_AT, :] = blank
        columns = jnp.where(place_ref[0] == strip - 1, last_ref[...], 0.0)
        columns = jnp.where(place_ref[0] == strip + 1, first_ref[...], columns)
        out_ref[strip, COLUMNS_AT:, :] = columns


def surface_step(place, *operands):
    return pl.pallas_call(
        surface_kernel,
        out_shape=jax.ShapeDtypeStruct((8, SENT_ROWS, 128), F32),
        in_specs=[pl.BlockSpec(memory_space=SMEM)] + [pl.BlockSpec(memory_space=VMEM)] * 5,
        out_specs=pl.BlockSpec(memory_space=VMEM),
        compiler_params=params(16),
        cost_estimate=pl.CostEstimate(flops=2000000, bytes_accessed=400000, transcendentals=0),
        name="surface_step",
    )(place, *operands)


def rounded(x):
    return x.astype(BF16).astype(F32)


def strip_fields(arrived_ref):
    sub, lane = iotas()
    even = (sub & 1) == 0
    base = 64 * (sub & 1)
    edge_sums = []
    for row in range(ROWS_SENT):
        total = None
        for fine in (2 * row, 2 * row + 1):
            edge = arrived_ref[:, EDGE_AT + fine, :]
            from_left = jnp.where(sub == 0, 0.0, sublane_down(edge))
            from_right = jnp.where(sub == 7, 0.0, sublane_up(edge))
            weight = pltpu.roll(edge, 112, 1)
            product = weight * jnp.where(lane < 8, from_left, from_right)
            total = product if total is None else total + product
        edge_sums.append(0.25 * total)

    def tiles(index, row, parts):
        value = arrived_ref[:, ROWS_SENT * index + row + 2, :]
        if parts:
            edge = edge_sums[row + 2]
            left = sum(edge[:, p : p + 1] for p in parts)
            right = sum(edge[:, 8 + p : 9 + p] for p in parts)
            value = value + jnp.where(lane == base, left, 0.0)
            value = value + jnp.where(lane == base + 63, right, 0.0)
        return value

    def field(index, parts):
        def of_rows(first_row, second_row):
            first = tiles(index, first_row, parts)
            second = tiles(index, second_row, parts)
            return jnp.where(even, first + sublane_up(first), second + sublane_down(second))

        return of_rows

    sums = [field(0, (0, 2)), field(1, (1, 3, 4)), field(2, (5,)), field(3, ())]
    u, v, depth = [lambda a, b, get=get: rounded(get(a, b)) for get in sums[:3]]
    return u, v, depth, lambda a, b: jnp.where(sums[3](a, b) > 0.5, 1.0, 0.0)


def propagate_direction(d, trig_ref, rows_of, faces_x, cells, speed_ref, emit):
    first_lane, last_lane, inside, border, face_v, edge_v, half_wet = cells
    along_x = trig_ref[0, d]
    along_y = trig_ref[1, d] * inside
    along_border = trig_ref[1, d] * border
    for quad in range(NF // 4):
        results = []
        for part, (faces, rows) in enumerate(rows_of(d, quad)):
            speed = speed_ref[2 * quad + part]
            speed_x = along_x * speed
            speed_y = along_y * speed
            speed_border = along_border * speed
            flux_x = []
            for (lower, upper), face in zip(faces, faces_x):
                through = speed_x + face
                flux_x.append(through * jnp.where(through > 0.0, lower, upper))
            moved = []
            for row, (here, beyond, entry, exit) in enumerate(rows):
                through = speed_y + face_v[row]
                following = pltpu.roll(jnp.where(first_lane, beyond, here), 127, 1)
                flux = through * jnp.where(through > 0.0, here, following)
                before = pltpu.roll(jnp.where(last_lane, sublane_down(flux), flux), 1, 1)
                lost = jnp.minimum(speed_border + edge_v[row], 0.0) * here
                change = here + (before - flux) + lost
                if entry is not None:
                    change = change + flux_x[entry]
                if exit is not None:
                    change = change - flux_x[exit]
                moved.append(half_wet[row] * change)
            results.append(moved)
        emit(d, quad, results)


def finish_direction(d, trig_ref, rows_of, faces_x, half_wet, speed_ref, emit):
    along_x = trig_ref[0, d]
    for quad in range(NF // 4):
        results = []
        for part, (below, first, second, above, moved) in enumerate(rows_of(d, quad)):
            speed_x = along_x * speed_ref[2 * quad + part]
            through = speed_x + faces_x[0]
            flux_in = through * jnp.where(through > 0.0, below, first)
            through = speed_x + faces_x[1]
            flux_out = through * jnp.where(through > 0.0, second, above)
            results.append([moved[0] + half_wet[0] * flux_in, moved[1] - half_wet[1] * flux_out])
        emit(d, quad, results)


def source_direction(d, trig_ref, moved_ref, damp_ref, rel_x, rel_y, breaking, emit):
    base = base_row(d)
    plus = base_row(lax.rem(d + 2, ND))
    minus = base_row(lax.rem(d + ND - 2, ND))
    wind_along = A_IN * (rel_x * trig_ref[0, d] + rel_y * trig_ref[1, d])
    spreads = {}

    def spread(f):
        if f not in spreads:
            spreads[f] = moved_ref[pl.ds(plus + 8 * f, 8), :] + moved_ref[pl.ds(minus + 8 * f, 8), :]
        return spreads[f]

    for quad in range(NF // 4):
        results = []
        for part in range(4):
            f = 4 * quad + part
            here = moved_ref[pl.ds(base + 8 * f, 8), :]
            growth = jnp.minimum(jnp.maximum(wind_along * float(SIGMA[f]), A_IN), 3.0 * A_IN)
            summed = (growth + damp_ref[f] - here) * here
            if 0 < f < NF - 1:
                summed = summed + (0.5 * C_NL) * spread(f + 1) * spread(f - 1)
            results.append(summed * breaking)
        emit(quad, results)


def by_row(turn_ref, index, field):
    turn_ref[16 * index : 16 * index + 8] = field
    turn_ref[16 * index + 8 : 16 * index + 16] = field
    return [pair_row(turn_ref, 16 * index, row) for row in range(2)]


def pass_cells(turn_ref, v, wet):
    sub, lane = iotas()
    first_lane, last_lane = lane == 0, lane == 127
    block = sub & 3
    inside = jnp.where(last_lane & (block == 3), 0.0, 1.0)
    border = jnp.where(
        first_lane & (block == 0), 1.0, jnp.where(last_lane & (block == 3), -1.0, 0.0)
    )
    half = 0.5 * LAM_W
    face_v, edge_v = [], []
    for v_row in by_row(turn_ref, 0, v):
        after_v = pltpu.roll(jnp.where(first_lane, sublane_up(v_row), v_row), 127, 1)
        face_v.append(inside * (half * (v_row + after_v)))
        edge_v.append(border * (half * v_row))
    half_wet = [0.5 * wet_row for wet_row in by_row(turn_ref, 1, wet)]
    return first_lane, last_lane, inside, border, face_v, edge_v, half_wet


def set_speeds(speed_ref):
    sub, _ = iotas()
    for pair in range(NF // 2):
        low, high = [float(LAM_W * 0.5 / SIGMA[2 * pair + i]) for i in range(2)]
        speed_ref[pair] = jnp.where(sub < 4, low, high)


def each_direction(body):
    lax.fori_loop(0, ND, lambda d, carry: body(d) or carry, 0)


def summing(moved_ref, sums_ref):
    for f in range(NF):
        sums_ref[f] = jnp.zeros((8, 128), F32)

    def emit(d, quad, results):
        for part, moved in enumerate(results):
            pair = 2 * quad + part
            for row in range(2):
                moved_ref[pl.ds(base_row(d) + 16 * pair + row, 8, stride=2), :] = moved[row]
                sums_ref[2 * pair + row] += moved[row]

    return emit


def packing(refs):
    def emit(d, quad, results):
        for row, ref in enumerate(refs):
            block = jnp.concatenate([moved[row] for moved in results], axis=0)
            ref[pl.ds(half_row(d) + 16 * quad, 16), :] = block.astype(BF16)

    return emit


def source_pass(trig_ref, u, v, depth, wet, wind, scratch, emit, initial=0, combine=None):
    moved_ref, damp_ref, sums_ref, turn_ref = scratch
    sub, _ = iotas()
    zeros = jnp.zeros((8, 128), F32)
    for row in range(2):
        zeroth, second = zeros, zeros
        for pair in range(NF // 2):
            low, high = [float(SIGMA[2 * pair + i] ** 2) for i in range(2)]
            zeroth = zeroth + sums_ref[2 * pair + row]
            second = second + sums_ref[2 * pair + row] * jnp.where(sub < 4, low, high)
        for index, value in ((2, zeroth), (3, second)):
            turn_ref[pl.ds(16 * index + row, 8, stride=2), :] = value + pltpu.roll(value, 4, 0)
    moment_zero = turn_ref[32:40] * (2.0 / BINS)
    moment_two = turn_ref[48:56] * (2.0 / BINS)
    limit = (GAMMA_BR * depth) * (GAMMA_BR * depth)
    breaking = jnp.where(wet > 0.5, 2.0 * limit / jnp.maximum(16.0 * moment_zero, limit), 0.0)
    for f in range(NF):
        damp_ref[f] = (1.0 - A_IN) - float(C_WC * SIGMA[f] ** 3) * moment_two
    rel_x = wind[0] - u
    rel_y = wind[1] - v

    def source(d, carried):
        parts = []
        source_direction(
            d,
            trig_ref,
            moved_ref,
            damp_ref,
            rel_x,
            rel_y,
            breaking,
            lambda quad, results: parts.append(emit(d, quad, results)),
        )
        return combine(d, carried, parts) if combine else carried

    return lax.fori_loop(0, ND, source, initial)


def packed_rows(refs, d, quad):
    blocks = [ref[pl.ds(half_row(d) + 16 * quad, 16), :].astype(F32) for ref in refs]
    return [[block[8 * part : 8 * part + 8] for block in blocks] for part in range(2)]


def wave_scratch():
    return [
        VMEM((CELL_ROWS + PAD, 128), F32),
        VMEM((NF, 8, 128), F32),
        VMEM((NF, 8, 128), F32),
        VMEM((64 + PAD, 128), F32),
        VMEM((NF // 2, 8, 128), F32),
    ]


def inner_rows(refs, d, quad):
    return [
        (
            [(lower, upper)],
            [(lower, sublane_up(lower), None, 0), (upper, sublane_up(upper), 0, None)],
        )
        for lower, upper in packed_rows(refs, d, quad)
    ]


def begin_kernel(
    trig_ref, upper_ref, lower_ref, arrived_ref, part_lower_ref, part_upper_ref, turn_ref, speed_ref
):
    u, v, _, wet = strip_fields(arrived_ref)
    own = by_row(turn_ref, 0, u(0, 1))
    face_own = (0.5 * LAM_W) * (own[0] + own[1])
    set_speeds(speed_ref)
    cells = pass_cells(turn_ref, v(0, 1), wet(0, 1))

    def rows_own(d, quad):
        return inner_rows((lower_ref, upper_ref), d, quad)

    emit = packing((part_lower_ref, part_upper_ref))
    each_direction(
        lambda d: propagate_direction(d, trig_ref, rows_own, (face_own,), cells, speed_ref, emit)
    )


def begin_step(trig, *operands):
    here = pl.BlockSpec(memory_space=VMEM)
    return pl.pallas_call(
        begin_kernel,
        out_shape=(jax.ShapeDtypeStruct((HALF_ROWS, 128), BF16),) * 2,
        in_specs=[pl.BlockSpec(memory_space=SMEM)] + [here] * len(operands),
        out_specs=(here,) * 2,
        scratch_shapes=wave_scratch()[-2:],
        compiler_params=params(16),
        cost_estimate=pl.CostEstimate(
            flops=100000000, bytes_accessed=20000000, transcendentals=0
        ),
        name="begin_wave_step",
    )(trig, *operands)


KEPT = 20


def first_kernel(
    trig_ref,
    upper_ref,
    lower_ref,
    above_ref,
    below_ref,
    part_lower_ref,
    part_upper_ref,
    arrived_ref,
    wind_ref,
    spec_lower_ref,
    spec_upper_ref,
    near_above_ref,
    near_below_ref,
    next_lower_ref,
    next_upper_ref,
    above_out_ref,
    below_out_ref,
    fields_ref,
    spec_ref,
    *scratch,
):
    moved_ref, damp_ref, sums_ref, turn_ref, speed_ref = scratch
    u, v, depth, wet = strip_fields(arrived_ref)
    u_own, u_near = u(0, 1), u(-1, 2)
    own = by_row(turn_ref, 0, u_own)
    near = by_row(turn_ref, 1, u_near)
    half = 0.5 * LAM_W
    face_low = half * (near[0] + own[0])
    face_own = half * (own[0] + own[1])
    face_high = half * (own[1] + near[1])
    wind = wind_ref[...].astype(F32)
    set_speeds(speed_ref)
    v_own, wet_own = v(0, 1), wet(0, 1)
    cells = pass_cells(turn_ref, v_own, wet_own)

    above_out_ref[...] = above_ref[0:HALF_ROWS, :]
    below_out_ref[...] = below_ref[0:HALF_ROWS, :]
    far = by_row(turn_ref, 2, u(-2, 3))
    wet_near = wet(-1, 2)
    for row, ref in ((0, above_ref), (1, below_ref)):
        arrived_wind = ref[HALF_ROWS:, :].astype(F32)[0:8]
        turn_ref[pl.ds(48 + row, 8, stride=2), :] = arrived_wind
    kept = [half * (far[0] + near[0]), half * (near[1] + far[1]), face_low, face_high]
    kept += [u_near, v(-1, 2), depth(-1, 2), wet_near, turn_ref[48:56], turn_ref[56:64]]
    kept += [u_own, v_own, depth(0, 1), wet_own, wind[0:8], wind[8:16]]
    kept += [0.5 * row for field in (wet_near, wet_own) for row in by_row(turn_ref, 0, field)]
    for index, field in enumerate(kept):
        fields_ref[index] = field

    def rows_first(d, quad):
        refs = (above_ref, lower_ref, upper_ref, below_ref, part_lower_ref, part_upper_ref)
        return [(*rows[:4], rows[4:]) for rows in packed_rows(refs, d, quad)]

    emit = summing(moved_ref, sums_ref)
    faces = (face_low, face_high)
    half_own = cells[-1]
    each_direction(
        lambda d: finish_direction(d, trig_ref, rows_first, faces, half_own, speed_ref, emit)
    )

    def emit_spec(d, quad, results):
        start = base_row(d) + 32 * quad
        spec_ref[pl.ds(start, 32), :] = jnp.concatenate(results, axis=0)
        for row, ref in ((0, spec_lower_ref), (1, spec_upper_ref)):
            halves = [pair_row(spec_ref, start + 16 * pair, row) for pair in range(2)]
            packed = jnp.concatenate(halves, axis=0).astype(BF16)
            ref[pl.ds(half_row(d) + 16 * quad, 16), :] = packed

    source_pass(
        trig_ref,
        u_own,
        v_own,
        depth(0, 1),
        wet_own,
        (wind[0:8], wind[8:16]),
        (moved_ref, damp_ref, sums_ref, turn_ref),
        emit_spec,
    )

    def rows_second(d, quad):
        return inner_rows((spec_lower_ref, spec_upper_ref), d, quad)

    emit_next = packing((next_lower_ref, next_upper_ref))
    each_direction(
        lambda d: propagate_direction(
            d, trig_ref, rows_second, (face_own,), cells, speed_ref, emit_next
        )
    )

    cells_near = pass_cells(turn_ref, v(-1, 2), wet(-1, 2))

    def rows_near(d, quad):
        return [
            (
                [(above, lower), (upper, below)],
                [(above, sublane_up(above), None, 0), (below, sublane_up(below), 1, None)],
            )
            for above, lower, upper, below in packed_rows(
                (above_ref, lower_ref, upper_ref, below_ref), d, quad
            )
        ]

    emit_near = packing((near_above_ref, near_below_ref))
    each_direction(
        lambda d: propagate_direction(
            d, trig_ref, rows_near, (face_low, face_high), cells_near, speed_ref, emit_near
        )
    )


def second_kernel(
    trig_ref,
    far_above_ref,
    far_below_ref,
    spec_lower_ref,
    spec_upper_ref,
    near_above_ref,
    near_below_ref,
    next_lower_ref,
    next_upper_ref,
    above_ref,
    below_ref,
    fields_ref,
    out_hbm,
    stress_hbm,
    near_ref,
    out_ref,
    sem,
    stress_ref,
    stress_sem,
    *scratch,
):
    moved_ref, damp_ref, sums_ref, turn_ref, speed_ref = scratch
    shared = (moved_ref, damp_ref, sums_ref, turn_ref)
    kept = [fields_ref[index] for index in range(KEPT)]
    faces_near, faces_own = kept[0:2], kept[2:4]
    half_near, half_own = kept[16:18], kept[18:20]
    set_speeds(speed_ref)

    def rows_near(d, quad):
        refs = (far_above_ref, above_ref, below_ref, far_below_ref, near_above_ref, near_below_ref)
        return [(*rows[:4], rows[4:]) for rows in packed_rows(refs, d, quad)]

    emit = summing(moved_ref, sums_ref)
    each_direction(
        lambda d: finish_direction(d, trig_ref, rows_near, faces_near, half_near, speed_ref, emit)
    )

    def emit_near(d, quad, results):
        near_ref[pl.ds(base_row(d) + 32 * quad, 32), :] = jnp.concatenate(results, axis=0)

    source_pass(trig_ref, *kept[4:8], kept[8:10], shared, emit_near)

    def rows_own(d, quad):
        refs = (spec_lower_ref, spec_upper_ref, next_lower_ref, next_upper_ref)
        parts = []
        for part, rows in enumerate(packed_rows(refs, d, quad)):
            start = base_row(d) + 32 * quad + 16 * part
            below, above = [pair_row(near_ref, start, row) for row in range(2)]
            parts.append((below, rows[0], rows[1], above, rows[2:]))
        return parts

    emit = summing(moved_ref, sums_ref)
    each_direction(
        lambda d: finish_direction(d, trig_ref, rows_own, faces_own, half_own, speed_ref, emit)
    )
    outgoing = chunk_copies(out_ref, out_hbm, sem)
    zeros = jnp.zeros((8, 128), F32)

    def emit_own(d, quad, results):
        packed = jnp.concatenate(results, axis=0).astype(BF16)
        out_ref[d, 32 * quad : 32 * quad + 32, :] = packed
        scales = [float(math.pi / ND * SIGMA[4 * quad + part] / NF) for part in range(4)]
        return sum(result * scale for result, scale in zip(results, scales))

    def add_stress(d, totals, parts):
        @pl.when(lax.rem(d, CHUNK) == CHUNK - 1)
        def _():
            outgoing(lax.div(d, CHUNK)).start()

        total = sum(parts)
        cos_d, sin_d = trig_ref[0, d], trig_ref[1, d]
        xx, xy, yy = totals
        return (
            xx + total * (cos_d * cos_d),
            xy + total * (cos_d * sin_d),
            yy + total * (sin_d * sin_d),
        )

    totals = source_pass(
        trig_ref,
        *kept[10:14],
        kept[14:16],
        shared,
        emit_own,
        (zeros, zeros, zeros),
        add_stress,
    )
    for c in range(3):
        for tile in range(8):
            part = tile // 2
            stress_ref[tile, 2 * c : 2 * c + 2, :] = totals[c][2 * part : 2 * part + 2]
    stress_copy = pltpu.make_async_copy(stress_ref, stress_hbm, stress_sem)
    stress_copy.start()
    for index in range(ND // CHUNK):
        outgoing(index).wait()
    stress_copy.wait()


def first_step(trig, *operands):
    here = pl.BlockSpec(memory_space=VMEM)
    return pl.pallas_call(
        first_kernel,
        out_shape=(jax.ShapeDtypeStruct((HALF_ROWS, 128), BF16),) * 8
        + (jax.ShapeDtypeStruct((KEPT, 8, 128), F32),),
        in_specs=[pl.BlockSpec(memory_space=SMEM)] + [here] * len(operands),
        out_specs=(here,) * 9,
        scratch_shapes=[VMEM((CELL_ROWS + PAD, 128), F32)] + wave_scratch(),
        compiler_params=params(32),
        cost_estimate=pl.CostEstimate(
            flops=100000000, bytes_accessed=60000000, transcendentals=0
        ),
        name="first_wave_step",
    )(trig, *operands)


def second_step(trig, *operands):
    here = pl.BlockSpec(memory_space=VMEM)
    full = jax.ShapeDtypeStruct((ND, NF * 8, 128), BF16)
    return pl.pallas_call(
        second_kernel,
        out_shape=(full, jax.ShapeDtypeStruct((8, 6, 128), F32)),
        in_specs=[pl.BlockSpec(memory_space=SMEM)] + [here] * len(operands),
        out_specs=(pl.BlockSpec(memory_space=pl.ANY),) * 2,
        scratch_shapes=[
            VMEM((CELL_ROWS + PAD, 128), F32),
            VMEM(full.shape, BF16),
            pltpu.SemaphoreType.DMA((ND // CHUNK,)),
            VMEM((8, 6, 128), F32),
            pltpu.SemaphoreType.DMA,
        ]
        + wave_scratch(),
        compiler_params=params(36),
        cost_estimate=pl.CostEstimate(
            flops=200000000, bytes_accessed=40000000, transcendentals=0
        ),
        name="second_wave_step",
    )(trig, *operands)


def ocean_kernel(place_ref, vel_ref, own_ref, low_ref, high_ref, arrived_ref, out_ref, level_ref):
    row = lax.broadcasted_iota(jnp.int32, (32, 128), 0)
    lane = lax.broadcasted_iota(jnp.int32, (32, 128), 1)
    first_row, last_row = row == 0, row == 31
    first_lane, last_lane = lane == 0, lane == 127
    levels = vel_ref.shape[1]
    place = place_ref[0]
    before = arrived_ref[jnp.maximum(place - 1, 0), COLUMNS_AT:, :]
    before = jnp.where(place > 0, before, 0.0)
    after = arrived_ref[jnp.minimum(place + 1, 7), COLUMNS_AT:, :]
    after = jnp.where(place < 7, after, 0.0)

    def down(x, edge):
        return jnp.where(first_row, edge, pltpu.roll(x, 1, 0))

    def up(x, edge):
        return jnp.where(last_row, edge, pltpu.roll(x, 31, 0))

    def left(x, index):
        return jnp.where(first_lane, before[:, index : index + 1], pltpu.roll(x, 1, 1))

    def right(x, index):
        return jnp.where(last_lane, after[:, index : index + 1], pltpu.roll(x, 127, 1))

    def edge_rows(index):
        return low_ref[index, 7:8, :], high_ref[index, 0:1, :]

    level, bathy, wet, sxx, sxy, syy = [own_ref[i] for i in range(6)]
    ubar, vbar = own_ref[10], own_ref[11]
    edges = [edge_rows(i) for i in range(FIELDS)]
    plane_count = 2 * levels
    depth = bathy + level
    flux_x = depth * ubar
    flux_low = (edges[0][0] + edges[1][0]) * edges[10][0]
    flux_high = (edges[0][1] + edges[1][1]) * edges[10][1]
    flux_y = depth * vbar
    divergence = (
        up(flux_x, flux_high)
        - down(flux_x, flux_low)
        + right(flux_y, plane_count + 3)
        - left(flux_y, plane_count + 3)
    )
    level_ref[...] = level - 0.5 * LAM_O * wet * divergence
    inverse = 1.0 / depth
    grad_x = 0.5 * (up(level, edges[0][1]) - down(level, edges[0][0]))
    grad_y = 0.5 * (right(level, plane_count) - left(level, plane_count))
    xx_x = up(sxx, edges[3][1]) - down(sxx, edges[3][0])
    xy_x = up(sxy, edges[4][1]) - down(sxy, edges[4][0])
    xy_y = right(sxy, plane_count + 1) - left(sxy, plane_count + 1)
    yy_y = right(syy, plane_count + 2) - left(syy, plane_count + 2)
    base = (
        -LAM_O * grad_x - 0.5 * LAM_O * (xx_x + xy_y) * inverse,
        -LAM_O * grad_y - 0.5 * LAM_O * (xy_x + yy_y) * inverse,
    )
    turn = (F_CORIOLIS, -F_CORIOLIS)
    for k in range(levels):
        for c in range(2):
            plane = c * levels + k
            here = vel_ref[c, k]
            other = vel_ref[1 - c, k]
            above = vel_ref[c, max(k - 1, 0)]
            below = vel_ref[c, min(k + 1, levels - 1)]
            block, place = FIELDS + plane // 8, plane % 8
            low = low_ref[block, place : place + 1, :]
            high = high_ref[block, place : place + 1, :]
            around = up(here, high) + down(here, low) + right(here, plane) + left(here, plane)
            tendency = (
                base[c]
                + turn[c] * other
                + NU_H * (around - 4.0 * here)
                + KAPPA_V * (above + below - 2.0 * here)
            )
            out_ref[c, k] = wet * (here + tendency)


def ocean_step(place, vel, *operands):
    return pl.pallas_call(
        ocean_kernel,
        out_shape=(
            jax.ShapeDtypeStruct(vel.shape, F32),
            jax.ShapeDtypeStruct((32, 128), F32),
        ),
        in_specs=[pl.BlockSpec(memory_space=SMEM)] + [pl.BlockSpec(memory_space=VMEM)] * 5,
        out_specs=(pl.BlockSpec(memory_space=VMEM),) * 2,
        compiler_params=params(16),
        cost_estimate=pl.CostEstimate(flops=10000000, bytes_accessed=3000000, transcendentals=0),
        name="ocean_step",
    )(place, vel, *operands)


def shifted(array, axis_name, up):
    count = lax.axis_size(axis_name)
    pairs = [(i, i + 1) for i in range(count - 1)]
    if not up:
        pairs = [(target, source) for source, target in pairs]
    return lax.ppermute(array, axis_name, pairs)


def after(value, *others):
    return lax.optimization_barrier((value,) + others)[0]


def per_device(ocean_level, ocean_velocity, bathymetry, sea_mask, stress_in, spectra, wind_field):
    both = ("wide", "deep")
    spec = spectra.reshape(ND, NF, 2, 4, 128).transpose(0, 1, 3, 2, 4).reshape(ND, NF * 8, 128)
    wind = wind_field.reshape(2, 2, 4, 128).transpose(0, 2, 1, 3).reshape(16, 128)
    trig = jnp.asarray(TRIG)

    own, low_edge, high_edge, first, last = gather_surface(
        ocean_level, ocean_velocity, bathymetry, sea_mask, stress_in
    )
    from_low = shifted(high_edge, "wide", True)
    from_high = shifted(low_edge, "wide", False)
    upper, lower = split_rows(after(spec, own), wind)
    place = lax.axis_index("deep").astype(jnp.int32).reshape(1)
    outgoing = surface_step(place, after(own, upper), from_low, from_high, first, last)
    arrived = lax.all_to_all(outgoing, "deep", split_axis=0, concat_axis=0, tiled=True)

    above = shifted(after(upper, from_low, from_high), both, True)
    below = shifted(after(lower, from_low, from_high), both, False)
    far_above = shifted(after(lower, arrived), both, True)
    far_below = shifted(after(upper, arrived), both, False)
    velocity_out, level_out = ocean_step(
        place, ocean_velocity, own, from_low, from_high, arrived
    )
    begun = begin_step(trig, upper, lower, arrived)
    partial = first_step(
        trig, upper, lower, above, below, *begun, after(arrived, level_out), wind
    )
    spec, stress = second_step(trig, far_above, far_below, *partial)
    stress = lax.all_to_all(stress, "deep", split_axis=0, concat_axis=0, tiled=True)
    stress = stress.reshape(8, 3, 2, 128).transpose(1, 0, 2, 3).reshape(3, 16, 128)
    stress_out = jnp.where((place[0] & 1) == 1, stress[:, :, 64:], stress[:, :, :64])
    spectra_out = (
        spec.reshape(ND, NF, 4, 2, 128).transpose(0, 1, 3, 2, 4).reshape(ND, NF, 2, 512)
    )
    return (level_out, velocity_out, spectra_out, stress_out)


def solution(mesh):
    in_specs = (
        P("wide", "deep"),
        P(None, None, "wide", "deep"),
        P("wide", "deep"),
        P("wide", "deep"),
        P(None, "wide", "deep"),
        P(None, None, ("wide", "deep"), None),
        P(None, ("wide", "deep"), None),
    )
    out_specs = (
        P("wide", "deep"),
        P(None, None, "wide", "deep"),
        P(None, None, ("wide", "deep"), None),
        P(None, "wide", "deep"),
    )
    return jax.shard_map(
        per_device, mesh=mesh, in_specs=in_specs, out_specs=out_specs, check_vma=False
    )
```

```python
import math

import numpy as np

import jax
import jax.numpy as jnp
from jax import lax
from jax.experimental import pallas as pl
from jax.experimental.pallas import tpu as pltpu
from jax.sharding import PartitionSpec as P

LAM_O = 0.2
F_CORIOLIS = 0.1
NU_H = 0.05
KAPPA_V = 0.2
LAM_W = 0.25
GAMMA_BR = 0.73
A_IN = 0.15
C_NL = 0.5
C_WC = 0.002

ND = 36
NF = 36
SIGMA = 0.4 * np.power(1.07, np.arange(NF))
ANGLE = 2.0 * math.pi * np.arange(ND) / ND
TRIG = np.stack([np.cos(ANGLE), np.sin(ANGLE)]).astype(np.float32)

F32 = jnp.float32
BF16 = jnp.bfloat16
VMEM = pltpu.VMEM
SMEM = pltpu.SMEM
HIGH = lax.Precision.HIGHEST


def params(mib):
    return pltpu.CompilerParams(vmem_limit_bytes=mib * 1024 * 1024)


BINS = ND * NF
CELL_ROWS = BINS * 8
PAD = 16
CHUNK = 3


def iotas():
    sub = lax.broadcasted_iota(jnp.int32, (8, 128), 0)
    lane = lax.broadcasted_iota(jnp.int32, (8, 128), 1)
    return sub, lane


def sublane_up(x):
    return pltpu.roll(x, 7, 0)


def sublane_down(x):
    return pltpu.roll(x, 1, 0)


def base_row(d):
    return pl.multiple_of(d * (NF * 8), 8)


def pair_row(ref, start, row):
    return ref[pl.ds(start + row, 8, stride=2), :]


def half_row(d):
    return pl.multiple_of(d * (NF * 4), 16)


HALF_ROWS = BINS * 4


def chunk_copies(source, target, sem):
    def copy(index):
        part = pl.ds(index * CHUNK, CHUNK)
        return pltpu.make_async_copy(source.at[part], target.at[part], sem.at[index])

    return copy


def split_rows_kernel(
    spec_hbm,
    wind_ref,
    upper_hbm,
    lower_hbm,
    held_ref,
    spec_ref,
    turn_ref,
    upper_ref,
    lower_ref,
    sem,
    out_sem,
):
    incoming = chunk_copies(spec_hbm, held_ref, sem)
    chunks = ND // CHUNK

    def outgoing(side, index):
        source, target = ((lower_ref, lower_hbm), (upper_ref, upper_hbm))[side]
        start = pl.multiple_of(index * (CHUNK * NF * 4), 16)
        part = pl.ds(start, CHUNK * NF * 4)
        return pltpu.make_async_copy(source.at[part], target.at[part], out_sem.at[side, index])

    def outgoing_wind(side):
        source, target = ((lower_ref, lower_hbm), (upper_ref, upper_hbm))[side]
        part = pl.ds(HALF_ROWS, 16)
        return pltpu.make_async_copy(source.at[part], target.at[part], out_sem.at[side, chunks])

    for index in range(ND // CHUNK):
        incoming(index).start()
    turn_ref[0:16, :] = wind_ref[...].astype(F32)
    sides = ((0, lower_ref), (1, upper_ref))
    for row, ref in sides:
        wind = jnp.concatenate([pair_row(turn_ref, 0, row), jnp.zeros((8, 128), F32)], axis=0)
        ref[HALF_ROWS:, :] = wind.astype(BF16)
        outgoing_wind(row).start()

    def body(d, carry):
        @pl.when(lax.rem(d, CHUNK) == 0)
        def _():
            incoming(lax.div(d, CHUNK)).wait()

        base = base_row(d)
        for quad in range(NF // 4):
            block = held_ref[d, 32 * quad : 32 * quad + 32, :].astype(F32)
            spec_ref[pl.ds(base + 32 * quad, 32), :] = block
        for quad in range(NF // 4):
            start = base + 32 * quad
            for row, ref in sides:
                halves = [pair_row(spec_ref, start + 16 * pair, row) for pair in range(2)]
                packed = jnp.concatenate(halves, axis=0).astype(BF16)
                ref[pl.ds(half_row(d) + 16 * quad, 16), :] = packed

        @pl.when(lax.rem(d, CHUNK) == CHUNK - 1)
        def _():
            for side in range(2):
                outgoing(side, lax.div(d, CHUNK)).start()

        return carry

    lax.fori_loop(0, ND, body, 0)
    for side in range(2):
        outgoing_wind(side).wait()
        for index in range(chunks):
            outgoing(side, index).wait()


def split_rows(spec, wind):
    half = jax.ShapeDtypeStruct((HALF_ROWS + 16, 128), BF16)
    return pl.pallas_call(
        split_rows_kernel,
        out_shape=(half, half),
        in_specs=[pl.BlockSpec(memory_space=pltpu.HBM), pl.BlockSpec(memory_space=VMEM)],
        out_specs=(pl.BlockSpec(memory_space=pl.ANY),) * 2,
        scratch_shapes=[
            VMEM(spec.shape, BF16),
            VMEM((CELL_ROWS + PAD, 128), F32),
            VMEM((16 + PAD, 128), F32),
            VMEM(half.shape, BF16),
            VMEM(half.shape, BF16),
            pltpu.SemaphoreType.DMA((ND // CHUNK,)),
            pltpu.SemaphoreType.DMA((2, ND // CHUNK + 1)),
        ],
        compiler_params=params(56),
        cost_estimate=pl.CostEstimate(flops=4000000, bytes_accessed=9000000, transcendentals=0),
        name="split_rows",
    )(spec, wind)


FIELDS = 12


def edge_columns(planes):
    lane = lax.broadcasted_iota(jnp.int32, (32, 128), 1)
    first = jnp.zeros((32, 128), F32)
    last = jnp.zeros((32, 128), F32)
    for index, plane in enumerate(planes):
        here = lane == index
        first = jnp.where(here, pltpu.roll(plane, index, 1), first)
        last = jnp.where(here, pltpu.roll(plane, (index + 1) % 128, 1), last)
    return first, last


def gather_kernel(
    level_ref,
    vel_ref,
    bathy_ref,
    mask_ref,
    stress_ref,
    own_hbm,
    low_hbm,
    high_hbm,
    first_ref,
    last_ref,
    own_ref,
    low_ref,
    high_ref,
    sem,
):
    levels = vel_ref.shape[1]
    fields = [
        level_ref[...],
        bathy_ref[...],
        mask_ref[...].astype(F32),
        stress_ref[0],
        stress_ref[1],
        stress_ref[2],
        vel_ref[0, 0],
        vel_ref[1, 0],
        vel_ref[0, 1],
        vel_ref[1, 1],
    ]
    for c in range(2):
        total = vel_ref[c, 0]
        for k in range(1, levels):
            total = total + vel_ref[c, k]
        fields.append(total * (1.0 / levels))
    for index, field in enumerate(fields):
        own_ref[index] = field
        low_ref[index] = field[0:8]
        high_ref[index] = field[24:32]
    blocks = levels // 8
    for c in range(2):
        part = slice(FIELDS + blocks * c, FIELDS + blocks * c + blocks)
        low_ref[part] = vel_ref[c, :, 0, :].reshape(blocks, 8, 128)
        high_ref[part] = vel_ref[c, :, 31, :].reshape(blocks, 8, 128)
    pairs = ((own_ref, own_hbm), (low_ref, low_hbm), (high_ref, high_hbm))
    copies = [pltpu.make_async_copy(*pair, sem.at[i]) for i, pair in enumerate(pairs)]
    for copy in copies:
        copy.start()
    planes = [vel_ref[c, k] for c in range(2) for k in range(levels)]
    planes += [fields[0], fields[4], fields[5], (fields[0] + fields[1]) * fields[11]]
    first_ref[...], last_ref[...] = edge_columns(planes)
    for copy in copies:
        copy.wait()


def gather_surface(level, vel, bathy, mask, stress):
    rows, cols = level.shape
    edge = jax.ShapeDtypeStruct((FIELDS + vel.shape[1] // 4, 8, cols), F32)
    column = jax.ShapeDtypeStruct((rows, cols), F32)
    return pl.pallas_call(
        gather_kernel,
        out_shape=(jax.ShapeDtypeStruct((FIELDS, rows, cols), F32), edge, edge, column, column),
        in_specs=[pl.BlockSpec(memory_space=VMEM)] * 5,
        out_specs=(pl.BlockSpec(memory_space=pl.ANY),) * 3
        + (pl.BlockSpec(memory_space=VMEM),) * 2,
        scratch_shapes=[
            VMEM((FIELDS, rows, cols), F32),
            VMEM(edge.shape, F32),
            VMEM(edge.shape, F32),
            pltpu.SemaphoreType.DMA((3,)),
        ],
        compiler_params=params(56),
        cost_estimate=pl.CostEstimate(flops=400000, bytes_accessed=1700000, transcendentals=0),
        name="gather_surface",
    )(level, vel, bathy, mask, stress)


EXT = 48
ROWS_SENT = 6
EDGE_AT = 4 * ROWS_SENT
COLUMNS_AT = 40
SENT_ROWS = COLUMNS_AT + 32


def surface_kernel(place_ref, own_ref, low_ref, high_ref, first_ref, last_ref, out_ref):
    lane = lax.broadcasted_iota(jnp.int32, (EXT, 128), 1)

    def field(index):
        return jnp.concatenate([low_ref[index], own_ref[index], high_ref[index]], axis=0)

    level, bathy, wet, sxx, sxy, syy, u, v, u1, v1, ubar, vbar = [field(i) for i in range(FIELDS)]

    def down(x):
        return pltpu.roll(x, 1, 0)

    def up(x):
        return pltpu.roll(x, EXT - 1, 0)

    def left(x):
        return jnp.where(lane == 0, 0.0, pltpu.roll(x, 1, 1))

    def right(x):
        return jnp.where(lane == 127, 0.0, pltpu.roll(x, 127, 1))

    depth = bathy + level
    inverse = 1.0 / jnp.where(depth > 0.0, depth, 1.0)
    flux_x = depth * ubar
    flux_y = depth * vbar
    divergence = up(flux_x) - down(flux_x) + right(flux_y) - left(flux_y)
    new_depth = bathy + (level - 0.5 * LAM_O * wet * divergence)
    grad_x = 0.5 * (up(level) - down(level))
    grad_y = 0.5 * (right(level) - left(level))
    force_x = -0.5 * (up(sxx) - down(sxx) + (right(sxy) - left(sxy))) * inverse
    force_y = -0.5 * (up(sxy) - down(sxy) + (right(syy) - left(syy))) * inverse
    laplace_u = up(u) + down(u) + right(u) + left(u) - 4.0 * u
    laplace_v = up(v) + down(v) + right(v) + left(v) - 4.0 * v
    new_u = wet * (
        u
        - LAM_O * grad_x
        + F_CORIOLIS * v
        + LAM_O * force_x
        + NU_H * laplace_u
        + KAPPA_V * (u1 - u)
    )
    new_v = wet * (
        v
        - LAM_O * grad_y
        - F_CORIOLIS * u
        + LAM_O * force_y
        + NU_H * laplace_v
        + KAPPA_V * (v1 - v)
    )

    column = lax.broadcasted_iota(jnp.int32, (128, 128), 0)
    target = lax.broadcasted_iota(jnp.int32, (128, 128), 1)
    to_coarse = jnp.where(target == 64 * (place_ref[0] & 1) + (column >> 1), 0.25, 0.0)
    coarse_row = lax.broadcasted_iota(jnp.int32, (24, EXT), 0)
    fine_row = lax.broadcasted_iota(jnp.int32, (24, EXT), 1)
    pair_sum = jnp.where((fine_row >> 1) == coarse_row, 1.0, 0.0)
    stacked = jnp.concatenate([new_u, new_v, new_depth, wet], axis=0)
    narrowed = jnp.dot(stacked, to_coarse, precision=HIGH, preferred_element_type=F32)
    for index in range(4):
        coarse = jnp.dot(
            pair_sum,
            narrowed[EXT * index : EXT * index + EXT],
            precision=HIGH,
            preferred_element_type=F32,
        )
        for strip in range(8):
            first = 2 * strip + 2
            rows = slice(ROWS_SENT * index, ROWS_SENT * index + ROWS_SENT)
            out_ref[strip, rows, :] = coarse[first : first + ROWS_SENT]

    wet_inverse = wet * inverse
    to_right = [u, v, sxy, syy, level, flux_y]
    to_left = [u, v, -sxy, -syy, -level, -flux_y]
    weights = [
        NU_H * wet,
        NU_H * wet,
        0.5 * LAM_O * wet_inverse,
        0.5 * LAM_O * wet_inverse,
        0.5 * LAM_O * wet,
        0.5 * LAM_O * wet,
    ]
    edges = jnp.zeros((EXT, 128), F32)
    for index in range(6):
        edges = jnp.where(lane == index, to_right[index][:, 127:128], edges)
        edges = jnp.where(lane == 8 + index, to_left[index][:, 0:1], edges)
        edges = jnp.where(lane == 16 + index, weights[index][:, 0:1], edges)
        edges = jnp.where(lane == 24 + index, weights[index][:, 127:128], edges)
    for strip in range(8):
        first = 4 * strip + 4
        rows = 2 * ROWS_SENT
        out_ref[strip, EDGE_AT : EDGE_AT + rows, :] = edges[first : first + rows]
        blank = jnp.zeros((COLUMNS_AT - EDGE_AT - rows, 128), F32)
        out_ref[strip, EDGE_AT + rows : COLUMNS_AT, :] = blank
        columns = jnp.where(place_ref[0] == strip - 1, last_ref[...], 0.0)
        columns = jnp.where(place_ref[0] == strip + 1, first_ref[...], columns)
        out_ref[strip, COLUMNS_AT:, :] = columns


def surface_step(place, *operands):
    return pl.pallas_call(
        surface_kernel,
        out_shape=jax.ShapeDtypeStruct((8, SENT_ROWS, 128), F32),
        in_specs=[pl.BlockSpec(memory_space=SMEM)] + [pl.BlockSpec(memory_space=VMEM)] * 5,
        out_specs=pl.BlockSpec(memory_space=VMEM),
        compiler_params=params(16),
        cost_estimate=pl.CostEstimate(flops=2000000, bytes_accessed=400000, transcendentals=0),
        name="surface_step",
    )(place, *operands)


def rounded(x):
    return x.astype(BF16).astype(F32)


def strip_fields(arrived_ref):
    sub, lane = iotas()
    even = (sub & 1) == 0
    base = 64 * (sub & 1)
    edge_sums = []
    for row in range(ROWS_SENT):
        total = None
        for fine in (2 * row, 2 * row + 1):
            edge = arrived_ref[:, EDGE_AT + fine, :]
            from_left = jnp.where(sub == 0, 0.0, sublane_down(edge))
            from_right = jnp.where(sub == 7, 0.0, sublane_up(edge))
            weight = pltpu.roll(edge, 112, 1)
            product = weight * jnp.where(lane < 8, from_left, from_right)
            total = product if total is None else total + product
        edge_sums.append(0.25 * total)

    def tiles(index, row, parts):
        value = arrived_ref[:, ROWS_SENT * index + row + 2, :]
        if parts:
            edge = edge_sums[row + 2]
            left = sum(edge[:, p : p + 1] for p in parts)
            right = sum(edge[:, 8 + p : 9 + p] for p in parts)
            value = value + jnp.where(lane == base, left, 0.0)
            value = value + jnp.where(lane == base + 63, right, 0.0)
        return value

    def field(index, parts):
        def of_rows(first_row, second_row):
            first = tiles(index, first_row, parts)
            second = tiles(index, second_row, parts)
            return jnp.where(even, first + sublane_up(first), second + sublane_down(second))

        return of_rows

    sums = [field(0, (0, 2)), field(1, (1, 3, 4)), field(2, (5,)), field(3, ())]
    u, v, depth = [lambda a, b, get=get: rounded(get(a, b)) for get in sums[:3]]
    return u, v, depth, lambda a, b: jnp.where(sums[3](a, b) > 0.5, 1.0, 0.0)


def propagate_direction(d, trig_ref, rows_of, faces_x, cells, speed_ref, emit):
    first_lane, last_lane, inside, border, face_v, edge_v, half_wet = cells
    along_x = trig_ref[0, d]
    along_y = trig_ref[1, d] * inside
    along_border = trig_ref[1, d] * border
    for quad in range(NF // 4):
        results = []
        for part, (faces, rows) in enumerate(rows_of(d, quad)):
            speed = speed_ref[2 * quad + part]
            speed_x = along_x * speed
            speed_y = along_y * speed
            speed_border = along_border * speed
            flux_x = []
            for (lower, upper), face in zip(faces, faces_x):
                through = speed_x + face
                flux_x.append(through * jnp.where(through > 0.0, lower, upper))
            moved = []
            for row, (here, beyond, entry, exit) in enumerate(rows):
                through = speed_y + face_v[row]
                following = pltpu.roll(jnp.where(first_lane, beyond, here), 127, 1)
                flux = through * jnp.where(through > 0.0, here, following)
                before = pltpu.roll(jnp.where(last_lane, sublane_down(flux), flux), 1, 1)
                lost = jnp.minimum(speed_border + edge_v[row], 0.0) * here
                change = here + (before - flux) + lost
                if entry is not None:
                    change = change + flux_x[entry]
                if exit is not None:
                    change = change - flux_x[exit]
                moved.append(half_wet[row] * change)
            results.append(moved)
        emit(d, quad, results)


def finish_direction(d, trig_ref, rows_of, faces_x, half_wet, speed_ref, emit):
    along_x = trig_ref[0, d]
    for quad in range(NF // 4):
        results = []
        for part, (below, first, second, above, moved) in enumerate(rows_of(d, quad)):
            speed_x = along_x * speed_ref[2 * quad + part]
            through = speed_x + faces_x[0]
            flux_in = through * jnp.where(through > 0.0, below, first)
            through = speed_x + faces_x[1]
            flux_out = through * jnp.where(through > 0.0, second, above)
            results.append([moved[0] + half_wet[0] * flux_in, moved[1] - half_wet[1] * flux_out])
        emit(d, quad, results)


def source_direction(d, trig_ref, moved_ref, damp_ref, rel_x, rel_y, breaking, emit):
    base = base_row(d)
    plus = base_row(lax.rem(d + 2, ND))
    minus = base_row(lax.rem(d + ND - 2, ND))
    wind_along = A_IN * (rel_x * trig_ref[0, d] + rel_y * trig_ref[1, d])
    spreads = {}

    def spread(f):
        if f not in spreads:
            spreads[f] = moved_ref[pl.ds(plus + 8 * f, 8), :] + moved_ref[pl.ds(minus + 8 * f, 8), :]
        return spreads[f]

    for quad in range(NF // 4):
        results = []
        for part in range(4):
            f = 4 * quad + part
            here = moved_ref[pl.ds(base + 8 * f, 8), :]
            growth = jnp.minimum(jnp.maximum(wind_along * float(SIGMA[f]), A_IN), 3.0 * A_IN)
            summed = (growth + damp_ref[f] - here) * here
            if 0 < f < NF - 1:
                summed = summed + (0.5 * C_NL) * spread(f + 1) * spread(f - 1)
            results.append(summed * breaking)
        emit(quad, results)


def by_row(turn_ref, index, field):
    turn_ref[16 * index : 16 * index + 8] = field
    turn_ref[16 * index + 8 : 16 * index + 16] = field
    return [pair_row(turn_ref, 16 * index, row) for row in range(2)]


def pass_cells(turn_ref, v, wet):
    sub, lane = iotas()
    first_lane, last_lane = lane == 0, lane == 127
    block = sub & 3
    inside = jnp.where(last_lane & (block == 3), 0.0, 1.0)
    border = jnp.where(
        first_lane & (block == 0), 1.0, jnp.where(last_lane & (block == 3), -1.0, 0.0)
    )
    half = 0.5 * LAM_W
    face_v, edge_v = [], []
    for v_row in by_row(turn_ref, 0, v):
        after_v = pltpu.roll(jnp.where(first_lane, sublane_up(v_row), v_row), 127, 1)
        face_v.append(inside * (half * (v_row + after_v)))
        edge_v.append(border * (half * v_row))
    half_wet = [0.5 * wet_row for wet_row in by_row(turn_ref, 1, wet)]
    return first_lane, last_lane, inside, border, face_v, edge_v, half_wet


def set_speeds(speed_ref):
    sub, _ = iotas()
    for pair in range(NF // 2):
        low, high = [float(LAM_W * 0.5 / SIGMA[2 * pair + i]) for i in range(2)]
        speed_ref[pair] = jnp.where(sub < 4, low, high)


def each_direction(body):
    lax.fori_loop(0, ND, lambda d, carry: body(d) or carry, 0)


def summing(moved_ref, sums_ref):
    for f in range(NF):
        sums_ref[f] = jnp.zeros((8, 128), F32)

    def emit(d, quad, results):
        for part, moved in enumerate(results):
            pair = 2 * quad + part
            for row in range(2):
                moved_ref[pl.ds(base_row(d) + 16 * pair + row, 8, stride=2), :] = moved[row]
                sums_ref[2 * pair + row] += moved[row]

    return emit


def packing(refs):
    def emit(d, quad, results):
        for row, ref in enumerate(refs):
            block = jnp.concatenate([moved[row] for moved in results], axis=0)
            ref[pl.ds(half_row(d) + 16 * quad, 16), :] = block.astype(BF16)

    return emit


def source_pass(trig_ref, u, v, depth, wet, wind, scratch, emit, initial=0, combine=None):
    moved_ref, damp_ref, sums_ref, turn_ref = scratch
    sub, _ = iotas()
    zeros = jnp.zeros((8, 128), F32)
    for row in range(2):
        zeroth, second = zeros, zeros
        for pair in range(NF // 2):
            low, high = [float(SIGMA[2 * pair + i] ** 2) for i in range(2)]
            zeroth = zeroth + sums_ref[2 * pair + row]
            second = second + sums_ref[2 * pair + row] * jnp.where(sub < 4, low, high)
        for index, value in ((2, zeroth), (3, second)):
            turn_ref[pl.ds(16 * index + row, 8, stride=2), :] = value + pltpu.roll(value, 4, 0)
    moment_zero = turn_ref[32:40] * (2.0 / BINS)
    moment_two = turn_ref[48:56] * (2.0 / BINS)
    limit = (GAMMA_BR * depth) * (GAMMA_BR * depth)
    breaking = jnp.where(wet > 0.5, 2.0 * limit / jnp.maximum(16.0 * moment_zero, limit), 0.0)
    for f in range(NF):
        damp_ref[f] = (1.0 - A_IN) - float(C_WC * SIGMA[f] ** 3) * moment_two
    rel_x = wind[0] - u
    rel_y = wind[1] - v

    def source(d, carried):
        parts = []
        source_direction(
            d,
            trig_ref,
            moved_ref,
            damp_ref,
            rel_x,
            rel_y,
            breaking,
            lambda quad, results: parts.append(emit(d, quad, results)),
        )
        return combine(d, carried, parts) if combine else carried

    return lax.fori_loop(0, ND, source, initial)


def packed_rows(refs, d, quad):
    blocks = [ref[pl.ds(half_row(d) + 16 * quad, 16), :].astype(F32) for ref in refs]
    return [[block[8 * part : 8 * part + 8] for block in blocks] for part in range(2)]


def wave_scratch():
    return [
        VMEM((CELL_ROWS + PAD, 128), F32),
        VMEM((NF, 8, 128), F32),
        VMEM((NF, 8, 128), F32),
        VMEM((64 + PAD, 128), F32),
        VMEM((NF // 2, 8, 128), F32),
    ]


def inner_rows(refs, d, quad):
    return [
        (
            [(lower, upper)],
            [(lower, sublane_up(lower), None, 0), (upper, sublane_up(upper), 0, None)],
        )
        for lower, upper in packed_rows(refs, d, quad)
    ]


def begin_kernel(
    trig_ref, upper_ref, lower_ref, arrived_ref, part_lower_ref, part_upper_ref, turn_ref, speed_ref
):
    u, v, _, wet = strip_fields(arrived_ref)
    own = by_row(turn_ref, 0, u(0, 1))
    face_own = (0.5 * LAM_W) * (own[0] + own[1])
    set_speeds(speed_ref)
    cells = pass_cells(turn_ref, v(0, 1), wet(0, 1))

    def rows_own(d, quad):
        return inner_rows((lower_ref, upper_ref), d, quad)

    emit = packing((part_lower_ref, part_upper_ref))
    each_direction(
        lambda d: propagate_direction(d, trig_ref, rows_own, (face_own,), cells, speed_ref, emit)
    )


def begin_step(trig, *operands):
    here = pl.BlockSpec(memory_space=VMEM)
    return pl.pallas_call(
        begin_kernel,
        out_shape=(jax.ShapeDtypeStruct((HALF_ROWS, 128), BF16),) * 2,
        in_specs=[pl.BlockSpec(memory_space=SMEM)] + [here] * len(operands),
        out_specs=(here,) * 2,
        scratch_shapes=wave_scratch()[-2:],
        compiler_params=params(16),
        cost_estimate=pl.CostEstimate(
            flops=100000000, bytes_accessed=20000000, transcendentals=0
        ),
        name="begin_wave_step",
    )(trig, *operands)


KEPT = 20


def first_kernel(
    trig_ref,
    upper_ref,
    lower_ref,
    above_ref,
    below_ref,
    part_lower_ref,
    part_upper_ref,
    arrived_ref,
    wind_ref,
    spec_lower_ref,
    spec_upper_ref,
    near_above_ref,
    near_below_ref,
    next_lower_ref,
    next_upper_ref,
    above_out_ref,
    below_out_ref,
    fields_ref,
    spec_ref,
    *scratch,
):
    moved_ref, damp_ref, sums_ref, turn_ref, speed_ref = scratch
    u, v, depth, wet = strip_fields(arrived_ref)
    u_own, u_near = u(0, 1), u(-1, 2)
    own = by_row(turn_ref, 0, u_own)
    near = by_row(turn_ref, 1, u_near)
    half = 0.5 * LAM_W
    face_low = half * (near[0] + own[0])
    face_own = half * (own[0] + own[1])
    face_high = half * (own[1] + near[1])
    wind = wind_ref[...].astype(F32)
    set_speeds(speed_ref)
    v_own, wet_own = v(0, 1), wet(0, 1)
    cells = pass_cells(turn_ref, v_own, wet_own)

    above_out_ref[...] = above_ref[0:HALF_ROWS, :]
    below_out_ref[...] = below_ref[0:HALF_ROWS, :]
    far = by_row(turn_ref, 2, u(-2, 3))
    wet_near = wet(-1, 2)
    for row, ref in ((0, above_ref), (1, below_ref)):
        arrived_wind = ref[HALF_ROWS:, :].astype(F32)[0:8]
        turn_ref[pl.ds(48 + row, 8, stride=2), :] = arrived_wind
    kept = [half * (far[0] + near[0]), half * (near[1] + far[1]), face_low, face_high]
    kept += [u_near, v(-1, 2), depth(-1, 2), wet_near, turn_ref[48:56], turn_ref[56:64]]
    kept += [u_own, v_own, depth(0, 1), wet_own, wind[0:8], wind[8:16]]
    kept += [0.5 * row for field in (wet_near, wet_own) for row in by_row(turn_ref, 0, field)]
    for index, field in enumerate(kept):
        fields_ref[index] = field

    def rows_first(d, quad):
        refs = (above_ref, lower_ref, upper_ref, below_ref, part_lower_ref, part_upper_ref)
        return [(*rows[:4], rows[4:]) for rows in packed_rows(refs, d, quad)]

    emit = summing(moved_ref, sums_ref)
    faces = (face_low, face_high)
    half_own = cells[-1]
    each_direction(
        lambda d: finish_direction(d, trig_ref, rows_first, faces, half_own, speed_ref, emit)
    )

    def emit_spec(d, quad, results):
        start = base_row(d) + 32 * quad
        spec_ref[pl.ds(start, 32), :] = jnp.concatenate(results, axis=0)
        for row, ref in ((0, spec_lower_ref), (1, spec_upper_ref)):
            halves = [pair_row(spec_ref, start + 16 * pair, row) for pair in range(2)]
            packed = jnp.concatenate(halves, axis=0).astype(BF16)
            ref[pl.ds(half_row(d) + 16 * quad, 16), :] = packed

    source_pass(
        trig_ref,
        u_own,
        v_own,
        depth(0, 1),
        wet_own,
        (wind[0:8], wind[8:16]),
        (moved_ref, damp_ref, sums_ref, turn_ref),
        emit_spec,
    )

    def rows_second(d, quad):
        return inner_rows((spec_lower_ref, spec_upper_ref), d, quad)

    emit_next = packing((next_lower_ref, next_upper_ref))
    each_direction(
        lambda d: propagate_direction(
            d, trig_ref, rows_second, (face_own,), cells, speed_ref, emit_next
        )
    )

    cells_near = pass_cells(turn_ref, v(-1, 2), wet(-1, 2))

    def rows_near(d, quad):
        return [
            (
                [(above, lower), (upper, below)],
                [(above, sublane_up(above), None, 0), (below, sublane_up(below), 1, None)],
            )
            for above, lower, upper, below in packed_rows(
                (above_ref, lower_ref, upper_ref, below_ref), d, quad
            )
        ]

    emit_near = packing((near_above_ref, near_below_ref))
    each_direction(
        lambda d: propagate_direction(
            d, trig_ref, rows_near, (face_low, face_high), cells_near, speed_ref, emit_near
        )
    )


def second_kernel(
    trig_ref,
    far_above_ref,
    far_below_ref,
    spec_lower_ref,
    spec_upper_ref,
    near_above_ref,
    near_below_ref,
    next_lower_ref,
    next_upper_ref,
    above_ref,
    below_ref,
    fields_ref,
    out_hbm,
    stress_hbm,
    near_ref,
    out_ref,
    sem,
    stress_ref,
    stress_sem,
    *scratch,
):
    moved_ref, damp_ref, sums_ref, turn_ref, speed_ref = scratch
    shared = (moved_ref, damp_ref, sums_ref, turn_ref)
    kept = [fields_ref[index] for index in range(KEPT)]
    faces_near, faces_own = kept[0:2], kept[2:4]
    half_near, half_own = kept[16:18], kept[18:20]
    set_speeds(speed_ref)

    def rows_near(d, quad):
        refs = (far_above_ref, above_ref, below_ref, far_below_ref, near_above_ref, near_below_ref)
        return [(*rows[:4], rows[4:]) for rows in packed_rows(refs, d, quad)]

    emit = summing(moved_ref, sums_ref)
    each_direction(
        lambda d: finish_direction(d, trig_ref, rows_near, faces_near, half_near, speed_ref, emit)
    )

    def emit_near(d, quad, results):
        near_ref[pl.ds(base_row(d) + 32 * quad, 32), :] = jnp.concatenate(results, axis=0)

    source_pass(trig_ref, *kept[4:8], kept[8:10], shared, emit_near)

    def rows_own(d, quad):
        refs = (spec_lower_ref, spec_upper_ref, next_lower_ref, next_upper_ref)
        parts = []
        for part, rows in enumerate(packed_rows(refs, d, quad)):
            start = base_row(d) + 32 * quad + 16 * part
            below, above = [pair_row(near_ref, start, row) for row in range(2)]
            parts.append((below, rows[0], rows[1], above, rows[2:]))
        return parts

    emit = summing(moved_ref, sums_ref)
    each_direction(
        lambda d: finish_direction(d, trig_ref, rows_own, faces_own, half_own, speed_ref, emit)
    )
    outgoing = chunk_copies(out_ref, out_hbm, sem)
    zeros = jnp.zeros((8, 128), F32)

    def emit_own(d, quad, results):
        packed = jnp.concatenate(results, axis=0).astype(BF16)
        out_ref[d, 32 * quad : 32 * quad + 32, :] = packed
        scales = [float(math.pi / ND * SIGMA[4 * quad + part] / NF) for part in range(4)]
        return sum(result * scale for result, scale in zip(results, scales))

    def add_stress(d, totals, parts):
        @pl.when(lax.rem(d, CHUNK) == CHUNK - 1)
        def _():
            outgoing(lax.div(d, CHUNK)).start()

        total = sum(parts)
        cos_d, sin_d = trig_ref[0, d], trig_ref[1, d]
        xx, xy, yy = totals
        return (
            xx + total * (cos_d * cos_d),
            xy + total * (cos_d * sin_d),
            yy + total * (sin_d * sin_d),
        )

    totals = source_pass(
        trig_ref,
        *kept[10:14],
        kept[14:16],
        shared,
        emit_own,
        (zeros, zeros, zeros),
        add_stress,
    )
    for c in range(3):
        for tile in range(8):
            part = tile // 2
            stress_ref[tile, 2 * c : 2 * c + 2, :] = totals[c][2 * part : 2 * part + 2]
    stress_copy = pltpu.make_async_copy(stress_ref, stress_hbm, stress_sem)
    stress_copy.start()
    for index in range(ND // CHUNK):
        outgoing(index).wait()
    stress_copy.wait()


def first_step(trig, *operands):
    here = pl.BlockSpec(memory_space=VMEM)
    return pl.pallas_call(
        first_kernel,
        out_shape=(jax.ShapeDtypeStruct((HALF_ROWS, 128), BF16),) * 8
        + (jax.ShapeDtypeStruct((KEPT, 8, 128), F32),),
        in_specs=[pl.BlockSpec(memory_space=SMEM)] + [here] * len(operands),
        out_specs=(here,) * 9,
        scratch_shapes=[VMEM((CELL_ROWS + PAD, 128), F32)] + wave_scratch(),
        compiler_params=params(32),
        cost_estimate=pl.CostEstimate(
            flops=100000000, bytes_accessed=60000000, transcendentals=0
        ),
        name="first_wave_step",
    )(trig, *operands)


def second_step(trig, *operands):
    here = pl.BlockSpec(memory_space=VMEM)
    full = jax.ShapeDtypeStruct((ND, NF * 8, 128), BF16)
    return pl.pallas_call(
        second_kernel,
        out_shape=(full, jax.ShapeDtypeStruct((8, 6, 128), F32)),
        in_specs=[pl.BlockSpec(memory_space=SMEM)] + [here] * len(operands),
        out_specs=(pl.BlockSpec(memory_space=pl.ANY),) * 2,
        scratch_shapes=[
            VMEM((CELL_ROWS + PAD, 128), F32),
            VMEM(full.shape, BF16),
            pltpu.SemaphoreType.DMA((ND // CHUNK,)),
            VMEM((8, 6, 128), F32),
            pltpu.SemaphoreType.DMA,
        ]
        + wave_scratch(),
        compiler_params=params(36),
        cost_estimate=pl.CostEstimate(
            flops=200000000, bytes_accessed=40000000, transcendentals=0
        ),
        name="second_wave_step",
    )(trig, *operands)


def ocean_kernel(place_ref, vel_ref, own_ref, low_ref, high_ref, arrived_ref, out_ref, level_ref):
    row = lax.broadcasted_iota(jnp.int32, (32, 128), 0)
    lane = lax.broadcasted_iota(jnp.int32, (32, 128), 1)
    first_row, last_row = row == 0, row == 31
    first_lane, last_lane = lane == 0, lane == 127
    levels = vel_ref.shape[1]
    place = place_ref[0]
    before = arrived_ref[jnp.maximum(place - 1, 0), COLUMNS_AT:, :]
    before = jnp.where(place > 0, before, 0.0)
    after = arrived_ref[jnp.minimum(place + 1, 7), COLUMNS_AT:, :]
    after = jnp.where(place < 7, after, 0.0)

    def down(x, edge):
        return jnp.where(first_row, edge, pltpu.roll(x, 1, 0))

    def up(x, edge):
        return jnp.where(last_row, edge, pltpu.roll(x, 31, 0))

    def left(x, index):
        return jnp.where(first_lane, before[:, index : index + 1], pltpu.roll(x, 1, 1))

    def right(x, index):
        return jnp.where(last_lane, after[:, index : index + 1], pltpu.roll(x, 127, 1))

    def edge_rows(index):
        return low_ref[index, 7:8, :], high_ref[index, 0:1, :]

    level, bathy, wet, sxx, sxy, syy = [own_ref[i] for i in range(6)]
    ubar, vbar = own_ref[10], own_ref[11]
    edges = [edge_rows(i) for i in range(FIELDS)]
    plane_count = 2 * levels
    depth = bathy + level
    flux_x = depth * ubar
    flux_low = (edges[0][0] + edges[1][0]) * edges[10][0]
    flux_high = (edges[0][1] + edges[1][1]) * edges[10][1]
    flux_y = depth * vbar
    divergence = (
        up(flux_x, flux_high)
        - down(flux_x, flux_low)
        + right(flux_y, plane_count + 3)
        - left(flux_y, plane_count + 3)
    )
    level_ref[...] = level - 0.5 * LAM_O * wet * divergence
    inverse = 1.0 / depth
    grad_x = 0.5 * (up(level, edges[0][1]) - down(level, edges[0][0]))
    grad_y = 0.5 * (right(level, plane_count) - left(level, plane_count))
    xx_x = up(sxx, edges[3][1]) - down(sxx, edges[3][0])
    xy_x = up(sxy, edges[4][1]) - down(sxy, edges[4][0])
    xy_y = right(sxy, plane_count + 1) - left(sxy, plane_count + 1)
    yy_y = right(syy, plane_count + 2) - left(syy, plane_count + 2)
    base = (
        -LAM_O * grad_x - 0.5 * LAM_O * (xx_x + xy_y) * inverse,
        -LAM_O * grad_y - 0.5 * LAM_O * (xy_x + yy_y) * inverse,
    )
    turn = (F_CORIOLIS, -F_CORIOLIS)
    for k in range(levels):
        for c in range(2):
            plane = c * levels + k
            here = vel_ref[c, k]
            other = vel_ref[1 - c, k]
            above = vel_ref[c, max(k - 1, 0)]
            below = vel_ref[c, min(k + 1, levels - 1)]
            block, place = FIELDS + plane // 8, plane % 8
            low = low_ref[block, place : place + 1, :]
            high = high_ref[block, place : place + 1, :]
            around = up(here, high) + down(here, low) + right(here, plane) + left(here, plane)
            tendency = (
                base[c]
                + turn[c] * other
                + NU_H * (around - 4.0 * here)
                + KAPPA_V * (above + below - 2.0 * here)
            )
            out_ref[c, k] = wet * (here + tendency)


def ocean_step(place, vel, *operands):
    return pl.pallas_call(
        ocean_kernel,
        out_shape=(
            jax.ShapeDtypeStruct(vel.shape, F32),
            jax.ShapeDtypeStruct((32, 128), F32),
        ),
        in_specs=[pl.BlockSpec(memory_space=SMEM)] + [pl.BlockSpec(memory_space=VMEM)] * 5,
        out_specs=(pl.BlockSpec(memory_space=VMEM),) * 2,
        compiler_params=params(16),
        cost_estimate=pl.CostEstimate(flops=10000000, bytes_accessed=3000000, transcendentals=0),
        name="ocean_step",
    )(place, vel, *operands)


def shifted(array, axis_name, up):
    count = lax.axis_size(axis_name)
    pairs = [(i, i + 1) for i in range(count - 1)]
    if not up:
        pairs = [(target, source) for source, target in pairs]
    return lax.ppermute(array, axis_name, pairs)


def after(value, *others):
    return lax.optimization_barrier((value,) + others)[0]


def per_device(ocean_level, ocean_velocity, bathymetry, sea_mask, stress_in, spectra, wind_field):
    both = ("wide", "deep")
    spec = spectra.reshape(ND, NF, 2, 4, 128).transpose(0, 1, 3, 2, 4).reshape(ND, NF * 8, 128)
    wind = wind_field.reshape(2, 2, 4, 128).transpose(0, 2, 1, 3).reshape(16, 128)
    trig = jnp.asarray(TRIG)

    own, low_edge, high_edge, first, last = gather_surface(
        ocean_level, ocean_velocity, bathymetry, sea_mask, stress_in
    )
    from_low = shifted(high_edge, "wide", True)
    from_high = shifted(low_edge, "wide", False)
    upper, lower = split_rows(after(spec, own), wind)
    place = lax.axis_index("deep").astype(jnp.int32).reshape(1)
    outgoing = surface_step(place, after(own, upper), from_low, from_high, first, last)
    arrived = lax.all_to_all(outgoing, "deep", split_axis=0, concat_axis=0, tiled=True)

    above = shifted(after(upper, from_low, from_high), both, True)
    below = shifted(after(lower, from_low, from_high), both, False)
    far_above = shifted(after(lower, arrived), both, True)
    far_below = shifted(after(upper, arrived), both, False)
    velocity_out, level_out = ocean_step(
        place, ocean_velocity, own, from_low, from_high, arrived
    )
    begun = begin_step(trig, upper, lower, arrived)
    partial = first_step(
        trig, upper, lower, above, below, *begun, after(arrived, level_out), wind
    )
    spec, stress = second_step(trig, far_above, far_below, *partial)
    stress = lax.all_to_all(stress, "deep", split_axis=0, concat_axis=0, tiled=True)
    stress = stress.reshape(8, 3, 2, 128).transpose(1, 0, 2, 3).reshape(3, 16, 128)
    stress_out = jnp.where((place[0] & 1) == 1, stress[:, :, 64:], stress[:, :, :64])
    spectra_out = (
        spec.reshape(ND, NF, 4, 2, 128).transpose(0, 1, 3, 2, 4).reshape(ND, NF, 2, 512)
    )
    return (level_out, velocity_out, spectra_out, stress_out)


def solution(mesh):
    in_specs = (
        P("wide", "deep"),
        P(None, None, "wide", "deep"),
        P("wide", "deep"),
        P("wide", "deep"),
        P(None, "wide", "deep"),
        P(None, None, ("wide", "deep"), None),
        P(None, ("wide", "deep"), None),
    )
    out_specs = (
        P("wide", "deep"),
        P(None, None, "wide", "deep"),
        P(None, None, ("wide", "deep"), None),
        P(None, "wide", "deep"),
    )
    return jax.shard_map(
        per_device, mesh=mesh, in_specs=in_specs, out_specs=out_specs, check_vma=False
    )
```
